32 devices in a mesh: fsdp: 16 (over z, x, core), seq: 2 (over y).
Axes of the slice: x: 2, y: 2, z: 4, core: 2. Of those that a mesh axis runs over, the one named last changes fastest.
Arguments:
- latents: bfloat16 [16, 1024, 1024], P('fsdp', 'seq'), may hold values from -6 to 6
- cond: bfloat16 [16, 1024], P('fsdp'), may hold values from -6 to 6
- cotangent: bfloat16 [16, 1024, 1024], P('fsdp', 'seq'), may hold values from -6 to 6
- w_qkv: bfloat16 [1024, 3072], P('fsdp'), may hold values from -0.1875 to 0.1875
- w_out: bfloat16 [1024, 1024], P('fsdp'), may hold values from -4 to 4
- w_up: bfloat16 [1024, 4096], P('fsdp', 'seq'), may hold values from -0.1875 to 0.1875
- w_down: bfloat16 [4096, 1024], P('seq', 'fsdp'), may hold values from -0.09375 to 0.09375
- w_ada: bfloat16 [1024, 6144], P(None, 'fsdp'), may hold values from -0.1875 to 0.1875
- b_ada: bfloat16 [6144], P('fsdp'), may hold values from -3 to 3
Outputs:
- mixed: bfloat16 [16, 1024, 1024], P('fsdp', 'seq')
- grad_latents: float32 [16, 1024, 1024], P('fsdp', 'seq')
- grad_cond: float32 [16, 1024], P('fsdp')
- grad_w_qkv: float32 [1024, 3072], P('fsdp')
- grad_w_out: float32 [1024, 1024], P('fsdp')
- grad_w_up: float32 [1024, 4096], P('fsdp', 'seq')
- grad_w_down: float32 [4096, 1024], P('seq', 'fsdp')
- grad_w_ada: float32 [1024, 6144], P(None, 'fsdp')
- grad_b_ada: float32 [6144], P('fsdp')
The draws below stay inside these ranges and needn't reach their ends.
All inputs are finite; a program needn't handle non-finite values.
Results may differ from the reference program's by a relative error of at most 0.015.
The reference program's roundings to bfloat16 on the way count: a program that leaves them out, or rounds other values in their place, can miss the bound.
Values may be sent and summed in bfloat16 or wider, within the bound.
No kernel may reach another device: no remote copies, remote signals or barrier semaphores. Data moves between devices by JAX's collectives and lax.ppermute only.
A program may use at most 128 MiB of HBM per device.

```python
import jax
import jax.numpy as jnp
from jax import lax

D = 1024
H = 16
HD = 64
FF = 4096
LEN = 1024
BATCH = 16
MODS = 6144


def steps_of(own_key, shape, split, low, top_value):
    def one(axis_at, shards_of):
        steps = jax.random.uniform(jax.random.fold_in(jax.random.fold_in(own_key, 6), axis_at), (shards_of,), jnp.float32, low / len(split), top_value / len(split))
        return jnp.repeat(jnp.exp(steps), shape[axis_at] // shards_of).reshape((-1,) + (1,) * (len(shape) - axis_at - 1))

    loudness = one(*split[0])
    for cut in split[1:]:
        loudness = loudness * one(*cut)
    return loudness


def noise(key, shape, scale, reach, pieces=(), held_as=jnp.bfloat16):
    entries = scale * jax.random.normal(key, shape, jnp.float32)
    if pieces:
        entries = entries * steps_of(key, shape, pieces, -0.22, 0.18)
    return jnp.clip(entries, -reach, reach).astype(held_as)


def setup_inputs(seed: int = 0) -> dict:
    key_list = jax.random.split(jax.random.key(seed), 10)
    latents = noise(key_list[0], (BATCH, LEN, D), 1.0, 6.0, ((0, 16), (1, 2)))
    cond = noise(key_list[1], (BATCH, D), 1.0, 6.0, ((0, 16),))
    cotangent = noise(key_list[2], (BATCH, LEN, D), 1.0, 6.0, ((0, 16), (1, 2)))
    w_qkv = noise(key_list[3], (D, 3 * D), D ** -0.5, 0.1875, ((0, 16),))
    w_out = noise(key_list[4], (D, D), (max(2 * D // LEN, 1)) ** -0.5, 4.0, ((0, 16),))
    w_up = noise(key_list[5], (D, FF), D ** -0.5, 0.1875, ((0, 16), (1, 2)))
    w_down = noise(key_list[6], (FF, D), FF ** -0.5, 0.09375, ((0, 2), (1, 16)))
    w_ada = noise(key_list[7], (D, MODS), D ** -0.5, 0.1875, ((1, 16),))
    b_ada = noise(key_list[8], (MODS,), 0.5, 3.0, ((0, 16),))
    return {"latents": latents, "cond": cond, "cotangent": cotangent, "w_qkv": w_qkv, "w_out": w_out, "w_up": w_up, "w_down": w_down, "w_ada": w_ada, "b_ada": b_ada}


PRECISE = lax.Precision.HIGHEST
EPSILON = 1e-06

@jax.custom_vjp
def low(v):
    return lax.optimization_barrier(v.astype(jnp.bfloat16)).astype(jnp.float32)

@jax.custom_vjp
def low_back(v):
    return v

def low_keep(v):
    return (low(v), None)

def low_pass(kept, grad):
    return (grad,)

def back_keep(v):
    return (v, None)

def back_low(kept, grad):
    return (low(grad),)
low.defvjp(low_keep, low_pass)
low_back.defvjp(back_keep, back_low)

def normalize(value_rows):
    center = value_rows - lax.optimization_barrier(jnp.mean(value_rows, -1, keepdims=True))
    return center * lax.rsqrt(lax.optimization_barrier(jnp.mean(center * center, -1, keepdims=True)) + EPSILON)

def attend(head_block):
    head_depth = head_block.shape[-1] // 3
    query_rows_all = head_block[..., :head_depth]
    key_tile_block = head_block[..., head_depth:2 * head_depth]
    value_rows = head_block[..., 2 * head_depth:]
    scores = low_back(jnp.einsum('qhd,khd->hqk', query_rows_all, key_tile_block, precision=PRECISE) * head_depth ** (-0.5))
    weight_matrices = low(jax.nn.softmax(scores, axis=-1))
    return jnp.einsum('hqk,khd->qhd', weight_matrices, value_rows, precision=PRECISE)

def one_latent(inputs, modulation, w_qkv, w_out, w_up, w_down):
    model_width = inputs.shape[-1]
    token_count = inputs.shape[0]
    shift_one, scale_one, gate_one, shift_two, scale_two, gate_two = [modulation[position * model_width:(position + 1) * model_width] for position in range(6)]
    hidden_one = low(normalize(inputs) * (1.0 + scale_one) + shift_one)
    qkv_rows = low_back(low(jnp.dot(hidden_one, w_qkv, precision=PRECISE)))
    attention_result = attend(qkv_rows.reshape(token_count, H, 3 * HD))
    attn_rows = low_back(low(attention_result.reshape(token_count, model_width)))
    branch_one = low_back(jnp.dot(attn_rows, w_out, precision=PRECISE))
    middle = inputs + gate_one * branch_one
    hidden_two = low(normalize(middle) * (1.0 + scale_two) + shift_two)
    up_values = low_back(jnp.dot(hidden_two, w_up, precision=PRECISE))
    activated = low(jax.nn.gelu(up_values, approximate=True))
    branch_two = low_back(jnp.dot(activated, w_down, precision=PRECISE))
    return middle + gate_two * branch_two

def forward(latents, cond, w_qkv, w_out, w_up, w_down, w_ada, b_ada):
    cond_act = low(jax.nn.silu(cond))
    modulation = low_back(low(jnp.dot(cond_act, w_ada, precision=PRECISE) + b_ada))
    blocked = jax.checkpoint(one_latent)
    return lax.map(lambda latent_pair: blocked(latent_pair[0], latent_pair[1], w_qkv, w_out, w_up, w_down), (latents, modulation))

def reference(latents, cond, cotangent, w_qkv, w_out, w_up, w_down, w_ada, b_ada):
    primals = [array.astype(jnp.float32) for array in (latents, cond, w_qkv, w_out, w_up, w_down, w_ada, b_ada)]
    mixed, pullback = jax.vjp(forward, *primals)
    gradients = pullback(cotangent.astype(jnp.float32))
    return (mixed.astype(jnp.bfloat16), gradients[0], gradients[1], gradients[2], gradients[3], gradients[4], gradients[5], gradients[6], gradients[7])
```

```python
from functools import partial

import jax
import jax.numpy as jnp
from jax import lax
from jax.experimental import pallas as pl
from jax.experimental.pallas import tpu as pltpu
from jax.sharding import PartitionSpec as P

H = 16
HD = 64
EPSILON = 1e-06
LOG2E = 1.4426950408889634
SCALE2 = HD**-0.5 * LOG2E
VMEM = 56 * 1024 * 1024
CHUNK = 256

NT = (((1,), (1,)), ((), ()))
TN = (((0,), (0,)), ((), ()))
NN = (((1,), (0,)), ((), ()))


def mm(a, b, dims=NN):
    return lax.dot_general(a, b, dims, preferred_element_type=jnp.float32)


def normalize(value_rows):
    center = value_rows - jnp.mean(value_rows, -1, keepdims=True)
    inverse = lax.rsqrt(jnp.mean(center * center, -1, keepdims=True) + EPSILON)
    return (center * inverse, inverse)


def norm_grad(normed, inverse, grad_normed):
    return inverse * (
        grad_normed
        - jnp.mean(grad_normed, -1, keepdims=True)
        - normed * jnp.mean(grad_normed * normed, -1, keepdims=True)
    )


def head_parts(ref, head, rows=slice(None)):
    base = head * 3 * HD
    return [ref[rows, base + j * HD : base + (j + 1) * HD] for j in range(3)]


def attend_kernel(query_ref, all_ref, out_ref, lse_ref):
    rows = query_ref.shape[0]
    for head in range(2):
        _, keys, values = head_parts(all_ref, head)
        chunk = min(CHUNK, rows)
        for at in range(0, rows, chunk):
            span = slice(at, at + chunk)
            queries = head_parts(query_ref, head, span)[0]
            scores = mm(keys, queries, NT)
            highest = jnp.max(scores, 0, keepdims=True)
            raised = jnp.exp2(scores * SCALE2 - highest * SCALE2)
            totals = jnp.sum(raised, 0, keepdims=True)
            result = mm(values, raised.astype(jnp.bfloat16), TN) / totals
            out_ref[span, head * HD : (head + 1) * HD] = result.T.astype(jnp.bfloat16)
            lse_ref[0, head : head + 1, span] = highest * SCALE2 + jnp.log2(totals)


def attend(qkv, tokens, first, count):
    length, columns = qkv.shape
    pairs = columns // (6 * HD)
    return pl.pallas_call(
        attend_kernel,
        grid=(pairs, count),
        in_specs=[
            pl.BlockSpec((tokens, 6 * HD), lambda p, b: (first + b, p)),
            pl.BlockSpec((length, 6 * HD), lambda p, b: (0, p)),
        ],
        out_specs=[
            pl.BlockSpec((tokens, 2 * HD), lambda p, b: (b, p)),
            pl.BlockSpec((1, 2, tokens), lambda p, b: (p, 0, b)),
        ],
        out_shape=[
            jax.ShapeDtypeStruct((count * tokens, pairs * 2 * HD), jnp.bfloat16),
            jax.ShapeDtypeStruct((pairs, 2, count * tokens), jnp.float32),
        ],
        compiler_params=pltpu.CompilerParams(vmem_limit_bytes=VMEM),
        cost_estimate=pl.CostEstimate(
            flops=4 * pairs * 2 * HD * length * count * tokens * 4,
            bytes_accessed=2 * length * columns,
            transcendentals=pairs * 2 * length * count * tokens,
        ),
        name="attend",
    )(qkv, qkv)


def attend_back_kernel(all_ref, grad_ref, lse_ref, delta_ref, out_ref, key_acc, value_acc):
    length = all_ref.shape[0]
    scaling = HD**-0.5
    for head in range(2):
        base = head * 3 * HD
        _, keys, values = head_parts(all_ref, head)
        for at in range(0, length, CHUNK):
            span = slice(at, at + CHUNK)
            queries = head_parts(all_ref, head, span)[0]
            grads = grad_ref[span, head * HD : (head + 1) * HD]
            lse = lse_ref[0, head : head + 1, span]
            delta = delta_ref[0, head : head + 1, span]
            probs = jnp.exp2(mm(keys, queries, NT) * SCALE2 - lse)
            score_grad = (probs * (mm(values, grads, NT) - delta)).astype(jnp.bfloat16)
            value_part = mm(probs.astype(jnp.bfloat16), grads)
            key_part = mm(score_grad, queries)
            if at == 0:
                value_acc[...] = value_part
                key_acc[...] = key_part
            else:
                value_acc[...] += value_part
                key_acc[...] += key_part
            query_grad = mm(keys, score_grad, TN) * scaling
            out_ref[span, base : base + HD] = query_grad.T.astype(jnp.bfloat16)
        out_ref[:, base + HD : base + 2 * HD] = (key_acc[...] * scaling).astype(jnp.bfloat16)
        out_ref[:, base + 2 * HD : base + 3 * HD] = value_acc[...].astype(jnp.bfloat16)


def attend_back(qkv, grad_attn, lse, delta):
    length, columns = qkv.shape
    pairs = columns // (6 * HD)
    return pl.pallas_call(
        attend_back_kernel,
        grid=(pairs,),
        in_specs=[
            pl.BlockSpec((length, 6 * HD), lambda p: (0, p)),
            pl.BlockSpec((length, 2 * HD), lambda p: (0, p)),
            pl.BlockSpec((1, 2, length), lambda p: (p, 0, 0)),
            pl.BlockSpec((1, 2, length), lambda p: (p, 0, 0)),
        ],
        out_specs=pl.BlockSpec((length, 6 * HD), lambda p: (0, p)),
        out_shape=jax.ShapeDtypeStruct((length, columns), jnp.bfloat16),
        scratch_shapes=[
            pltpu.VMEM((length, HD), jnp.float32),
            pltpu.VMEM((length, HD), jnp.float32),
        ],
        compiler_params=pltpu.CompilerParams(vmem_limit_bytes=VMEM),
        cost_estimate=pl.CostEstimate(
            flops=10 * pairs * 2 * HD * length * length * 4,
            bytes_accessed=4 * length * columns,
            transcendentals=pairs * 2 * length * length,
        ),
        name="attend_back",
    )(qkv, grad_attn, lse, delta)


def per_device(sizes, latents, cond, cotangent, w_qkv, w_out, w_up, w_down, w_ada, b_ada):
    shards, splits = sizes["fsdp"], sizes["seq"]
    me = lax.axis_index("seq")
    tokens, width = latents.shape[1:]
    heads = H // splits
    low = jnp.bfloat16
    wide = jnp.float32

    def fetch(value, step):
        return lax.ppermute(value, "seq", [((i + step) % splits, i) for i in range(splits)])

    def send(value, step):
        return lax.ppermute(value, "seq", [(i, (i + step) % splits) for i in range(splits)])

    def everyone(value):
        return [value] + [fetch(value, step) for step in range(1, splits)]

    def in_order(pieces, axis):
        if splits == 1:
            return pieces[0]
        return jnp.concatenate(
            [
                lax.select_n(
                    (position - me) % splits == 1, *pieces
                ) if splits == 2 else
                lax.dynamic_index_in_dim(
                    jnp.stack(pieces), (position - me) % splits, 0, keepdims=False
                )
                for position in range(splits)
            ],
            axis,
        )

    def seq_sum(value):
        if splits != 2:
            return lax.psum(value, "seq").astype(wide)
        return value.astype(wide) + fetch(value, 1).astype(wide)

    spot = lax.axis_index("fsdp")
    depth = shards // 4
    core_at, x_at, z_at = spot % 2, (spot // 2) % 2, spot // 4

    def core_swap(value):
        return lax.ppermute(value, "fsdp", [(i, i ^ 1) for i in range(shards)])

    def x_swap(value):
        return lax.ppermute(value, "fsdp", [(i, i ^ 2) for i in range(shards)])

    def z_send(value, step):
        return lax.ppermute(value, "fsdp", [(i, (i + 4 * step) % shards) for i in range(shards)])

    def two(mine, other, at):
        return jnp.stack(
            [jnp.where(at == 0, mine, other), jnp.where(at == 0, other, mine)], 1
        )

    def gather_rows(shard):
        rows, cols = shard.shape
        line = jnp.zeros((depth, rows, cols), shard.dtype)
        for step in range(depth):
            piece = z_send(shard, step) if step else shard
            line = lax.dynamic_update_slice_in_dim(
                line, piece[None], (z_at - step) % depth, 0
            )
        plane = two(line, x_swap(line), x_at).reshape(2 * depth, rows, cols)
        return two(plane, core_swap(plane), core_at).reshape(shards * rows, cols)

    def halve(value, at, swap):
        mine = lax.dynamic_index_in_dim(value, at, 1, keepdims=False)
        other = lax.dynamic_index_in_dim(value, 1 - at, 1, keepdims=False)
        return (mine.astype(wide) + swap(other).astype(wide)).astype(low)

    def scatter_rows(value):
        rows, cols = value.shape[0] // shards, value.shape[1]
        value = halve(value.reshape(2 * depth, 2, rows, cols), core_at, core_swap)
        value = halve(value.reshape(depth, 2, rows, cols), x_at, x_swap)
        total = lax.dynamic_index_in_dim(value, z_at, 0, keepdims=False).astype(wide)
        for step in range(1, depth):
            piece = lax.dynamic_index_in_dim(value, (z_at + step) % depth, 0, keepdims=False)
            total = total + z_send(piece, step).astype(wide)
        return total

    own_latents, own_cotangent = latents[0], cotangent[0]
    cond_act, silu_back = jax.vjp(jax.nn.silu, cond.astype(wide))
    cond_all = lax.all_to_all(
        jnp.broadcast_to(cond_act.astype(low), (shards, width)),
        "fsdp",
        split_axis=0,
        concat_axis=0,
        tiled=True,
    )
    mod_cols = (mm(cond_all, w_ada) + b_ada.astype(wide)).astype(low)
    modulation = lax.all_to_all(
        mod_cols, "fsdp", split_axis=0, concat_axis=1, tiled=True
    ).astype(wide)
    shift_one, scale_one, gate_one, shift_two, scale_two, gate_two = [
        modulation[:, position * width : (position + 1) * width] for position in range(6)
    ]
    columns = heads * 3 * HD
    qkv_shard = lax.dynamic_slice_in_dim(w_qkv, me * columns, columns, 1)
    qkv_half = lax.all_gather(qkv_shard, "fsdp", axis=0, tiled=True)
    out_full = gather_rows(w_out)
    up_down = lax.all_gather(jnp.concatenate([w_up, w_down.T], 1), "fsdp", axis=0, tiled=True)
    hidden_units = w_up.shape[1]
    up_full, down_full = up_down[:, :hidden_units], up_down[:, hidden_units:]

    latents_all = jnp.concatenate(everyone(own_latents), 0)
    cotangents = everyone(own_cotangent)
    grad_rows = [(gate_two * value.astype(wide)).astype(low) for value in cotangents]

    normed_all, inverse_all = normalize(latents_all.astype(wide))
    hidden_one = (normed_all * (1.0 + scale_one) + shift_one).astype(low)
    qkv = mm(hidden_one, qkv_half).astype(low)
    attn_peers, lse_peers = attend(qkv, tokens, 1, splits - 1)
    peer_rows = [attn_peers[r * tokens : (r + 1) * tokens] for r in range(splits - 1)]
    arrived = [send(value, r + 1) for r, value in enumerate(peer_rows)]
    attn_own, lse_own = attend(qkv, tokens, 0, 1)
    attn_rows = in_order([attn_own] + arrived[::-1], 1)
    branch_one = mm(attn_rows, out_full)
    inputs = own_latents.astype(wide)
    middle = inputs + gate_one * branch_one
    normed_two, inverse_two = normalize(middle)
    hidden_two = (normed_two * (1.0 + scale_two) + shift_two).astype(low)

    hidden_pieces = everyone(hidden_two)
    branch_parts, grad_parts, term_up, term_down = [], [], 0.0, 0.0
    for hidden, grads in zip(hidden_pieces, grad_rows):
        up_values = mm(hidden, up_full)
        activated, gelu_back = jax.vjp(partial(jax.nn.gelu, approximate=True), up_values)
        activated = activated.astype(low)
        grad_up = gelu_back(mm(grads, down_full))[0].astype(low)
        grad_parts.append(mm(grad_up, up_full, NT))
        branch_parts.append(mm(activated, down_full, NT))
        term_up = term_up + mm(hidden, grad_up, TN)
        term_down = term_down + mm(grads, activated, TN)

    def send_parts(parts):
        return [send(parts[step].astype(low), step) for step in range(1, splits)]

    def add_parts(own, received):
        for value in received:
            own = own + value.astype(wide)
        return own

    term_up, term_down = term_up.astype(low), term_down.astype(low)
    grad_sent = send_parts(grad_parts)
    branch_sent = send_parts(branch_parts)
    grad_sent, term_up, term_down = lax.optimization_barrier((grad_sent, term_up, term_down))
    grad_hidden_two = add_parts(grad_parts[0], grad_sent)
    branch_two = add_parts(branch_parts[0], branch_sent)
    grad_w_down = lax.psum_scatter(term_down, "fsdp", scatter_dimension=0, tiled=True)
    grad_w_up = lax.psum_scatter(term_up, "fsdp", scatter_dimension=0, tiled=True)
    grad_mixed = own_cotangent.astype(wide)
    mixed = (middle + gate_two * branch_two).astype(low)
    grad_gate_two = jnp.sum(grad_mixed * branch_two, 0)
    grad_shift_two = jnp.sum(grad_hidden_two, 0)
    grad_scale_two = jnp.sum(grad_hidden_two * normed_two, 0)
    grad_middle = grad_mixed + norm_grad(
        normed_two, inverse_two, grad_hidden_two * (1.0 + scale_two)
    )
    grad_gate_one = jnp.sum(grad_middle * branch_one, 0)
    grad_branch_one = (gate_one * grad_middle).astype(low)

    grad_attn = mm(grad_branch_one, out_full, NT).astype(low)
    own_width = heads * HD
    grad_pieces = [
        lax.dynamic_slice_in_dim(grad_attn, ((me + r) % splits) * own_width, own_width, 1)
        for r in range(splits)
    ]
    grad_arrived = [send(grad_pieces[r], r) for r in range(1, splits)]
    grad_heads = jnp.concatenate([grad_pieces[0]] + grad_arrived[::-1], 0)
    attn_all = jnp.concatenate([attn_own, attn_peers], 0)
    lse = jnp.concatenate([lse_own, lse_peers], 2)
    delta = jnp.sum(
        (grad_heads.astype(wide) * attn_all.astype(wide)).reshape(-1, heads // 2, 2, HD), -1
    ).transpose(1, 2, 0)
    grad_qkv = attend_back(qkv, grad_heads, lse, delta)
    term_out = mm(attn_rows, grad_branch_one, TN)
    grad_w_out = scatter_rows(term_out.astype(low)).astype(low)
    term_qkv = mm(hidden_one, grad_qkv, TN)
    grad_w_qkv = scatter_rows(term_qkv.astype(low)).astype(low)
    hidden_grad_all = mm(grad_qkv, qkv_half, NT)
    grad_shift_one = jnp.sum(hidden_grad_all, 0)
    grad_scale_one = jnp.sum(hidden_grad_all * normed_all, 0)
    hidden_parts = [hidden_grad_all[r * tokens : (r + 1) * tokens] for r in range(splits)]
    grad_hidden_one = add_parts(hidden_parts[0], send_parts(hidden_parts))
    grad_latents = grad_middle + norm_grad(
        normed_all[:tokens], inverse_all[:tokens], grad_hidden_one * (1.0 + scale_one)
    )

    grad_mod = seq_sum(
        jnp.concatenate(
            [
                grad_shift_one,
                grad_scale_one,
                grad_gate_one,
                grad_shift_two,
                grad_scale_two,
                grad_gate_two,
            ]
        )[None]
    ).astype(low)
    grad_mod_cols = lax.all_to_all(grad_mod, "fsdp", split_axis=1, concat_axis=0, tiled=True)
    grad_w_ada = mm(cond_all, grad_mod_cols, TN)
    grad_b_ada = jnp.sum(grad_mod_cols.astype(wide), 0)
    cond_term = mm(grad_mod_cols, w_ada, NT).astype(low)
    cond_terms = lax.all_to_all(cond_term, "fsdp", split_axis=0, concat_axis=0, tiled=True)
    grad_cond = silu_back(jnp.sum(cond_terms.astype(wide), 0, keepdims=True))[0]

    grad_w_qkv = in_order(everyone(grad_w_qkv), 1).astype(wide)
    grad_w_out = seq_sum(grad_w_out)
    return (
        mixed[None],
        grad_latents[None],
        grad_cond,
        grad_w_qkv,
        grad_w_out,
        grad_w_up.astype(wide),
        grad_w_down.T.astype(wide),
        grad_w_ada,
        grad_b_ada,
    )


def solution(mesh):
    return jax.shard_map(
        partial(per_device, dict(mesh.shape)),
        mesh=mesh,
        in_specs=(
            P("fsdp", "seq", None),
            P("fsdp", None),
            P("fsdp", "seq", None),
            P("fsdp", None),
            P("fsdp", None),
            P("fsdp", "seq"),
            P("seq", "fsdp"),
            P(None, "fsdp"),
            P("fsdp"),
        ),
        out_specs=(
            P("fsdp", "seq", None),
            P("fsdp", "seq", None),
            P("fsdp", None),
            P("fsdp", None),
            P("fsdp", None),
            P("fsdp", "seq"),
            P("seq", "fsdp"),
            P(None, "fsdp"),
            P("fsdp"),
        ),
        check_vma=False,
    )
```

```python
from functools import partial

import jax
import jax.numpy as jnp
from jax import lax
from jax.experimental import pallas as pl
from jax.experimental.pallas import tpu as pltpu
from jax.sharding import PartitionSpec as P

H = 16
HD = 64
EPSILON = 1e-06
LOG2E = 1.4426950408889634
SCALE2 = HD**-0.5 * LOG2E
VMEM = 56 * 1024 * 1024
CHUNK = 256
ROOT = 0.7978845608028654
CUBE = 0.044715

NT = (((1,), (1,)), ((), ()))
TN = (((0,), (0,)), ((), ()))
NN = (((1,), (0,)), ((), ()))


def mm(a, b, dims=NN):
    return lax.dot_general(a, b, dims, preferred_element_type=jnp.float32)


def normalize(value_rows):
    center = value_rows - jnp.mean(value_rows, -1, keepdims=True)
    inverse = lax.rsqrt(jnp.mean(center * center, -1, keepdims=True) + EPSILON)
    return (center * inverse, inverse)


def norm_grad(normed, inverse, grad_normed):
    return inverse * (
        grad_normed
        - jnp.mean(grad_normed, -1, keepdims=True)
        - normed * jnp.mean(grad_normed * normed, -1, keepdims=True)
    )


def head_parts(ref, head, rows=slice(None)):
    base = head * 3 * HD
    return [ref[rows, base + j * HD : base + (j + 1) * HD] for j in range(3)]


def attend_kernel(query_ref, all_ref, out_ref, lse_ref):
    rows = query_ref.shape[0]
    for head in range(2):
        _, keys, values = head_parts(all_ref, head)
        chunk = min(CHUNK, rows)
        for at in range(0, rows, chunk):
            span = slice(at, at + chunk)
            queries = head_parts(query_ref, head, span)[0]
            scores = mm(keys, queries, NT)
            highest = jnp.max(scores, 0, keepdims=True)
            raised = jnp.exp2(scores * SCALE2 - highest * SCALE2)
            totals = jnp.sum(raised, 0, keepdims=True)
            result = mm(values, raised.astype(jnp.bfloat16), TN) / totals
            out_ref[span, head * HD : (head + 1) * HD] = result.T.astype(jnp.bfloat16)
            lse_ref[0, head : head + 1, span] = highest * SCALE2 + jnp.log2(totals)


def attend(qkv, tokens, first, count):
    length, columns = qkv.shape
    pairs = columns // (6 * HD)
    return pl.pallas_call(
        attend_kernel,
        grid=(pairs, count),
        in_specs=[
            pl.BlockSpec((tokens, 6 * HD), lambda p, b: (first + b, p)),
            pl.BlockSpec((length, 6 * HD), lambda p, b: (0, p)),
        ],
        out_specs=[
            pl.BlockSpec((tokens, 2 * HD), lambda p, b: (b, p)),
            pl.BlockSpec((1, 2, tokens), lambda p, b: (p, 0, b)),
        ],
        out_shape=[
            jax.ShapeDtypeStruct((count * tokens, pairs * 2 * HD), jnp.bfloat16),
            jax.ShapeDtypeStruct((pairs, 2, count * tokens), jnp.float32),
        ],
        compiler_params=pltpu.CompilerParams(vmem_limit_bytes=VMEM),
        cost_estimate=pl.CostEstimate(
            flops=4 * pairs * 2 * HD * length * count * tokens * 4,
            bytes_accessed=2 * length * columns,
            transcendentals=pairs * 2 * length * count * tokens,
        ),
        name="attend",
    )(qkv, qkv)


def feed_kernel(aliased, hidden_ref, grad_ref, up_ref, down_ref, *rest):
    act_ref, grad_up_ref, branch_ref, part_ref, branch_acc, part_acc = rest[2 * aliased :]
    step = pl.program_id(0)
    up_weights, down_weights = up_ref[...], down_ref[...]
    value = mm(hidden_ref[...], up_weights)
    grad_act = mm(grad_ref[...], down_weights)
    square = value * value
    tanh = jnp.tanh(ROOT * value * (1.0 + CUBE * square))
    half = 0.5 * (1.0 + tanh)
    act = (value * half).astype(jnp.bfloat16)
    slope = half + (0.5 * ROOT) * value * (1.0 - tanh * tanh) * (1.0 + 3.0 * CUBE * square)
    grad_up = (grad_act * slope).astype(jnp.bfloat16)
    act_ref[...] = act
    grad_up_ref[...] = grad_up
    part = mm(grad_up, up_weights, NT)
    branch = mm(act, down_weights, NT)

    @pl.when(step == 0)
    def _():
        part_acc[...] = part
        branch_acc[...] = branch

    @pl.when(step > 0)
    def _():
        part_acc[...] += part
        branch_acc[...] += branch

    @pl.when(step == pl.num_programs(0) - 1)
    def _():
        part_ref[...] = part_acc[...].astype(part_ref.dtype)
        branch_ref[...] = branch_acc[...].astype(branch_ref.dtype)


def feed(hidden, grads_all, up_full, down_full, piece, buffers, out_type):
    tokens, width = hidden.shape
    units = up_full.shape[1]
    block = min(512, units)
    length = grads_all.shape[0]
    weights = pl.BlockSpec((width, block), lambda j: (0, j))
    rows = pl.BlockSpec((tokens, block), lambda j: (piece, j))
    whole = pl.BlockSpec((tokens, width), lambda j: (0, 0))
    aliased = buffers is not None
    return pl.pallas_call(
        partial(feed_kernel, int(aliased)),
        grid=(units // block,),
        in_specs=[whole, pl.BlockSpec((tokens, width), lambda j: (piece, 0)), weights, weights]
        + [pl.BlockSpec(memory_space=pl.ANY)] * (2 * aliased),
        out_specs=[rows, rows, whole, whole],
        out_shape=[jax.ShapeDtypeStruct((length, units), jnp.bfloat16)] * 2
        + [jax.ShapeDtypeStruct((tokens, width), out_type)] * 2,
        scratch_shapes=[pltpu.VMEM((tokens, width), jnp.float32)] * 2,
        input_output_aliases={4: 0, 5: 1} if aliased else {},
        compiler_params=pltpu.CompilerParams(vmem_limit_bytes=VMEM),
        cost_estimate=pl.CostEstimate(
            flops=8 * tokens * width * units,
            bytes_accessed=4 * width * units + 8 * tokens * width + 4 * tokens * units,
            transcendentals=tokens * units,
        ),
        name="feed",
    )(hidden, grads_all, up_full, down_full, *(buffers or ()))


def attend_back_kernel(all_ref, grad_ref, lse_ref, delta_ref, out_ref, key_acc, value_acc):
    length = all_ref.shape[0]
    scaling = HD**-0.5
    for head in range(2):
        base = head * 3 * HD
        _, keys, values = head_parts(all_ref, head)
        for at in range(0, length, CHUNK):
            span = slice(at, at + CHUNK)
            queries = head_parts(all_ref, head, span)[0]
            grads = grad_ref[span, head * HD : (head + 1) * HD]
            lse = lse_ref[0, head : head + 1, span]
            delta = delta_ref[0, head : head + 1, span]
            probs = jnp.exp2(mm(keys, queries, NT) * SCALE2 - lse)
            score_grad = (probs * (mm(values, grads, NT) - delta)).astype(jnp.bfloat16)
            value_part = mm(probs.astype(jnp.bfloat16), grads)
            key_part = mm(score_grad, queries)
            if at == 0:
                value_acc[...] = value_part
                key_acc[...] = key_part
            else:
                value_acc[...] += value_part
                key_acc[...] += key_part
            query_grad = mm(keys, score_grad, TN) * scaling
            out_ref[span, base : base + HD] = query_grad.T.astype(jnp.bfloat16)
        out_ref[:, base + HD : base + 2 * HD] = (key_acc[...] * scaling).astype(jnp.bfloat16)
        out_ref[:, base + 2 * HD : base + 3 * HD] = value_acc[...].astype(jnp.bfloat16)


def attend_back(qkv, grad_attn, lse, delta, first, pairs):
    length = qkv.shape[0]
    columns = pairs * 6 * HD
    return pl.pallas_call(
        attend_back_kernel,
        grid=(pairs,),
        in_specs=[
            pl.BlockSpec((length, 6 * HD), lambda p: (0, first + p)),
            pl.BlockSpec((length, 2 * HD), lambda p: (0, first + p)),
            pl.BlockSpec((1, 2, length), lambda p: (first + p, 0, 0)),
            pl.BlockSpec((1, 2, length), lambda p: (first + p, 0, 0)),
        ],
        out_specs=pl.BlockSpec((length, 6 * HD), lambda p: (0, p)),
        out_shape=jax.ShapeDtypeStruct((length, columns), jnp.bfloat16),
        scratch_shapes=[
            pltpu.VMEM((length, HD), jnp.float32),
            pltpu.VMEM((length, HD), jnp.float32),
        ],
        compiler_params=pltpu.CompilerParams(vmem_limit_bytes=VMEM),
        cost_estimate=pl.CostEstimate(
            flops=10 * pairs * 2 * HD * length * length * 4,
            bytes_accessed=4 * length * columns,
            transcendentals=pairs * 2 * length * length,
        ),
        name="attend_back",
    )(qkv, grad_attn, lse, delta)


def per_device(sizes, latents, cond, cotangent, w_qkv, w_out, w_up, w_down, w_ada, b_ada):
    shards, splits = sizes["fsdp"], sizes["seq"]
    me = lax.axis_index("seq")
    tokens, width = latents.shape[1:]
    heads = H // splits
    low = jnp.bfloat16
    wide = jnp.float32

    def fetch(value, step):
        return lax.ppermute(value, "seq", [((i + step) % splits, i) for i in range(splits)])

    def send(value, step):
        return lax.ppermute(value, "seq", [(i, (i + step) % splits) for i in range(splits)])

    def everyone(value):
        return [value] + [fetch(value, step) for step in range(1, splits)]

    def in_order(pieces, axis):
        if splits == 1:
            return pieces[0]
        return jnp.concatenate(
            [
                lax.select_n(
                    (position - me) % splits == 1, *pieces
                ) if splits == 2 else
                lax.dynamic_index_in_dim(
                    jnp.stack(pieces), (position - me) % splits, 0, keepdims=False
                )
                for position in range(splits)
            ],
            axis,
        )

    def seq_sum(value):
        if splits != 2:
            return lax.psum(value, "seq").astype(wide)
        return value.astype(wide) + fetch(value, 1).astype(wide)

    spot = lax.axis_index("fsdp")
    depth = shards // 4
    core_at, x_at, z_at = spot % 2, (spot // 2) % 2, spot // 4

    def core_swap(value):
        return lax.ppermute(value, "fsdp", [(i, i ^ 1) for i in range(shards)])

    def x_swap(value):
        return lax.ppermute(value, "fsdp", [(i, i ^ 2) for i in range(shards)])

    def z_send(value, step):
        return lax.ppermute(value, "fsdp", [(i, (i + 4 * step) % shards) for i in range(shards)])

    def two(mine, other, at):
        return jnp.stack(
            [jnp.where(at == 0, mine, other), jnp.where(at == 0, other, mine)], 1
        )

    def gather_z(shard):
        return [shard] + [z_send(shard, step) for step in range(1, depth)]

    def gather_x(pieces):
        rows, cols = pieces[0].shape
        line = jnp.zeros((depth, rows, cols), pieces[0].dtype)
        for step, piece in enumerate(pieces):
            line = lax.dynamic_update_slice_in_dim(line, piece[None], (z_at - step) % depth, 0)
        return line, x_swap(line)

    def gather_core(pair):
        rows, cols = pair[0].shape[1:]
        plane = two(*pair, x_at).reshape(2 * depth, rows, cols)
        return plane, core_swap(plane)

    def gather_end(pair):
        rows, cols = pair[0].shape[1:]
        return two(*pair, core_at).reshape(shards * rows, cols)

    def halve(value, at, swap):
        mine = lax.dynamic_index_in_dim(value, at, 1, keepdims=False)
        other = lax.dynamic_index_in_dim(value, 1 - at, 1, keepdims=False)
        return mine, swap(other)

    def add(pair):
        return (pair[0].astype(wide) + pair[1].astype(wide)).astype(low)

    def scatter_core(value):
        rows, cols = value.shape[0] // shards, value.shape[1]
        return halve(value.reshape(2 * depth, 2, rows, cols), core_at, core_swap)

    def scatter_x(pair):
        rows, cols = pair[0].shape[1:]
        return halve(add(pair).reshape(depth, 2, rows, cols), x_at, x_swap)

    def scatter_z(pair):
        value = add(pair)
        pieces = [lax.dynamic_index_in_dim(value, z_at, 0, keepdims=False)]
        for step in range(1, depth):
            piece = lax.dynamic_index_in_dim(value, (z_at + step) % depth, 0, keepdims=False)
            pieces.append(z_send(piece, step))
        return pieces

    def scatter_end(pieces):
        total = pieces[0].astype(wide)
        for piece in pieces[1:]:
            total = total + piece.astype(wide)
        return total

    after = lax.optimization_barrier
    own_latents, own_cotangent = latents[0], cotangent[0]
    cond_act, silu_back = jax.vjp(jax.nn.silu, cond.astype(wide))
    cond_all = lax.all_to_all(
        jnp.broadcast_to(cond_act.astype(low), (shards, width)),
        "fsdp",
        split_axis=0,
        concat_axis=0,
        tiled=True,
    )
    cond_all, out_shard, up_shard = after((cond_all, w_out, w_up))
    out_pieces, up_pieces = gather_z(out_shard), gather_z(up_shard)
    mod_cols = (mm(cond_all, w_ada) + b_ada.astype(wide)).astype(low)
    modulation = lax.all_to_all(
        mod_cols, "fsdp", split_axis=0, concat_axis=1, tiled=True
    ).astype(wide)
    modulation, out_pieces, up_pieces = after((modulation, out_pieces, up_pieces))
    out_pair, up_pair = gather_x(out_pieces), gather_x(up_pieces)
    shift_one, scale_one, gate_one, shift_two, scale_two, gate_two = [
        modulation[:, position * width : (position + 1) * width] for position in range(6)
    ]
    columns = heads * 3 * HD
    qkv_shard = lax.dynamic_slice_in_dim(w_qkv, me * columns, columns, 1)
    qkv_half = lax.all_gather(qkv_shard, "fsdp", axis=0, tiled=True)
    down_full = lax.all_gather(w_down.T, "fsdp", axis=0, tiled=True)

    latents_all = jnp.concatenate(everyone(own_latents), 0)
    cotangent_all = jnp.concatenate(everyone(own_cotangent), 0)
    grad_rows = (gate_two * cotangent_all.astype(wide)).astype(low)

    normed_all, inverse_all = normalize(latents_all.astype(wide))
    hidden_one = (normed_all * (1.0 + scale_one) + shift_one).astype(low)
    qkv = mm(hidden_one, qkv_half).astype(low)
    attn_peers, lse_peers = attend(qkv, tokens, 1, splits - 1)
    attn_peers, out_pair = after((attn_peers, out_pair))
    out_pair = gather_core(out_pair)
    peer_rows = [attn_peers[r * tokens : (r + 1) * tokens] for r in range(splits - 1)]
    arrived = [send(value, r + 1) for r, value in enumerate(peer_rows)]
    attn_own, lse_own = attend(qkv, tokens, 0, 1)
    attn_own, out_pair, up_pair = after((attn_own, out_pair, up_pair))
    out_full, up_pair = gather_end(out_pair), gather_core(up_pair)
    attn_rows = in_order([attn_own] + arrived[::-1], 1)
    branch_one = mm(attn_rows, out_full)
    inputs = own_latents.astype(wide)
    middle = inputs + gate_one * branch_one
    normed_two, inverse_two = normalize(middle)
    hidden_two = (normed_two * (1.0 + scale_two) + shift_two).astype(low)

    hidden_pieces = everyone(hidden_two)
    up_full = gather_end(up_pair)
    buffers, grad_parts, branch_parts = None, [], []
    for piece in range(splits):
        act, grad_up, branch_part, grad_part = feed(
            hidden_pieces[piece],
            grad_rows,
            up_full,
            down_full,
            piece,
            buffers,
            low if piece else wide,
        )
        buffers = (act, grad_up)
        grad_parts.append(grad_part)
        branch_parts.append(branch_part)
        if piece + 1 < splits:
            hidden_pieces[piece + 1], buffers = after((hidden_pieces[piece + 1], buffers))

    def send_parts(parts):
        return [send(parts[step].astype(low), step) for step in range(1, splits)]

    def add_parts(own, received):
        for value in received:
            own = own + value.astype(wide)
        return own

    grad_sent = send_parts(grad_parts)
    term_up = mm(jnp.concatenate(hidden_pieces, 0), grad_up, TN).astype(low)
    up_pair = scatter_core(term_up)
    term_down = mm(grad_rows, act, TN).astype(low)
    grad_w_down = lax.psum_scatter(term_down, "fsdp", scatter_dimension=0, tiled=True)
    grad_sent, up_pair, term_down, branch_parts = after(
        (grad_sent, up_pair, term_down, branch_parts)
    )
    up_pair = scatter_x(up_pair)
    grad_hidden_two = add_parts(grad_parts[0], grad_sent)
    grad_mixed = own_cotangent.astype(wide)
    grad_shift_two = jnp.sum(grad_hidden_two, 0)
    grad_scale_two = jnp.sum(grad_hidden_two * normed_two, 0)
    grad_middle = grad_mixed + norm_grad(
        normed_two, inverse_two, grad_hidden_two * (1.0 + scale_two)
    )
    grad_gate_one = jnp.sum(grad_middle * branch_one, 0)
    grad_branch_one = (gate_one * grad_middle).astype(low)

    grad_attn = mm(grad_branch_one, out_full, NT).astype(low)
    own_width = heads * HD
    grad_pieces = [
        lax.dynamic_slice_in_dim(grad_attn, ((me + r) % splits) * own_width, own_width, 1)
        for r in range(splits)
    ]
    grad_arrived = [send(grad_pieces[r], r) for r in range(1, splits)]
    term_out = mm(attn_rows, grad_branch_one, TN).astype(low)
    out_pair = scatter_core(term_out)
    grad_arrived, branch_parts, up_pair, out_pair = after(
        (grad_arrived, branch_parts, up_pair, out_pair)
    )
    branch_sent = send_parts(branch_parts)
    up_pieces, out_pair = scatter_z(up_pair), scatter_x(out_pair)
    grad_heads = jnp.concatenate([grad_pieces[0]] + grad_arrived[::-1], 0)
    attn_all = jnp.concatenate([attn_own, attn_peers], 0)
    lse = jnp.concatenate([lse_own, lse_peers], 2)
    delta = jnp.sum(
        (grad_heads.astype(wide) * attn_all.astype(wide)).reshape(-1, heads // 2, 2, HD), -1
    ).transpose(1, 2, 0)
    pairs = heads // 2
    groups = 2 if pairs % 2 == 0 else 1
    each = pairs // groups
    grad_qkv, qkv_pairs = [], []
    for group in range(groups):
        grad_qkv.append(attend_back(qkv, grad_heads, lse, delta, group * each, each))
        term_qkv = mm(hidden_one, grad_qkv[-1], TN).astype(low)
        pair = scatter_core(term_qkv)
        if group + 1 < groups:
            pair, grad_heads, out_pair = after((pair, grad_heads, out_pair))
            out_pieces = scatter_z(out_pair)
            pair = scatter_x(pair)
        else:
            pair, grad_qkv = after((pair, grad_qkv))
        qkv_pairs.append(pair)
    if groups == 1:
        out_pieces = scatter_z(out_pair)
    size = each * 6 * HD
    hidden_grad_all = sum(
        mm(value, qkv_half[:, group * size : (group + 1) * size], NT)
        for group, value in enumerate(grad_qkv)
    )
    grad_shift_one = jnp.sum(hidden_grad_all, 0)
    grad_scale_one = jnp.sum(hidden_grad_all * normed_all, 0)
    hidden_parts = [hidden_grad_all[r * tokens : (r + 1) * tokens] for r in range(splits)]
    hidden_sent = send_parts(hidden_parts)
    qkv_pairs[-1] = scatter_x(qkv_pairs[-1])
    grad_w_up = scatter_end(up_pieces)
    grad_w_out = scatter_end(out_pieces).astype(low)
    grad_w_qkv = jnp.concatenate(
        [scatter_end(scatter_z(pair)).astype(low) for pair in qkv_pairs], 1
    )
    branch_two = add_parts(branch_parts[0], branch_sent)
    mixed = (middle + gate_two * branch_two).astype(low)
    grad_gate_two = jnp.sum(grad_mixed * branch_two, 0)
    grad_hidden_one = add_parts(hidden_parts[0], hidden_sent)
    grad_latents = grad_middle + norm_grad(
        normed_all[:tokens], inverse_all[:tokens], grad_hidden_one * (1.0 + scale_one)
    )

    grad_mod = seq_sum(
        jnp.concatenate(
            [
                grad_shift_one,
                grad_scale_one,
                grad_gate_one,
                grad_shift_two,
                grad_scale_two,
                grad_gate_two,
            ]
        )[None]
    ).astype(low)
    grad_mod_cols = lax.all_to_all(grad_mod, "fsdp", split_axis=1, concat_axis=0, tiled=True)
    grad_w_ada = mm(cond_all, grad_mod_cols, TN)
    grad_b_ada = jnp.sum(grad_mod_cols.astype(wide), 0)
    cond_term = mm(grad_mod_cols, w_ada, NT).astype(low)
    cond_terms = lax.all_to_all(cond_term, "fsdp", split_axis=0, concat_axis=0, tiled=True)
    grad_cond = silu_back(jnp.sum(cond_terms.astype(wide), 0, keepdims=True))[0]

    grad_w_qkv = in_order(everyone(grad_w_qkv), 1).astype(wide)
    grad_w_out = seq_sum(grad_w_out)
    return (
        mixed[None],
        grad_latents[None],
        grad_cond,
        grad_w_qkv,
        grad_w_out,
        grad_w_up,
        grad_w_down.T.astype(wide),
        grad_w_ada,
        grad_b_ada,
    )


def solution(mesh):
    return jax.shard_map(
        partial(per_device, dict(mesh.shape)),
        mesh=mesh,
        in_specs=(
            P("fsdp", "seq", None),
            P("fsdp", None),
            P("fsdp", "seq", None),
            P("fsdp", None),
            P("fsdp", None),
            P("fsdp", "seq"),
            P("seq", "fsdp"),
            P(None, "fsdp"),
            P("fsdp"),
        ),
        out_specs=(
            P("fsdp", "seq", None),
            P("fsdp", "seq", None),
            P("fsdp", None),
            P("fsdp", None),
            P("fsdp", None),
            P("fsdp", "seq"),
            P("seq", "fsdp"),
            P(None, "fsdp"),
            P("fsdp"),
        ),
        check_vma=False,
    )
```

```python
from functools import partial

import jax
import jax.numpy as jnp
from jax import lax
from jax.experimental import pallas as pl
from jax.experimental.pallas import tpu as pltpu
from jax.sharding import PartitionSpec as P

H = 16
HD = 64
EPSILON = 1e-06
LOG2E = 1.4426950408889634
SCALE2 = HD**-0.5 * LOG2E
VMEM = 56 * 1024 * 1024
CHUNK = 256
ROOT = 0.7978845608028654
CUBE = 0.044715

NT = (((1,), (1,)), ((), ()))
TN = (((0,), (0,)), ((), ()))
NN = (((1,), (0,)), ((), ()))


def mm(a, b, dims=NN):
    return lax.dot_general(a, b, dims, preferred_element_type=jnp.float32)


def normalize(value_rows):
    center = value_rows - jnp.mean(value_rows, -1, keepdims=True)
    inverse = lax.rsqrt(jnp.mean(center * center, -1, keepdims=True) + EPSILON)
    return (center * inverse, inverse)


def norm_grad(normed, inverse, grad_normed):
    return inverse * (
        grad_normed
        - jnp.mean(grad_normed, -1, keepdims=True)
        - normed * jnp.mean(grad_normed * normed, -1, keepdims=True)
    )


def head_parts(ref, head, rows=slice(None)):
    base = head * 3 * HD
    return [ref[rows, base + j * HD : base + (j + 1) * HD] for j in range(3)]


def attend_kernel(query_ref, all_ref, out_ref, lse_ref):
    rows = query_ref.shape[0]
    for head in range(2):
        _, keys, values = head_parts(all_ref, head)
        chunk = min(CHUNK, rows)
        for at in range(0, rows, chunk):
            span = slice(at, at + chunk)
            queries = head_parts(query_ref, head, span)[0]
            scores = mm(keys, queries, NT)
            highest = jnp.max(scores, 0, keepdims=True)
            raised = jnp.exp2(scores * SCALE2 - highest * SCALE2)
            totals = jnp.sum(raised, 0, keepdims=True)
            result = mm(values, raised.astype(jnp.bfloat16), TN) / totals
            out_ref[span, head * HD : (head + 1) * HD] = result.T.astype(jnp.bfloat16)
            lse_ref[0, head : head + 1, span] = highest * SCALE2 + jnp.log2(totals)


def attend(qkv, tokens, first, count):
    length, columns = qkv.shape
    pairs = columns // (6 * HD)
    return pl.pallas_call(
        attend_kernel,
        grid=(pairs, count),
        in_specs=[
            pl.BlockSpec((tokens, 6 * HD), lambda p, b: (first + b, p)),
            pl.BlockSpec((length, 6 * HD), lambda p, b: (0, p)),
        ],
        out_specs=[
            pl.BlockSpec((tokens, 2 * HD), lambda p, b: (b, p)),
            pl.BlockSpec((1, 2, tokens), lambda p, b: (p, 0, b)),
        ],
        out_shape=[
            jax.ShapeDtypeStruct((count * tokens, pairs * 2 * HD), jnp.bfloat16),
            jax.ShapeDtypeStruct((pairs, 2, count * tokens), jnp.float32),
        ],
        compiler_params=pltpu.CompilerParams(vmem_limit_bytes=VMEM),
        cost_estimate=pl.CostEstimate(
            flops=4 * pairs * 2 * HD * length * count * tokens * 4,
            bytes_accessed=2 * length * columns,
            transcendentals=pairs * 2 * length * count * tokens,
        ),
        name="attend",
    )(qkv, qkv)


def feed_kernel(aliased, hidden_ref, grad_ref, up_ref, down_ref, *rest):
    act_ref, grad_up_ref, branch_ref, part_ref, branch_acc, part_acc = rest[2 * aliased :]
    step = pl.program_id(0)
    up_weights, down_weights = up_ref[...], down_ref[...]
    value = mm(hidden_ref[...], up_weights)
    grad_act = mm(grad_ref[...], down_weights)
    square = value * value
    tanh = jnp.tanh(ROOT * value * (1.0 + CUBE * square))
    half = 0.5 * (1.0 + tanh)
    act = (value * half).astype(jnp.bfloat16)
    slope = half + (0.5 * ROOT) * value * (1.0 - tanh * tanh) * (1.0 + 3.0 * CUBE * square)
    grad_up = (grad_act * slope).astype(jnp.bfloat16)
    act_ref[...] = act
    grad_up_ref[...] = grad_up
    part = mm(grad_up, up_weights, NT)
    branch = mm(act, down_weights, NT)

    @pl.when(step == 0)
    def _():
        part_acc[...] = part
        branch_acc[...] = branch

    @pl.when(step > 0)
    def _():
        part_acc[...] += part
        branch_acc[...] += branch

    @pl.when(step == pl.num_programs(0) - 1)
    def _():
        part_ref[...] = part_acc[...].astype(part_ref.dtype)
        branch_ref[...] = branch_acc[...].astype(branch_ref.dtype)


def feed(hidden, grads_all, up_full, down_full, piece, buffers, out_type):
    tokens, width = hidden.shape
    units = up_full.shape[1]
    block = min(512, units)
    length = grads_all.shape[0]
    weights = pl.BlockSpec((width, block), lambda j: (0, j))
    rows = pl.BlockSpec((tokens, block), lambda j: (piece, j))
    whole = pl.BlockSpec((tokens, width), lambda j: (0, 0))
    aliased = buffers is not None
    return pl.pallas_call(
        partial(feed_kernel, int(aliased)),
        grid=(units // block,),
        in_specs=[whole, pl.BlockSpec((tokens, width), lambda j: (piece, 0)), weights, weights]
        + [pl.BlockSpec(memory_space=pl.ANY)] * (2 * aliased),
        out_specs=[rows, rows, whole, whole],
        out_shape=[jax.ShapeDtypeStruct((length, units), jnp.bfloat16)] * 2
        + [jax.ShapeDtypeStruct((tokens, width), out_type)] * 2,
        scratch_shapes=[pltpu.VMEM((tokens, width), jnp.float32)] * 2,
        input_output_aliases={4: 0, 5: 1} if aliased else {},
        compiler_params=pltpu.CompilerParams(vmem_limit_bytes=VMEM),
        cost_estimate=pl.CostEstimate(
            flops=8 * tokens * width * units,
            bytes_accessed=4 * width * units + 8 * tokens * width + 4 * tokens * units,
            transcendentals=tokens * units,
        ),
        name="feed",
    )(hidden, grads_all, up_full, down_full, *(buffers or ()))


def attend_back_kernel(all_ref, grad_ref, lse_ref, delta_ref, out_ref, key_acc, value_acc):
    length = all_ref.shape[0]
    scaling = HD**-0.5
    for head in range(2):
        base = head * 3 * HD
        _, keys, values = head_parts(all_ref, head)
        for at in range(0, length, CHUNK):
            span = slice(at, at + CHUNK)
            queries = head_parts(all_ref, head, span)[0]
            grads = grad_ref[span, head * HD : (head + 1) * HD]
            lse = lse_ref[0, head : head + 1, span]
            delta = delta_ref[0, head : head + 1, span]
            probs = jnp.exp2(mm(keys, queries, NT) * SCALE2 - lse)
            score_grad = (probs * (mm(values, grads, NT) - delta)).astype(jnp.bfloat16)
            value_part = mm(probs.astype(jnp.bfloat16), grads)
            key_part = mm(score_grad, queries)
            if at == 0:
                value_acc[...] = value_part
                key_acc[...] = key_part
            else:
                value_acc[...] += value_part
                key_acc[...] += key_part
            query_grad = mm(keys, score_grad, TN) * scaling
            out_ref[span, base : base + HD] = query_grad.T.astype(jnp.bfloat16)
        out_ref[:, base + HD : base + 2 * HD] = (key_acc[...] * scaling).astype(jnp.bfloat16)
        out_ref[:, base + 2 * HD : base + 3 * HD] = value_acc[...].astype(jnp.bfloat16)


def attend_back(qkv, grad_attn, lse, delta, first, pairs):
    length = qkv.shape[0]
    columns = pairs * 6 * HD
    return pl.pallas_call(
        attend_back_kernel,
        grid=(pairs,),
        in_specs=[
            pl.BlockSpec((length, 6 * HD), lambda p: (0, first + p)),
            pl.BlockSpec((length, 2 * HD), lambda p: (0, first + p)),
            pl.BlockSpec((1, 2, length), lambda p: (first + p, 0, 0)),
            pl.BlockSpec((1, 2, length), lambda p: (first + p, 0, 0)),
        ],
        out_specs=pl.BlockSpec((length, 6 * HD), lambda p: (0, p)),
        out_shape=jax.ShapeDtypeStruct((length, columns), jnp.bfloat16),
        scratch_shapes=[
            pltpu.VMEM((length, HD), jnp.float32),
            pltpu.VMEM((length, HD), jnp.float32),
        ],
        compiler_params=pltpu.CompilerParams(vmem_limit_bytes=VMEM),
        cost_estimate=pl.CostEstimate(
            flops=10 * pairs * 2 * HD * length * length * 4,
            bytes_accessed=4 * length * columns,
            transcendentals=pairs * 2 * length * length,
        ),
        name="attend_back",
    )(qkv, grad_attn, lse, delta)


def per_device(sizes, latents, cond, cotangent, w_qkv, w_out, w_up, w_down, w_ada, b_ada):
    shards, splits = sizes["fsdp"], sizes["seq"]
    me = lax.axis_index("seq")
    tokens, width = latents.shape[1:]
    heads = H // splits
    low = jnp.bfloat16
    wide = jnp.float32

    def fetch(value, step):
        return lax.ppermute(value, "seq", [((i + step) % splits, i) for i in range(splits)])

    def send(value, step):
        return lax.ppermute(value, "seq", [(i, (i + step) % splits) for i in range(splits)])

    def everyone(value):
        return [value] + [fetch(value, step) for step in range(1, splits)]

    def in_order(pieces, axis):
        if splits == 1:
            return pieces[0]
        return jnp.concatenate(
            [
                lax.select_n(
                    (position - me) % splits == 1, *pieces
                ) if splits == 2 else
                lax.dynamic_index_in_dim(
                    jnp.stack(pieces), (position - me) % splits, 0, keepdims=False
                )
                for position in range(splits)
            ],
            axis,
        )

    def seq_sum(value):
        if splits != 2:
            return lax.psum(value, "seq").astype(wide)
        return value.astype(wide) + fetch(value, 1).astype(wide)

    spot = lax.axis_index("fsdp")
    depth = shards // 4
    core_at, x_at, z_at = spot % 2, (spot // 2) % 2, spot // 4

    def core_swap(value):
        return lax.ppermute(value, "fsdp", [(i, i ^ 1) for i in range(shards)])

    def x_swap(value):
        return lax.ppermute(value, "fsdp", [(i, i ^ 2) for i in range(shards)])

    def z_send(value, step):
        return lax.ppermute(value, "fsdp", [(i, (i + 4 * step) % shards) for i in range(shards)])

    def two(mine, other, at):
        return jnp.stack(
            [jnp.where(at == 0, mine, other), jnp.where(at == 0, other, mine)], 1
        )

    def gather_z(shard):
        return [shard] + [z_send(shard, step) for step in range(1, depth)]

    def gather_x(pieces):
        rows, cols = pieces[0].shape
        line = jnp.zeros((depth, rows, cols), pieces[0].dtype)
        for step, piece in enumerate(pieces):
            line = lax.dynamic_update_slice_in_dim(line, piece[None], (z_at - step) % depth, 0)
        return line, x_swap(line)

    def gather_core(pair):
        rows, cols = pair[0].shape[1:]
        plane = two(*pair, x_at).reshape(2 * depth, rows, cols)
        return plane, core_swap(plane)

    def gather_end(pair):
        rows, cols = pair[0].shape[1:]
        return two(*pair, core_at).reshape(shards * rows, cols)

    def halve(value, at, swap):
        mine = lax.dynamic_index_in_dim(value, at, 1, keepdims=False)
        other = lax.dynamic_index_in_dim(value, 1 - at, 1, keepdims=False)
        return mine, swap(other)

    def add(pair):
        return (pair[0].astype(wide) + pair[1].astype(wide)).astype(low)

    def scatter_core(value):
        rows, cols = value.shape[0] // shards, value.shape[1]
        return halve(value.reshape(2 * depth, 2, rows, cols), core_at, core_swap)

    def scatter_x(pair):
        rows, cols = pair[0].shape[1:]
        return halve(add(pair).reshape(depth, 2, rows, cols), x_at, x_swap)

    def scatter_z(pair):
        value = add(pair)
        pieces = [lax.dynamic_index_in_dim(value, z_at, 0, keepdims=False)]
        for step in range(1, depth):
            piece = lax.dynamic_index_in_dim(value, (z_at + step) % depth, 0, keepdims=False)
            pieces.append(z_send(piece, step))
        return pieces

    def scatter_end(pieces):
        total = pieces[0].astype(wide)
        for piece in pieces[1:]:
            total = total + piece.astype(wide)
        return total

    after = lax.optimization_barrier
    own_latents, own_cotangent = latents[0], cotangent[0]
    cond_act, silu_back = jax.vjp(jax.nn.silu, cond.astype(wide))
    cond_all = lax.all_to_all(
        jnp.broadcast_to(cond_act.astype(low), (shards, width)),
        "fsdp",
        split_axis=0,
        concat_axis=0,
        tiled=True,
    )
    mod_cols = (mm(cond_all, w_ada) + b_ada.astype(wide)).astype(low)
    peer_latents = [fetch(own_latents, step) for step in range(1, splits)]
    mod_cols, peer_latents = after((mod_cols, peer_latents))
    modulation = lax.all_to_all(
        mod_cols, "fsdp", split_axis=0, concat_axis=1, tiled=True
    ).astype(wide)
    modulation, out_shard = after((modulation, w_out))
    out_pieces = gather_z(out_shard)
    shift_one, scale_one, gate_one, shift_two, scale_two, gate_two = [
        modulation[:, position * width : (position + 1) * width] for position in range(6)
    ]
    columns = heads * 3 * HD
    qkv_shard = lax.dynamic_slice_in_dim(w_qkv, me * columns, columns, 1)
    qkv_half = lax.all_gather(qkv_shard, "fsdp", axis=0, tiled=True)
    up_down = lax.all_gather(jnp.concatenate([w_up, w_down.T], 1), "fsdp", axis=0, tiled=True)
    units = w_up.shape[1]

    latents_all = jnp.concatenate([own_latents] + peer_latents, 0)
    cotangent_all = jnp.concatenate(everyone(own_cotangent), 0)
    grad_rows = (gate_two * cotangent_all.astype(wide)).astype(low)

    normed_all, inverse_all = normalize(latents_all.astype(wide))
    hidden_one = (normed_all * (1.0 + scale_one) + shift_one).astype(low)
    qkv = mm(hidden_one, qkv_half).astype(low)
    qkv, out_pieces = after((qkv, out_pieces))
    out_pair = gather_x(out_pieces)
    attn_peers, lse_peers = attend(qkv, tokens, 1, splits - 1)
    attn_peers, qkv, out_pair = after((attn_peers, qkv, out_pair))
    out_pair = gather_core(out_pair)
    blocks = [None] + [attn_peers[r * tokens : (r + 1) * tokens] for r in range(splits - 1)]
    theirs = [{} for _ in range(splits)]
    for r in range(1, splits):
        for q in range(1, splits):
            theirs[(r + q) % splits][q] = fetch(blocks[r], q)
    attn_own, lse_own = attend(qkv, tokens, 0, 1)
    blocks[0] = attn_own
    attn_own, out_pair, theirs = after((attn_own, out_pair, theirs))
    for q in range(1, splits):
        theirs[q][q] = fetch(attn_own, q)
    out_full = gather_end(out_pair)

    def to_feed(rows, heads_of, piece):
        inputs = latents_all[piece * tokens : (piece + 1) * tokens].astype(wide)
        attn_rows = in_order([rows] + [heads_of[q] for q in range(1, splits)], 1)
        branch_one = mm(attn_rows, out_full)
        middle = inputs + gate_one * branch_one
        normed, inverse = normalize(middle)
        hidden = (normed * (1.0 + scale_two) + shift_two).astype(low)
        return hidden, attn_rows, branch_one, middle, normed, inverse

    own_theirs = theirs[0]
    hidden_two, attn_rows, branch_one, middle, normed_two, inverse_two = to_feed(
        attn_own, own_theirs, 0
    )
    hidden_two, theirs = after((hidden_two, theirs))
    hidden_pieces = [hidden_two] + [
        to_feed(blocks[r], theirs[r], r)[0] for r in range(1, splits)
    ]

    up_full, down_full = up_down[:, :units], up_down[:, units:]
    buffers, grad_parts, branch_parts = None, [], []
    for piece in range(splits):
        act, grad_up, branch_part, grad_part = feed(
            hidden_pieces[piece],
            grad_rows,
            up_full,
            down_full,
            piece,
            buffers,
            low if piece else wide,
        )
        buffers = (act, grad_up)
        grad_parts.append(grad_part)
        branch_parts.append(branch_part)

    def send_parts(parts):
        return [send(parts[step].astype(low), step) for step in range(1, splits)]

    def add_parts(own, received):
        for value in received:
            own = own + value.astype(wide)
        return own

    grad_sent = send_parts(grad_parts)
    term_down = mm(grad_rows, act, TN).astype(low)
    term_up = mm(jnp.concatenate(hidden_pieces, 0), grad_up, TN).astype(low)
    up_pair = scatter_core(term_up)
    grad_w_down = lax.psum_scatter(term_down, "fsdp", scatter_dimension=0, tiled=True)
    grad_sent, up_pair, term_down, branch_parts = after(
        (grad_sent, up_pair, term_down, branch_parts)
    )
    up_pair = scatter_x(up_pair)
    grad_hidden_two = add_parts(grad_parts[0], grad_sent)
    grad_mixed = own_cotangent.astype(wide)
    grad_shift_two = jnp.sum(grad_hidden_two, 0)
    grad_scale_two = jnp.sum(grad_hidden_two * normed_two, 0)
    grad_middle = grad_mixed + norm_grad(
        normed_two, inverse_two, grad_hidden_two * (1.0 + scale_two)
    )
    grad_gate_one = jnp.sum(grad_middle * branch_one, 0)
    grad_branch_one = (gate_one * grad_middle).astype(low)

    grad_attn = mm(grad_branch_one, out_full, NT).astype(low)
    own_width = heads * HD
    grad_pieces = [
        lax.dynamic_slice_in_dim(grad_attn, ((me + r) % splits) * own_width, own_width, 1)
        for r in range(splits)
    ]
    grad_arrived = [send(grad_pieces[r], r) for r in range(1, splits)]
    term_out = mm(attn_rows, grad_branch_one, TN).astype(low)
    out_pair = scatter_core(term_out)
    grad_arrived, branch_parts, out_pair = after((grad_arrived, branch_parts, out_pair))
    branch_sent = send_parts(branch_parts)
    out_pair = scatter_x(out_pair)
    grad_heads = jnp.concatenate([grad_pieces[0]] + grad_arrived[::-1], 0)
    attn_all = jnp.concatenate([attn_own, attn_peers], 0)
    lse = jnp.concatenate([lse_own, lse_peers], 2)
    delta = jnp.sum(
        (grad_heads.astype(wide) * attn_all.astype(wide)).reshape(-1, heads // 2, 2, HD), -1
    ).transpose(1, 2, 0)
    pairs = heads // 2
    groups = 2 if pairs % 2 == 0 else 1
    each = pairs // groups
    size = each * 6 * HD
    qkv_pieces, hidden_grads = [], []
    for group in range(groups):
        if group:
            qkv_pair, grad_heads = after((qkv_pair, grad_heads))
            qkv_pair = scatter_x(qkv_pair)
        value = attend_back(qkv, grad_heads, lse, delta, group * each, each)
        if group == 0:
            value, up_pair, out_pair = after((value, up_pair, out_pair))
            up_pieces, out_pieces = scatter_z(up_pair), scatter_z(out_pair)
        else:
            value, qkv_pair, up_pieces, out_pieces, branch_sent = after(
                (value, qkv_pair, up_pieces, out_pieces, branch_sent)
            )
            qkv_pieces = scatter_z(qkv_pair)
        term_qkv = mm(hidden_one, value, TN).astype(low)
        qkv_pair = scatter_core(term_qkv)
        term_qkv, value = after((term_qkv, value))
        hidden_grads.append((value, qkv_half[:, group * size : (group + 1) * size]))
    hidden_grad_all = sum(mm(value, weight, NT) for value, weight in hidden_grads)
    grad_shift_one = jnp.sum(hidden_grad_all, 0)
    grad_scale_one = jnp.sum(hidden_grad_all * normed_all, 0)
    branch_two = add_parts(branch_parts[0], branch_sent)
    grad_gate_two = jnp.sum(grad_mixed * branch_two, 0)

    grad_mod_part = jnp.concatenate(
        [
            grad_shift_one,
            grad_scale_one,
            grad_gate_one,
            grad_shift_two,
            grad_scale_two,
            grad_gate_two,
        ]
    )[None]
    grad_mod = seq_sum(grad_mod_part).astype(low)
    hidden_parts = [hidden_grad_all[r * tokens : (r + 1) * tokens] for r in range(splits)]
    qkv_pair, grad_mod, hidden_parts = after((qkv_pair, grad_mod, hidden_parts))
    hidden_sent = send_parts(hidden_parts)
    qkv_pair = scatter_x(qkv_pair)
    grad_w_out = seq_sum(scatter_end(out_pieces).astype(low))
    grad_w_up = scatter_end(up_pieces)
    mixed = (middle + gate_two * branch_two).astype(low)
    grad_mod_cols = lax.all_to_all(grad_mod, "fsdp", split_axis=1, concat_axis=0, tiled=True)
    grad_w_ada = mm(cond_all, grad_mod_cols, TN)
    grad_b_ada = jnp.sum(grad_mod_cols.astype(wide), 0)
    cond_term = mm(grad_mod_cols, w_ada, NT).astype(low)
    cond_term, qkv_pair, qkv_pieces, mixed = after((cond_term, qkv_pair, qkv_pieces, mixed))
    shards_qkv = [scatter_end(qkv_pieces).astype(low)] if groups == 2 else []
    qkv_pieces = scatter_z(qkv_pair)
    cond_terms = lax.all_to_all(cond_term, "fsdp", split_axis=0, concat_axis=0, tiled=True)
    grad_cond = silu_back(jnp.sum(cond_terms.astype(wide), 0, keepdims=True))[0]
    grad_hidden_one = add_parts(hidden_parts[0], hidden_sent)
    grad_latents = grad_middle + norm_grad(
        normed_all[:tokens], inverse_all[:tokens], grad_hidden_one * (1.0 + scale_one)
    )
    qkv_pieces, grad_latents, grad_cond = after((qkv_pieces, grad_latents, grad_cond))
    shards_qkv.append(scatter_end(qkv_pieces).astype(low))
    grad_w_qkv = in_order(everyone(jnp.concatenate(shards_qkv, 1)), 1).astype(wide)
    return (
        mixed[None],
        grad_latents[None],
        grad_cond,
        grad_w_qkv,
        grad_w_out,
        grad_w_up,
        grad_w_down.T.astype(wide),
        grad_w_ada,
        grad_b_ada,
    )


def solution(mesh):
    return jax.shard_map(
        partial(per_device, dict(mesh.shape)),
        mesh=mesh,
        in_specs=(
            P("fsdp", "seq", None),
            P("fsdp", None),
            P("fsdp", "seq", None),
            P("fsdp", None),
            P("fsdp", None),
            P("fsdp", "seq"),
            P("seq", "fsdp"),
            P(None, "fsdp"),
            P("fsdp"),
        ),
        out_specs=(
            P("fsdp", "seq", None),
            P("fsdp", "seq", None),
            P("fsdp", None),
            P("fsdp", None),
            P("fsdp", None),
            P("fsdp", "seq"),
            P("seq", "fsdp"),
            P(None, "fsdp"),
            P("fsdp"),
        ),
        check_vma=False,
    )
```

```python
from functools import partial

import jax
import jax.numpy as jnp
from jax import lax
from jax.experimental import pallas as pl
from jax.experimental.pallas import tpu as pltpu
from jax.sharding import PartitionSpec as P

H = 16
HD = 64
EPSILON = 1e-06
LOG2E = 1.4426950408889634
SCALE2 = HD**-0.5 * LOG2E
VMEM = 56 * 1024 * 1024
CHUNK = 256
ROOT = 0.7978845608028654
CUBE = 0.044715

NT = (((1,), (1,)), ((), ()))
TN = (((0,), (0,)), ((), ()))
NN = (((1,), (0,)), ((), ()))


def mm(a, b, dims=NN):
    return lax.dot_general(a, b, dims, preferred_element_type=jnp.float32)


def normalize(value_rows):
    center = value_rows - jnp.mean(value_rows, -1, keepdims=True)
    inverse = lax.rsqrt(jnp.mean(center * center, -1, keepdims=True) + EPSILON)
    return (center * inverse, inverse)


def norm_grad(normed, inverse, grad_normed):
    return inverse * (
        grad_normed
        - jnp.mean(grad_normed, -1, keepdims=True)
        - normed * jnp.mean(grad_normed * normed, -1, keepdims=True)
    )


def head_parts(ref, head, rows=slice(None)):
    base = head * 3 * HD
    return [ref[rows, base + j * HD : base + (j + 1) * HD] for j in range(3)]


def attend_kernel(query_ref, all_ref, out_ref, lse_ref):
    rows = query_ref.shape[0]
    for head in range(2):
        _, keys, values = head_parts(all_ref, head)
        chunk = min(CHUNK, rows)
        for at in range(0, rows, chunk):
            span = slice(at, at + chunk)
            queries = head_parts(query_ref, head, span)[0]
            scores = mm(keys, queries, NT)
            highest = jnp.max(scores, 0, keepdims=True)
            raised = jnp.exp2(scores * SCALE2 - highest * SCALE2)
            totals = jnp.sum(raised, 0, keepdims=True)
            result = mm(values, raised.astype(jnp.bfloat16), TN) / totals
            out_ref[span, head * HD : (head + 1) * HD] = result.T.astype(jnp.bfloat16)
            lse_ref[0, head : head + 1, span] = highest * SCALE2 + jnp.log2(totals)


def attend(qkv, tokens, first, count):
    length, columns = qkv.shape
    pairs = columns // (6 * HD)
    return pl.pallas_call(
        attend_kernel,
        grid=(pairs, count),
        in_specs=[
            pl.BlockSpec((tokens, 6 * HD), lambda p, b: (first + b, p)),
            pl.BlockSpec((length, 6 * HD), lambda p, b: (0, p)),
        ],
        out_specs=[
            pl.BlockSpec((tokens, 2 * HD), lambda p, b: (b, p)),
            pl.BlockSpec((1, 2, tokens), lambda p, b: (p, 0, b)),
        ],
        out_shape=[
            jax.ShapeDtypeStruct((count * tokens, pairs * 2 * HD), jnp.bfloat16),
            jax.ShapeDtypeStruct((pairs, 2, count * tokens), jnp.float32),
        ],
        compiler_params=pltpu.CompilerParams(vmem_limit_bytes=VMEM),
        cost_estimate=pl.CostEstimate(
            flops=4 * pairs * 2 * HD * length * count * tokens,
            bytes_accessed=0,
            transcendentals=0,
        ),
        name="attend",
    )(qkv, qkv)


def feed_kernel(aliased, hidden_ref, grad_ref, up_ref, down_ref, *rest):
    act_ref, grad_up_ref, branch_ref, part_ref, branch_acc, part_acc = rest[2 * aliased :]
    step = pl.program_id(0)
    up_weights, down_weights = up_ref[...], down_ref[...]
    value = mm(hidden_ref[...], up_weights)
    grad_act = mm(grad_ref[...], down_weights)
    square = value * value
    tanh = jnp.tanh(ROOT * value * (1.0 + CUBE * square))
    half = 0.5 * (1.0 + tanh)
    act = (value * half).astype(jnp.bfloat16)
    slope = half + (0.5 * ROOT) * value * (1.0 - tanh * tanh) * (1.0 + 3.0 * CUBE * square)
    grad_up = (grad_act * slope).astype(jnp.bfloat16)
    act_ref[...] = act
    grad_up_ref[...] = grad_up
    part = mm(grad_up, up_weights, NT)
    branch = mm(act, down_weights, NT)

    @pl.when(step == 0)
    def _():
        part_acc[...] = part
        branch_acc[...] = branch

    @pl.when(step > 0)
    def _():
        part_acc[...] += part
        branch_acc[...] += branch

    @pl.when(step == pl.num_programs(0) - 1)
    def _():
        part_ref[...] = part_acc[...].astype(part_ref.dtype)
        branch_ref[...] = branch_acc[...].astype(branch_ref.dtype)


def feed(hidden, grads_all, up_down, piece, buffers, out_type):
    tokens, width = hidden.shape
    units = up_down.shape[1] // 2
    block = min(512, units)
    count = units // block
    length = grads_all.shape[0]
    rows = pl.BlockSpec((tokens, block), lambda j: (piece, j))
    whole = pl.BlockSpec((tokens, width), lambda j: (0, 0))
    aliased = buffers is not None
    return pl.pallas_call(
        partial(feed_kernel, int(aliased)),
        grid=(count,),
        in_specs=[
            whole,
            pl.BlockSpec((tokens, width), lambda j: (piece, 0)),
            pl.BlockSpec((width, block), lambda j: (0, j)),
            pl.BlockSpec((width, block), lambda j: (0, count + j)),
        ]
        + [pl.BlockSpec(memory_space=pl.ANY)] * (2 * aliased),
        out_specs=[rows, rows, whole, whole],
        out_shape=[jax.ShapeDtypeStruct((length, units), jnp.bfloat16)] * 2
        + [jax.ShapeDtypeStruct((tokens, width), out_type)] * 2,
        scratch_shapes=[pltpu.VMEM((tokens, width), jnp.float32)] * 2,
        input_output_aliases={4: 0, 5: 1} if aliased else {},
        compiler_params=pltpu.CompilerParams(vmem_limit_bytes=VMEM),
        cost_estimate=pl.CostEstimate(
            flops=8 * tokens * width * units,
            bytes_accessed=4 * width * units + 8 * tokens * width + 4 * tokens * units,
            transcendentals=tokens * units,
        ),
        name="feed",
    )(hidden, grads_all, up_down, up_down, *(buffers or ()))


def terms_kernel(hidden_ref, grads_ref, grad_up_ref, act_ref, out_ref, turned):
    step = pl.program_id(0)
    half = pl.num_programs(0) // 2

    @pl.when(step == 0)
    def _():
        turned[...] = hidden_ref[...].T

    @pl.when(step == half)
    def _():
        turned[...] = grads_ref[...].T

    @pl.when(step < half)
    def _():
        out_ref[...] = mm(turned[...], grad_up_ref[...]).astype(out_ref.dtype)

    @pl.when(step >= half)
    def _():
        out_ref[...] = mm(turned[...], act_ref[...]).astype(out_ref.dtype)


def feed_terms(hidden_all, grads_all, grad_up, act):
    length, width = hidden_all.shape
    units = act.shape[1]
    block = min(512, units)
    count = units // block
    whole = pl.BlockSpec((length, width), lambda j: (0, 0))
    return pl.pallas_call(
        terms_kernel,
        grid=(2 * count,),
        in_specs=[
            whole,
            whole,
            pl.BlockSpec((length, block), lambda j: (0, jnp.minimum(j, count - 1))),
            pl.BlockSpec((length, block), lambda j: (0, jnp.maximum(j - count, 0))),
        ],
        out_specs=pl.BlockSpec((width, block), lambda j: (0, j)),
        out_shape=jax.ShapeDtypeStruct((width, 2 * units), jnp.bfloat16),
        scratch_shapes=[pltpu.VMEM((width, length), jnp.bfloat16)],
        compiler_params=pltpu.CompilerParams(vmem_limit_bytes=VMEM),
        cost_estimate=pl.CostEstimate(
            flops=width * units * length // 4, bytes_accessed=0, transcendentals=0
        ),
        name="feed_terms",
    )(hidden_all, grads_all, grad_up, act)


def attend_back_kernel(pieces, all_ref, lse_ref, *rest):
    grad_refs, (out_ref, key_acc, value_acc) = rest[:pieces], rest[pieces:]
    tokens = grad_refs[0].shape[0]
    scaling = HD**-0.5
    chunk = min(CHUNK, tokens)
    for head in range(2):
        base = head * 3 * HD
        _, keys, values = head_parts(all_ref, head)
        for at in range(0, pieces * tokens, chunk):
            span = slice(at, at + chunk)
            inner = slice(at % tokens, at % tokens + chunk)
            queries = head_parts(all_ref, head, span)[0]
            grads = grad_refs[at // tokens][inner, head * HD : (head + 1) * HD]
            lse = lse_ref[0, head : head + 1, span]
            probs = jnp.exp2(mm(keys, queries, NT) * SCALE2 - lse)
            product = probs * mm(values, grads, NT)
            inner_sum = jnp.sum(product, 0, keepdims=True)
            score_grad = (product - probs * inner_sum).astype(jnp.bfloat16)
            value_part = mm(probs.astype(jnp.bfloat16), grads)
            key_part = mm(score_grad, queries)
            if at == 0:
                value_acc[...] = value_part
                key_acc[...] = key_part
            else:
                value_acc[...] += value_part
                key_acc[...] += key_part
            query_grad = mm(keys, score_grad, TN) * scaling
            out_ref[span, base : base + HD] = query_grad.T.astype(jnp.bfloat16)
        out_ref[:, base + HD : base + 2 * HD] = (key_acc[...] * scaling).astype(jnp.bfloat16)
        out_ref[:, base + 2 * HD : base + 3 * HD] = value_acc[...].astype(jnp.bfloat16)


def attend_back(qkv, grad_pieces, lse, first, pairs):
    length = qkv.shape[0]
    columns = pairs * 6 * HD
    tokens = grad_pieces[0].shape[0]
    return pl.pallas_call(
        partial(attend_back_kernel, len(grad_pieces)),
        grid=(pairs,),
        in_specs=[
            pl.BlockSpec((length, 6 * HD), lambda p: (0, first + p)),
            pl.BlockSpec((1, 2, length), lambda p: (first + p, 0, 0)),
        ]
        + [pl.BlockSpec((tokens, 2 * HD), lambda p: (0, first + p))] * len(grad_pieces),
        out_specs=pl.BlockSpec((length, 6 * HD), lambda p: (0, p)),
        out_shape=jax.ShapeDtypeStruct((length, columns), jnp.bfloat16),
        scratch_shapes=[
            pltpu.VMEM((length, HD), jnp.float32),
            pltpu.VMEM((length, HD), jnp.float32),
        ],
        compiler_params=pltpu.CompilerParams(vmem_limit_bytes=VMEM),
        cost_estimate=pl.CostEstimate(
            flops=10 * pairs * 2 * HD * length * length,
            bytes_accessed=0,
            transcendentals=0,
        ),
        name="attend_back",
    )(qkv, lse, *grad_pieces)


def per_device(sizes, latents, cond, cotangent, w_qkv, w_out, w_up, w_down, w_ada, b_ada):
    shards, splits = sizes["fsdp"], sizes["seq"]
    me = lax.axis_index("seq")
    tokens, width = latents.shape[1:]
    heads = H // splits
    low = jnp.bfloat16
    wide = jnp.float32

    def fetch(value, step):
        return lax.ppermute(value, "seq", [((i + step) % splits, i) for i in range(splits)])

    def send(value, step):
        return lax.ppermute(value, "seq", [(i, (i + step) % splits) for i in range(splits)])

    def everyone(value):
        return [value] + [fetch(value, step) for step in range(1, splits)]

    def in_order(pieces, axis):
        if splits == 1:
            return pieces[0]
        return jnp.concatenate(
            [
                lax.select_n(
                    (position - me) % splits == 1, *pieces
                ) if splits == 2 else
                lax.dynamic_index_in_dim(
                    jnp.stack(pieces), (position - me) % splits, 0, keepdims=False
                )
                for position in range(splits)
            ],
            axis,
        )

    def seq_sum(value):
        if splits != 2:
            return lax.psum(value, "seq").astype(wide)
        return value.astype(wide) + fetch(value, 1).astype(wide)

    spot = lax.axis_index("fsdp")
    depth = shards // 4
    core_at, x_at, z_at = spot % 2, (spot // 2) % 2, spot // 4

    def core_swap(value):
        return lax.ppermute(value, "fsdp", [(i, i ^ 1) for i in range(shards)])

    def x_swap(value):
        return lax.ppermute(value, "fsdp", [(i, i ^ 2) for i in range(shards)])

    def z_send(value, step):
        return lax.ppermute(value, "fsdp", [(i, (i + 4 * step) % shards) for i in range(shards)])

    def two(mine, other, at):
        return jnp.stack(
            [jnp.where(at == 0, mine, other), jnp.where(at == 0, other, mine)], 1
        )

    def gather_z(shard):
        return [shard] + [z_send(shard, step) for step in range(1, depth)]

    def gather_x(pieces):
        rows, cols = pieces[0].shape
        line = jnp.zeros((depth, rows, cols), pieces[0].dtype)
        for step, piece in enumerate(pieces):
            line = lax.dynamic_update_slice_in_dim(line, piece[None], (z_at - step) % depth, 0)
        return line, x_swap(line)

    def gather_core(pair):
        rows, cols = pair[0].shape[1:]
        plane = two(*pair, x_at).reshape(2 * depth, rows, cols)
        return plane, core_swap(plane)

    def gather_end(pair):
        rows, cols = pair[0].shape[1:]
        return two(*pair, core_at).reshape(shards * rows, cols)

    def halve(value, at, swap):
        mine = lax.dynamic_index_in_dim(value, at, 1, keepdims=False)
        other = lax.dynamic_index_in_dim(value, 1 - at, 1, keepdims=False)
        return mine, swap(other)

    def add(pair):
        return (pair[0].astype(wide) + pair[1].astype(wide)).astype(low)

    def scatter_core(value):
        rows, cols = value.shape[0] // shards, value.shape[1]
        return halve(value.reshape(2 * depth, 2, rows, cols), core_at, core_swap)

    def scatter_x(pair):
        rows, cols = pair[0].shape[1:]
        return halve(add(pair).reshape(depth, 2, rows, cols), x_at, x_swap)

    def scatter_z(pair):
        value = add(pair)
        pieces = [lax.dynamic_index_in_dim(value, z_at, 0, keepdims=False)]
        for step in range(1, depth):
            piece = lax.dynamic_index_in_dim(value, (z_at + step) % depth, 0, keepdims=False)
            pieces.append(z_send(piece, step))
        return pieces

    def scatter_end(pieces):
        total = pieces[0].astype(wide)
        for piece in pieces[1:]:
            total = total + piece.astype(wide)
        return total

    after = lax.optimization_barrier
    own_latents, own_cotangent = latents[0], cotangent[0]
    cond_act, silu_back = jax.vjp(jax.nn.silu, cond.astype(wide))
    cond_all = lax.all_to_all(
        jnp.broadcast_to(cond_act.astype(low), (shards, width)),
        "fsdp",
        split_axis=0,
        concat_axis=0,
        tiled=True,
    )
    mod_cols = (mm(cond_all, w_ada) + b_ada.astype(wide)).astype(low)
    peer_latents = [fetch(own_latents, step) for step in range(1, splits)]
    mod_cols, peer_latents = after((mod_cols, peer_latents))
    modulation = lax.all_to_all(
        mod_cols, "fsdp", split_axis=0, concat_axis=1, tiled=True
    ).astype(wide)
    modulation, out_shard = after((modulation, w_out))
    out_pieces = gather_z(out_shard)
    shift_one, scale_one, gate_one, shift_two, scale_two, gate_two = [
        modulation[:, position * width : (position + 1) * width] for position in range(6)
    ]
    columns = heads * 3 * HD
    qkv_shard = lax.dynamic_slice_in_dim(w_qkv, me * columns, columns, 1)
    qkv_half = lax.all_gather(qkv_shard, "fsdp", axis=0, tiled=True)
    cond_all, up_shard, down_shard = after((cond_all, w_up, w_down))
    up_down = lax.all_gather(
        jnp.concatenate([up_shard, down_shard.T], 1), "fsdp", axis=0, tiled=True
    )
    units = w_up.shape[1]

    latents_all = jnp.concatenate([own_latents] + peer_latents, 0)
    cotangents = everyone(own_cotangent)

    normed_all, inverse_all = normalize(latents_all.astype(wide))
    hidden_one = (normed_all * (1.0 + scale_one) + shift_one).astype(low)
    qkv = mm(hidden_one, qkv_half).astype(low)
    qkv, out_pieces = after((qkv, out_pieces))
    out_pair = gather_x(out_pieces)
    attn_peers, lse_peers = attend(qkv, tokens, 1, splits - 1)
    attn_peers, qkv, out_pair = after((attn_peers, qkv, out_pair))
    out_pair = gather_core(out_pair)
    blocks = [None] + [attn_peers[r * tokens : (r + 1) * tokens] for r in range(splits - 1)]
    theirs = [{} for _ in range(splits)]
    for r in range(1, splits):
        for q in range(1, splits):
            theirs[(r + q) % splits][q] = fetch(blocks[r], q)
    attn_own, lse_own = attend(qkv, tokens, 0, 1)
    blocks[0] = attn_own
    attn_own, out_pair, theirs = after((attn_own, out_pair, theirs))
    for q in range(1, splits):
        theirs[q][q] = fetch(attn_own, q)
    out_full = gather_end(out_pair)

    def to_feed(rows, heads_of, piece):
        inputs = latents_all[piece * tokens : (piece + 1) * tokens].astype(wide)
        attn_rows = in_order([rows] + [heads_of[q] for q in range(1, splits)], 1)
        branch_one = mm(attn_rows, out_full)
        middle = inputs + gate_one * branch_one
        normed, inverse = normalize(middle)
        hidden = (normed * (1.0 + scale_two) + shift_two).astype(low)
        return hidden, attn_rows, branch_one, middle, normed, inverse

    own_theirs = theirs[0]
    hidden_two, attn_rows, branch_one, middle, normed_two, inverse_two = to_feed(
        attn_own, own_theirs, 0
    )
    hidden_two, theirs, cotangents = after((hidden_two, theirs, cotangents))
    grad_rows = (gate_two * jnp.concatenate(cotangents, 0).astype(wide)).astype(low)
    hidden_pieces = [hidden_two] + [
        to_feed(blocks[r], theirs[r], r)[0] for r in range(1, splits)
    ]

    buffers, grad_parts, branch_parts = None, [], []
    for piece in range(splits):
        act, grad_up, branch_part, grad_part = feed(
            hidden_pieces[piece],
            grad_rows,
            up_down,
            piece,
            buffers,
            low if piece else wide,
        )
        buffers = (act, grad_up)
        grad_parts.append(grad_part)
        branch_parts.append(branch_part)

    def send_parts(parts):
        return [send(parts[step].astype(low), step) for step in range(1, splits)]

    def add_parts(own, received):
        for value in received:
            own = own + value.astype(wide)
        return own

    grad_sent = send_parts(grad_parts)
    hidden_all = jnp.concatenate(hidden_pieces, 0)
    terms = feed_terms(hidden_all, grad_rows, grad_up, act)
    grad_sent, terms, branch_parts = after((grad_sent, terms, branch_parts))
    grad_feed = lax.psum_scatter(terms, "fsdp", scatter_dimension=0, tiled=True).astype(wide)
    grad_hidden_two = add_parts(grad_parts[0], grad_sent)
    grad_mixed = own_cotangent.astype(wide)
    grad_shift_two = jnp.sum(grad_hidden_two, 0)
    grad_scale_two = jnp.sum(grad_hidden_two * normed_two, 0)
    grad_middle = grad_mixed + norm_grad(
        normed_two, inverse_two, grad_hidden_two * (1.0 + scale_two)
    )
    grad_gate_one = jnp.sum(grad_middle * branch_one, 0)
    grad_branch_one = (gate_one * grad_middle).astype(low)

    grad_attn = mm(grad_branch_one, out_full, NT).astype(low)
    own_width = heads * HD
    grad_pieces = [
        lax.dynamic_slice_in_dim(grad_attn, ((me + r) % splits) * own_width, own_width, 1)
        for r in range(splits)
    ]
    grad_arrived = [send(grad_pieces[r], r) for r in range(1, splits)]
    term_out = mm(attn_rows, grad_branch_one, TN).astype(low)
    out_pair = scatter_core(term_out)
    grad_arrived, branch_parts, out_pair = after((grad_arrived, branch_parts, out_pair))
    branch_sent = send_parts(branch_parts)
    out_pair = scatter_x(out_pair)
    grad_heads = [grad_pieces[0]] + grad_arrived[::-1]
    lse = jnp.concatenate([lse_own, lse_peers], 2)
    pairs = heads // 2
    groups = 2 if pairs % 2 == 0 else 1
    each = pairs // groups
    size = each * 6 * HD
    qkv_pair, hidden_grads = [], []
    for group in range(groups):
        if group:
            qkv_pair, grad_heads, lse = after((qkv_pair, grad_heads, lse))
            first_pair = scatter_x(qkv_pair)
        value = attend_back(qkv, grad_heads, lse, group * each, each)
        term_qkv = mm(hidden_one, value, TN).astype(low)
        qkv_pair = scatter_core(term_qkv)
        term_qkv, value = after((term_qkv, value))
        hidden_grads.append((value, qkv_half[:, group * size : (group + 1) * size]))
    hidden_grad_all = sum(mm(value, weight, NT) for value, weight in hidden_grads)
    grad_shift_one = jnp.sum(hidden_grad_all, 0)
    grad_scale_one = jnp.sum(hidden_grad_all * normed_all, 0)
    qkv_pair, hidden_grad_all, grad_shift_one, grad_scale_one, branch_sent = after(
        (qkv_pair, hidden_grad_all, grad_shift_one, grad_scale_one, branch_sent)
    )
    qkv_pair = scatter_x(qkv_pair)
    branch_two = add_parts(branch_parts[0], branch_sent)
    grad_gate_two = jnp.sum(grad_mixed * branch_two, 0)

    grad_mod_part = jnp.concatenate(
        [
            grad_shift_one,
            grad_scale_one,
            grad_gate_one,
            grad_shift_two,
            grad_scale_two,
            grad_gate_two,
        ]
    )[None]
    grad_mod = seq_sum(grad_mod_part).astype(low)
    hidden_parts = [hidden_grad_all[r * tokens : (r + 1) * tokens] for r in range(splits)]
    if groups == 2:
        grad_mod, hidden_parts, first_pair, out_pair = after(
            (grad_mod, hidden_parts, first_pair, out_pair)
        )
        first_pieces = scatter_z(first_pair)
    hidden_sent = send_parts(hidden_parts)
    out_pieces = scatter_z(out_pair)
    mixed = (middle + gate_two * branch_two).astype(low)
    grad_mod_cols = lax.all_to_all(grad_mod, "fsdp", split_axis=1, concat_axis=0, tiled=True)
    grad_w_ada = mm(cond_all, grad_mod_cols, TN)
    grad_b_ada = jnp.sum(grad_mod_cols.astype(wide), 0)
    cond_term = mm(grad_mod_cols, w_ada, NT).astype(low)
    cond_term, qkv_pair, mixed = after((cond_term, qkv_pair, mixed))
    qkv_pieces = scatter_z(qkv_pair)
    cond_terms = lax.all_to_all(cond_term, "fsdp", split_axis=0, concat_axis=0, tiled=True)
    grad_cond = silu_back(jnp.sum(cond_terms.astype(wide), 0, keepdims=True))[0]
    grad_hidden_one = add_parts(hidden_parts[0], hidden_sent)
    grad_latents = grad_middle + norm_grad(
        normed_all[:tokens], inverse_all[:tokens], grad_hidden_one * (1.0 + scale_one)
    )
    qkv_pieces, grad_latents, grad_cond, out_pieces = after(
        (qkv_pieces, grad_latents, grad_cond, out_pieces)
    )
    shards_qkv = [scatter_end(first_pieces).astype(low)] if groups == 2 else []
    shards_qkv.append(scatter_end(qkv_pieces).astype(low))
    grad_w_qkv = in_order(everyone(jnp.concatenate(shards_qkv, 1)), 1).astype(wide)
    grad_w_out = seq_sum(scatter_end(out_pieces).astype(low))
    grad_w_up, grad_w_down = grad_feed[:, :units], grad_feed[:, units:]
    return (
        mixed[None],
        grad_latents[None],
        grad_cond,
        grad_w_qkv,
        grad_w_out,
        grad_w_up,
        grad_w_down.T,
        grad_w_ada,
        grad_b_ada,
    )


def solution(mesh):
    return jax.shard_map(
        partial(per_device, dict(mesh.shape)),
        mesh=mesh,
        in_specs=(
            P("fsdp", "seq", None),
            P("fsdp", None),
            P("fsdp", "seq", None),
            P("fsdp", None),
            P("fsdp", None),
            P("fsdp", "seq"),
            P("seq", "fsdp"),
            P(None, "fsdp"),
            P("fsdp"),
        ),
        out_specs=(
            P("fsdp", "seq", None),
            P("fsdp", "seq", None),
            P("fsdp", None),
            P("fsdp", None),
            P("fsdp", None),
            P("fsdp", "seq"),
            P("seq", "fsdp"),
            P(None, "fsdp"),
            P("fsdp"),
        ),
        check_vma=False,
    )
```

```python
from functools import partial

import jax
import jax.numpy as jnp
from jax import lax
from jax.experimental import pallas as pl
from jax.experimental.pallas import tpu as pltpu
from jax.sharding import PartitionSpec as P

H = 16
HD = 64
EPSILON = 1e-06
LOG2E = 1.4426950408889634
SCALE2 = HD**-0.5 * LOG2E
VMEM = 56 * 1024 * 1024
CHUNK = 256
ROOT = 0.7978845608028654
CUBE = 0.044715

NT = (((1,), (1,)), ((), ()))
TN = (((0,), (0,)), ((), ()))
NN = (((1,), (0,)), ((), ()))


def mm(a, b, dims=NN):
    return lax.dot_general(a, b, dims, preferred_element_type=jnp.float32)


def normalize(value_rows):
    center = value_rows - jnp.mean(value_rows, -1, keepdims=True)
    inverse = lax.rsqrt(jnp.mean(center * center, -1, keepdims=True) + EPSILON)
    return (center * inverse, inverse)


def norm_grad(normed, inverse, grad_normed):
    return inverse * (
        grad_normed
        - jnp.mean(grad_normed, -1, keepdims=True)
        - normed * jnp.mean(grad_normed * normed, -1, keepdims=True)
    )


def head_parts(ref, head, rows=slice(None)):
    base = head * 3 * HD
    return [ref[rows, base + j * HD : base + (j + 1) * HD] for j in range(3)]


def attend_kernel(query_ref, all_ref, out_ref, lse_ref):
    rows = query_ref.shape[0]
    for head in range(2):
        _, keys, values = head_parts(all_ref, head)
        chunk = min(CHUNK, rows)
        for at in range(0, rows, chunk):
            span = slice(at, at + chunk)
            queries = head_parts(query_ref, head, span)[0]
            scores = mm(keys, queries, NT)
            highest = jnp.max(scores, 0, keepdims=True)
            raised = jnp.exp2(scores * SCALE2 - highest * SCALE2)
            totals = jnp.sum(raised, 0, keepdims=True)
            result = mm(values, raised.astype(jnp.bfloat16), TN) / totals
            out_ref[span, head * HD : (head + 1) * HD] = result.T.astype(jnp.bfloat16)
            lse_ref[0, head : head + 1, span] = highest * SCALE2 + jnp.log2(totals)


def attend(qkv, tokens, first, count):
    length, columns = qkv.shape
    pairs = columns // (6 * HD)
    return pl.pallas_call(
        attend_kernel,
        grid=(pairs, count),
        in_specs=[
            pl.BlockSpec((tokens, 6 * HD), lambda p, b: (first + b, p)),
            pl.BlockSpec((length, 6 * HD), lambda p, b: (0, p)),
        ],
        out_specs=[
            pl.BlockSpec((tokens, 2 * HD), lambda p, b: (b, p)),
            pl.BlockSpec((1, 2, tokens), lambda p, b: (p, 0, b)),
        ],
        out_shape=[
            jax.ShapeDtypeStruct((count * tokens, pairs * 2 * HD), jnp.bfloat16),
            jax.ShapeDtypeStruct((pairs, 2, count * tokens), jnp.float32),
        ],
        compiler_params=pltpu.CompilerParams(vmem_limit_bytes=VMEM),
        cost_estimate=pl.CostEstimate(
            flops=4 * pairs * 2 * HD * length * count * tokens,
            bytes_accessed=0,
            transcendentals=0,
        ),
        name="attend",
    )(qkv, qkv)


def feed_kernel(aliased, hidden_ref, grad_ref, up_ref, down_ref, *rest):
    act_ref, grad_up_ref, branch_ref, part_ref, branch_acc, part_acc = rest[2 * aliased :]
    step = pl.program_id(0)
    up_weights, down_weights = up_ref[...], down_ref[...]
    value = mm(hidden_ref[...], up_weights)
    grad_act = mm(grad_ref[...], down_weights)
    square = value * value
    tanh = jnp.tanh(ROOT * value * (1.0 + CUBE * square))
    half = 0.5 * (1.0 + tanh)
    act = (value * half).astype(jnp.bfloat16)
    slope = half + (0.5 * ROOT) * value * (1.0 - tanh * tanh) * (1.0 + 3.0 * CUBE * square)
    grad_up = (grad_act * slope).astype(jnp.bfloat16)
    act_ref[...] = act
    grad_up_ref[...] = grad_up
    part = mm(grad_up, up_weights, NT)
    branch = mm(act, down_weights, NT)

    @pl.when(step == 0)
    def _():
        part_acc[...] = part
        branch_acc[...] = branch

    @pl.when(step > 0)
    def _():
        part_acc[...] += part
        branch_acc[...] += branch

    @pl.when(step == pl.num_programs(0) - 1)
    def _():
        part_ref[...] = part_acc[...].astype(part_ref.dtype)
        branch_ref[...] = branch_acc[...].astype(branch_ref.dtype)


def feed(hidden, grads_all, up_down, piece, buffers, out_type):
    tokens, width = hidden.shape
    units = up_down.shape[1] // 2
    block = min(512, units)
    count = units // block
    length = grads_all.shape[0]
    rows = pl.BlockSpec((tokens, block), lambda j: (piece, j))
    whole = pl.BlockSpec((tokens, width), lambda j: (0, 0))
    aliased = buffers is not None
    return pl.pallas_call(
        partial(feed_kernel, int(aliased)),
        grid=(count,),
        in_specs=[
            whole,
            pl.BlockSpec((tokens, width), lambda j: (piece, 0)),
            pl.BlockSpec((width, block), lambda j: (0, j)),
            pl.BlockSpec((width, block), lambda j: (0, count + j)),
        ]
        + [pl.BlockSpec(memory_space=pl.ANY)] * (2 * aliased),
        out_specs=[rows, rows, whole, whole],
        out_shape=[jax.ShapeDtypeStruct((length, units), jnp.bfloat16)] * 2
        + [jax.ShapeDtypeStruct((tokens, width), out_type)] * 2,
        scratch_shapes=[pltpu.VMEM((tokens, width), jnp.float32)] * 2,
        input_output_aliases={4: 0, 5: 1} if aliased else {},
        compiler_params=pltpu.CompilerParams(vmem_limit_bytes=VMEM),
        cost_estimate=pl.CostEstimate(
            flops=8 * tokens * width * units,
            bytes_accessed=4 * width * units + 8 * tokens * width + 4 * tokens * units,
            transcendentals=tokens * units,
        ),
        name="feed",
    )(hidden, grads_all, up_down, up_down, *(buffers or ()))


def turn_kernel(rows, place_ref, value_ref, out_ref):
    at = pl.program_id(0)
    turned = value_ref[...].T
    each = 128 // rows
    for part in range(each):
        start = pl.multiple_of(place_ref[at * each + part] * rows, rows)
        out_ref[pl.ds(start, rows), :] = turned[part * rows : (part + 1) * rows, :]


def turn(value, place):
    length, width = value.shape
    rows = width // place.shape[0]
    return pl.pallas_call(
        partial(turn_kernel, rows),
        grid_spec=pltpu.PrefetchScalarGridSpec(
            num_scalar_prefetch=1,
            grid=(width // 128,),
            in_specs=[pl.BlockSpec((length, 128), lambda b, p: (0, b))],
            out_specs=pl.BlockSpec((width, length), lambda b, p: (0, 0)),
        ),
        out_shape=jax.ShapeDtypeStruct((width, length), value.dtype),
        compiler_params=pltpu.CompilerParams(vmem_limit_bytes=VMEM),
        cost_estimate=pl.CostEstimate(flops=0, bytes_accessed=4 * length * width, transcendentals=0),
        name="turn",
    )(place, value)


def attend_back_kernel(pieces, all_ref, lse_ref, *rest):
    grad_refs, (out_ref, key_acc, value_acc) = rest[:pieces], rest[pieces:]
    tokens = grad_refs[0].shape[0]
    scaling = HD**-0.5
    chunk = min(CHUNK, tokens)
    for head in range(2):
        base = head * 3 * HD
        _, keys, values = head_parts(all_ref, head)
        for at in range(0, pieces * tokens, chunk):
            span = slice(at, at + chunk)
            inner = slice(at % tokens, at % tokens + chunk)
            queries = head_parts(all_ref, head, span)[0]
            grads = grad_refs[at // tokens][inner, head * HD : (head + 1) * HD]
            lse = lse_ref[0, head : head + 1, span]
            probs = jnp.exp2(mm(keys, queries, NT) * SCALE2 - lse)
            product = probs * mm(values, grads, NT)
            inner_sum = jnp.sum(product, 0, keepdims=True)
            score_grad = (product - probs * inner_sum).astype(jnp.bfloat16)
            value_part = mm(probs.astype(jnp.bfloat16), grads)
            key_part = mm(score_grad, queries)
            if at == 0:
                value_acc[...] = value_part
                key_acc[...] = key_part
            else:
                value_acc[...] += value_part
                key_acc[...] += key_part
            query_grad = mm(keys, score_grad, TN) * scaling
            out_ref[span, base : base + HD] = query_grad.T.astype(jnp.bfloat16)
        out_ref[:, base + HD : base + 2 * HD] = (key_acc[...] * scaling).astype(jnp.bfloat16)
        out_ref[:, base + 2 * HD : base + 3 * HD] = value_acc[...].astype(jnp.bfloat16)


def attend_back(qkv, grad_pieces, lse, first, pairs):
    length = qkv.shape[0]
    columns = pairs * 6 * HD
    tokens = grad_pieces[0].shape[0]
    return pl.pallas_call(
        partial(attend_back_kernel, len(grad_pieces)),
        grid=(pairs,),
        in_specs=[
            pl.BlockSpec((length, 6 * HD), lambda p: (0, first + p)),
            pl.BlockSpec((1, 2, length), lambda p: (first + p, 0, 0)),
        ]
        + [pl.BlockSpec((tokens, 2 * HD), lambda p: (0, first + p))] * len(grad_pieces),
        out_specs=pl.BlockSpec((length, 6 * HD), lambda p: (0, p)),
        out_shape=jax.ShapeDtypeStruct((length, columns), jnp.bfloat16),
        scratch_shapes=[
            pltpu.VMEM((length, HD), jnp.float32),
            pltpu.VMEM((length, HD), jnp.float32),
        ],
        compiler_params=pltpu.CompilerParams(vmem_limit_bytes=VMEM),
        cost_estimate=pl.CostEstimate(
            flops=10 * pairs * 2 * HD * length * length,
            bytes_accessed=0,
            transcendentals=0,
        ),
        name="attend_back",
    )(qkv, lse, *grad_pieces)


def per_device(sizes, latents, cond, cotangent, w_qkv, w_out, w_up, w_down, w_ada, b_ada):
    shards, splits = sizes["fsdp"], sizes["seq"]
    me = lax.axis_index("seq")
    tokens, width = latents.shape[1:]
    heads = H // splits
    low = jnp.bfloat16
    wide = jnp.float32

    def fetch(value, step):
        return lax.ppermute(value, "seq", [((i + step) % splits, i) for i in range(splits)])

    def send(value, step):
        return lax.ppermute(value, "seq", [(i, (i + step) % splits) for i in range(splits)])

    def everyone(value):
        return [value] + [fetch(value, step) for step in range(1, splits)]

    def in_order(pieces, axis):
        if splits == 1:
            return pieces[0]
        return jnp.concatenate(
            [
                lax.select_n(
                    (position - me) % splits == 1, *pieces
                ) if splits == 2 else
                lax.dynamic_index_in_dim(
                    jnp.stack(pieces), (position - me) % splits, 0, keepdims=False
                )
                for position in range(splits)
            ],
            axis,
        )

    def seq_sum(value):
        if splits != 2:
            return lax.psum(value, "seq").astype(wide)
        return value.astype(wide) + fetch(value, 1).astype(wide)

    spot = lax.axis_index("fsdp")
    depth = shards // 4
    core_at, x_at, z_at = spot % 2, (spot // 2) % 2, spot // 4

    def core_swap(value):
        return lax.ppermute(value, "fsdp", [(i, i ^ 1) for i in range(shards)])

    def x_swap(value):
        return lax.ppermute(value, "fsdp", [(i, i ^ 2) for i in range(shards)])

    def z_send(value, step):
        return lax.ppermute(value, "fsdp", [(i, (i + 4 * step) % shards) for i in range(shards)])

    def two(mine, other, at):
        return jnp.stack(
            [jnp.where(at == 0, mine, other), jnp.where(at == 0, other, mine)], 1
        )

    def gather_z(shard):
        return [shard] + [z_send(shard, step) for step in range(1, depth)]

    def gather_x(pieces):
        rows, cols = pieces[0].shape
        line = jnp.zeros((depth, rows, cols), pieces[0].dtype)
        for step, piece in enumerate(pieces):
            line = lax.dynamic_update_slice_in_dim(line, piece[None], (z_at - step) % depth, 0)
        return line, x_swap(line)

    def gather_core(pair):
        rows, cols = pair[0].shape[1:]
        plane = two(*pair, x_at).reshape(2 * depth, rows, cols)
        return plane, core_swap(plane)

    def gather_end(pair):
        rows, cols = pair[0].shape[1:]
        return two(*pair, core_at).reshape(shards * rows, cols)

    blocks_at = jnp.arange(shards)
    place = (
        ((blocks_at % 2) ^ core_at) * 2 + ((blocks_at // 2) % 2 ^ x_at)
    ) * depth + (blocks_at // 4 - z_at) % depth
    place = place.astype(jnp.int32)

    def scatter_core(turned, value):
        half = turned.shape[0] // 2
        other = mm(turned[half:], value).astype(low)
        return mm(turned[:half], value).astype(low), core_swap(other)

    def x_part(pair):
        half = pair[0].shape[0] // 2
        return (pair[0][half:].astype(wide) + pair[1][half:].astype(wide)).astype(low)

    def scatter_x(pair, part):
        half = pair[0].shape[0] // 2
        return pair[0][:half], pair[1][:half], x_swap(part)

    def scatter_z(terms):
        total = sum(term.astype(wide) for term in terms)
        rows = total.shape[0] // depth
        return [total[:rows]] + [
            z_send(total[step * rows : (step + 1) * rows].astype(low), step)
            for step in range(1, depth)
        ]

    def scatter_end(pieces):
        return sum(piece.astype(wide) for piece in pieces)

    after = lax.optimization_barrier
    own_latents, own_cotangent = latents[0], cotangent[0]
    cond_act, silu_back = jax.vjp(jax.nn.silu, cond.astype(wide))
    cond_all = lax.all_to_all(
        jnp.broadcast_to(cond_act.astype(low), (shards, width)),
        "fsdp",
        split_axis=0,
        concat_axis=0,
        tiled=True,
    )
    mod_cols = (mm(cond_all, w_ada) + b_ada.astype(wide)).astype(low)
    peer_latents = [fetch(own_latents, step) for step in range(1, splits)]
    modulation = lax.all_to_all(
        mod_cols, "fsdp", split_axis=0, concat_axis=1, tiled=True
    ).astype(wide)
    modulation, peer_latents, out_shard = after((modulation, peer_latents, w_out))
    out_pieces = gather_z(out_shard)
    shift_one, scale_one, gate_one, shift_two, scale_two, gate_two = [
        modulation[:, position * width : (position + 1) * width] for position in range(6)
    ]
    columns = heads * 3 * HD
    qkv_shard = lax.dynamic_slice_in_dim(w_qkv, me * columns, columns, 1)
    qkv_half = lax.all_gather(qkv_shard, "fsdp", axis=0, tiled=True)
    cond_all, up_shard, down_shard = after((cond_all, w_up, w_down))
    up_down = lax.all_gather(
        jnp.concatenate([up_shard, down_shard.T], 1), "fsdp", axis=0, tiled=True
    )
    units = w_up.shape[1]

    latents_all = jnp.concatenate([own_latents] + peer_latents, 0)
    cotangents = everyone(own_cotangent)

    normed_all, inverse_all = normalize(latents_all.astype(wide))
    hidden_one = (normed_all * (1.0 + scale_one) + shift_one).astype(low)
    turned_one = turn(hidden_one, place)
    hidden_one, turned_one, out_pieces = after((hidden_one, turned_one, out_pieces))
    out_pair = gather_x(out_pieces)
    qkv = mm(hidden_one, qkv_half).astype(low)
    attn_peers, lse_peers = attend(qkv, tokens, 1, splits - 1)
    attn_peers, qkv, out_pair, cotangents = after((attn_peers, qkv, out_pair, cotangents))
    out_pair = gather_core(out_pair)
    blocks = [None] + [attn_peers[r * tokens : (r + 1) * tokens] for r in range(splits - 1)]
    theirs = [{} for _ in range(splits)]
    for r in range(1, splits):
        for q in range(1, splits):
            theirs[(r + q) % splits][q] = fetch(blocks[r], q)
    attn_own, lse_own = attend(qkv, tokens, 0, 1)
    blocks[0] = attn_own
    attn_own, out_pair, theirs = after((attn_own, out_pair, theirs))
    for q in range(1, splits):
        theirs[q][q] = fetch(attn_own, q)
    out_full = gather_end(out_pair)

    def to_feed(rows, heads_of, piece):
        inputs = latents_all[piece * tokens : (piece + 1) * tokens].astype(wide)
        attn_rows = in_order([rows] + [heads_of[q] for q in range(1, splits)], 1)
        branch_one = mm(attn_rows, out_full)
        middle = inputs + gate_one * branch_one
        normed, inverse = normalize(middle)
        hidden = (normed * (1.0 + scale_two) + shift_two).astype(low)
        return hidden, attn_rows, branch_one, middle, normed, inverse

    own_theirs = theirs[0]
    hidden_two, attn_rows, branch_one, middle, normed_two, inverse_two = to_feed(
        attn_own, own_theirs, 0
    )
    hidden_two, theirs = after((hidden_two, theirs))
    grad_rows = (gate_two * jnp.concatenate(cotangents, 0).astype(wide)).astype(low)
    hidden_pieces = [hidden_two] + [
        to_feed(blocks[r], theirs[r], r)[0] for r in range(1, splits)
    ]

    hidden_all = jnp.concatenate(hidden_pieces, 0)
    turned_two, turned_attn = turn(hidden_all, place), turn(attn_rows, place)
    hidden_pieces, grad_rows, turned_two, turned_attn = after(
        (hidden_pieces, grad_rows, turned_two, turned_attn)
    )
    buffers, grad_parts, branch_parts = None, [], []
    for piece in range(splits):
        act, grad_up, branch_part, grad_part = feed(
            hidden_pieces[piece],
            grad_rows,
            up_down,
            piece,
            buffers,
            low if piece else wide,
        )
        buffers = (act, grad_up)
        grad_parts.append(grad_part)
        branch_parts.append(branch_part)

    def send_parts(parts):
        return [send(parts[step].astype(low), step) for step in range(1, splits)]

    def add_parts(own, received):
        for value in received:
            own = own + value.astype(wide)
        return own

    grad_sent = send_parts(grad_parts)
    term_down = mm(grad_rows, act, TN).astype(low)
    term_down, grad_up = after((term_down, grad_up))
    grad_w_down = lax.psum_scatter(term_down, "fsdp", scatter_dimension=0, tiled=True).astype(wide)
    up_pair = scatter_core(turned_two, grad_up)
    up_part = x_part(up_pair)
    grad_sent, up_pair, up_part, branch_parts = after((grad_sent, up_pair, up_part, branch_parts))
    up_terms = scatter_x(up_pair, up_part)
    grad_hidden_two = add_parts(grad_parts[0], grad_sent)
    grad_mixed = own_cotangent.astype(wide)
    grad_shift_two = jnp.sum(grad_hidden_two, 0)
    grad_scale_two = jnp.sum(grad_hidden_two * normed_two, 0)
    grad_middle = grad_mixed + norm_grad(
        normed_two, inverse_two, grad_hidden_two * (1.0 + scale_two)
    )
    grad_gate_one = jnp.sum(grad_middle * branch_one, 0)
    grad_branch_one = (gate_one * grad_middle).astype(low)

    grad_attn = mm(grad_branch_one, out_full, NT).astype(low)
    own_width = heads * HD
    grad_pieces = [
        lax.dynamic_slice_in_dim(grad_attn, ((me + r) % splits) * own_width, own_width, 1)
        for r in range(splits)
    ]
    grad_arrived = [send(grad_pieces[r], r) for r in range(1, splits)]
    out_pair = scatter_core(turned_attn, grad_branch_one)
    out_part = x_part(out_pair)
    grad_arrived, branch_parts, out_pair, out_part = after(
        (grad_arrived, branch_parts, out_pair, out_part)
    )
    branch_sent = send_parts(branch_parts)
    out_terms = scatter_x(out_pair, out_part)
    grad_heads = [grad_pieces[0]] + grad_arrived[::-1]
    lse = jnp.concatenate([lse_own, lse_peers], 2)
    pairs = heads // 2
    groups = 2 if pairs % 2 == 0 else 1
    each = pairs // groups
    size = each * 6 * HD
    values, first_terms, first_pieces = [], [], []
    for group in range(groups):
        value = attend_back(qkv, grad_heads, lse, group * each, each)
        values.append(value)
        if group + 1 < groups:
            values, up_terms = after((values, up_terms))
            pair = scatter_core(turned_one, values[0])
            up_pieces = scatter_z(up_terms)
            part = x_part(pair)
            pair, part, grad_heads, lse = after((pair, part, grad_heads, lse))
            first_terms = scatter_x(pair, part)
    values, first_terms, out_terms, branch_sent = after(
        (values, first_terms, out_terms, branch_sent)
    )
    pair = scatter_core(turned_one, values[-1])
    if groups == 1:
        up_pieces = scatter_z(up_terms)
    out_pieces = scatter_z(out_terms)
    part = x_part(pair)
    pair, part, values, first_terms = after((pair, part, values, first_terms))
    last_terms = scatter_x(pair, part)
    hidden_grad_all = sum(
        mm(value, qkv_half[:, group * size : (group + 1) * size], NT)
        for group, value in enumerate(values)
    )
    grad_shift_one = jnp.sum(hidden_grad_all, 0)
    grad_scale_one = jnp.sum(hidden_grad_all * normed_all, 0)
    branch_two = add_parts(branch_parts[0], branch_sent)
    grad_gate_two = jnp.sum(grad_mixed * branch_two, 0)

    grad_mod_part = jnp.concatenate(
        [
            grad_shift_one,
            grad_scale_one,
            grad_gate_one,
            grad_shift_two,
            grad_scale_two,
            grad_gate_two,
        ]
    )[None]
    grad_mod = seq_sum(grad_mod_part).astype(low)
    hidden_parts = [hidden_grad_all[r * tokens : (r + 1) * tokens] for r in range(splits)]
    grad_mod, hidden_parts, first_terms = after((grad_mod, hidden_parts, first_terms))
    grad_mod_cols = lax.all_to_all(grad_mod, "fsdp", split_axis=1, concat_axis=0, tiled=True)
    hidden_sent = send_parts(hidden_parts)
    if groups > 1:
        first_pieces = scatter_z(first_terms)
    mixed = (middle + gate_two * branch_two).astype(low)
    grad_w_ada = mm(cond_all, grad_mod_cols, TN)
    grad_b_ada = jnp.sum(grad_mod_cols.astype(wide), 0)
    cond_term = mm(grad_mod_cols, w_ada, NT).astype(low)
    cond_term, last_terms, mixed, out_pieces, up_pieces = after(
        (cond_term, last_terms, mixed, out_pieces, up_pieces)
    )
    cond_terms = lax.all_to_all(cond_term, "fsdp", split_axis=0, concat_axis=0, tiled=True)
    last_pieces = scatter_z(last_terms)
    grad_w_up = scatter_end(up_pieces)
    grad_w_out = seq_sum(scatter_end(out_pieces).astype(low))
    grad_hidden_one = add_parts(hidden_parts[0], hidden_sent)
    grad_latents = grad_middle + norm_grad(
        normed_all[:tokens], inverse_all[:tokens], grad_hidden_one * (1.0 + scale_one)
    )
    grad_cond = silu_back(jnp.sum(cond_terms.astype(wide), 0, keepdims=True))[0]
    last_pieces, grad_latents, grad_cond, first_pieces, grad_w_out = after(
        (last_pieces, grad_latents, grad_cond, first_pieces, grad_w_out)
    )
    shards_qkv = [scatter_end(pieces).astype(low) for pieces in (first_pieces, last_pieces) if pieces]
    grad_w_qkv = in_order(everyone(jnp.concatenate(shards_qkv, 1)), 1).astype(wide)
    return (
        mixed[None],
        grad_latents[None],
        grad_cond,
        grad_w_qkv,
        grad_w_out,
        grad_w_up,
        grad_w_down.T,
        grad_w_ada,
        grad_b_ada,
    )


def solution(mesh):
    return jax.shard_map(
        partial(per_device, dict(mesh.shape)),
        mesh=mesh,
        in_specs=(
            P("fsdp", "seq", None),
            P("fsdp", None),
            P("fsdp", "seq", None),
            P("fsdp", None),
            P("fsdp", None),
            P("fsdp", "seq"),
            P("seq", "fsdp"),
            P(None, "fsdp"),
            P("fsdp"),
        ),
        out_specs=(
            P("fsdp", "seq", None),
            P("fsdp", "seq", None),
            P("fsdp", None),
            P("fsdp", None),
            P("fsdp", None),
            P("fsdp", "seq"),
            P("seq", "fsdp"),
            P(None, "fsdp"),
            P("fsdp"),
        ),
        check_vma=False,
    )
```

```python
from functools import partial

import jax
import jax.numpy as jnp
from jax import lax
from jax.experimental import pallas as pl
from jax.experimental.pallas import tpu as pltpu
from jax.sharding import PartitionSpec as P

H = 16
HD = 64
EPSILON = 1e-06
LOG2E = 1.4426950408889634
SCALE2 = HD**-0.5 * LOG2E
VMEM = 56 * 1024 * 1024
CHUNK = 512
ROOT = 0.7978845608028654
CUBE = 0.044715

NT = (((1,), (1,)), ((), ()))
TN = (((0,), (0,)), ((), ()))
NN = (((1,), (0,)), ((), ()))


def mm(a, b, dims=NN):
    return lax.dot_general(a, b, dims, preferred_element_type=jnp.float32)


def normalize(value_rows):
    center = value_rows - jnp.mean(value_rows, -1, keepdims=True)
    inverse = lax.rsqrt(jnp.mean(center * center, -1, keepdims=True) + EPSILON)
    return (center * inverse, inverse)


def norm_grad(normed, inverse, grad_normed):
    return inverse * (
        grad_normed
        - jnp.mean(grad_normed, -1, keepdims=True)
        - normed * jnp.mean(grad_normed * normed, -1, keepdims=True)
    )


def head_parts(ref, head, rows=slice(None)):
    base = head * 3 * HD
    return [ref[rows, base + j * HD : base + (j + 1) * HD] for j in range(3)]


def attend_kernel(query_ref, all_ref, out_ref, lse_ref):
    rows = query_ref.shape[0]
    for head in range(2):
        _, keys, values = head_parts(all_ref, head)
        chunk = min(CHUNK, rows)
        for at in range(0, rows, chunk):
            span = slice(at, at + chunk)
            queries = head_parts(query_ref, head, span)[0]
            scores = mm(keys, queries, NT)
            highest = jnp.max(scores, 0, keepdims=True)
            raised = jnp.exp2(scores * SCALE2 - highest * SCALE2)
            totals = jnp.sum(raised, 0, keepdims=True)
            result = mm(values, raised.astype(jnp.bfloat16), TN) / totals
            out_ref[span, head * HD : (head + 1) * HD] = result.T.astype(jnp.bfloat16)
            lse_ref[0, head : head + 1, span] = highest * SCALE2 + jnp.log2(totals)


def attend(qkv, tokens, first, count):
    length, columns = qkv.shape
    pairs = columns // (6 * HD)
    return pl.pallas_call(
        attend_kernel,
        grid=(pairs, count),
        in_specs=[
            pl.BlockSpec((tokens, 6 * HD), lambda p, b: (first + b, p)),
            pl.BlockSpec((length, 6 * HD), lambda p, b: (0, p)),
        ],
        out_specs=[
            pl.BlockSpec((tokens, 2 * HD), lambda p, b: (b, p)),
            pl.BlockSpec((1, 2, tokens), lambda p, b: (p, 0, b)),
        ],
        out_shape=[
            jax.ShapeDtypeStruct((count * tokens, pairs * 2 * HD), jnp.bfloat16),
            jax.ShapeDtypeStruct((pairs, 2, count * tokens), jnp.float32),
        ],
        compiler_params=pltpu.CompilerParams(vmem_limit_bytes=VMEM),
        cost_estimate=pl.CostEstimate(
            flops=4 * pairs * 2 * HD * length * count * tokens,
            bytes_accessed=0,
            transcendentals=0,
        ),
        name="attend",
    )(qkv, qkv)


def feed_kernel(aliased, hidden_ref, grad_ref, up_ref, down_ref, *rest):
    act_ref, grad_up_ref, branch_ref, part_ref, branch_acc, part_acc = rest[2 * aliased :]
    step = pl.program_id(0)
    up_weights, down_weights = up_ref[...], down_ref[...]
    value = mm(hidden_ref[...], up_weights)
    grad_act = mm(grad_ref[...], down_weights)
    square = value * value
    tanh = jnp.tanh(ROOT * value * (1.0 + CUBE * square))
    half = 0.5 * (1.0 + tanh)
    act = (value * half).astype(jnp.bfloat16)
    slope = half + (0.5 * ROOT) * value * (1.0 - tanh * tanh) * (1.0 + 3.0 * CUBE * square)
    grad_up = (grad_act * slope).astype(jnp.bfloat16)
    act_ref[...] = act
    grad_up_ref[...] = grad_up
    part = mm(grad_up, up_weights, NT)
    branch = mm(act, down_weights, NT)

    @pl.when(step == 0)
    def _():
        part_acc[...] = part
        branch_acc[...] = branch

    @pl.when(step > 0)
    def _():
        part_acc[...] += part
        branch_acc[...] += branch

    @pl.when(step == pl.num_programs(0) - 1)
    def _():
        part_ref[...] = part_acc[...].astype(part_ref.dtype)
        branch_ref[...] = branch_acc[...].astype(branch_ref.dtype)


def feed(hidden, grads_all, up_down, piece, buffers, out_type):
    tokens, width = hidden.shape
    units = up_down.shape[1] // 2
    block = min(512, units)
    count = units // block
    length = grads_all.shape[0]
    rows = pl.BlockSpec((tokens, block), lambda j: (piece, j))
    whole = pl.BlockSpec((tokens, width), lambda j: (0, 0))
    aliased = buffers is not None
    return pl.pallas_call(
        partial(feed_kernel, int(aliased)),
        grid=(count,),
        in_specs=[
            whole,
            pl.BlockSpec((tokens, width), lambda j: (piece, 0)),
            pl.BlockSpec((width, block), lambda j: (0, j)),
            pl.BlockSpec((width, block), lambda j: (0, count + j)),
        ]
        + [pl.BlockSpec(memory_space=pl.ANY)] * (2 * aliased),
        out_specs=[rows, rows, whole, whole],
        out_shape=[jax.ShapeDtypeStruct((length, units), jnp.bfloat16)] * 2
        + [jax.ShapeDtypeStruct((tokens, width), out_type)] * 2,
        scratch_shapes=[pltpu.VMEM((tokens, width), jnp.float32)] * 2,
        input_output_aliases={4: 0, 5: 1} if aliased else {},
        compiler_params=pltpu.CompilerParams(vmem_limit_bytes=VMEM),
        cost_estimate=pl.CostEstimate(
            flops=8 * tokens * width * units,
            bytes_accessed=4 * width * units + 8 * tokens * width + 4 * tokens * units,
            transcendentals=tokens * units,
        ),
        name="feed",
    )(hidden, grads_all, up_down, up_down, *(buffers or ()))


def turn_kernel(rows, place_ref, value_ref, out_ref):
    at = pl.program_id(0)
    turned = value_ref[...].T
    each = 128 // rows
    for part in range(each):
        start = pl.multiple_of(place_ref[at * each + part] * rows, rows)
        out_ref[pl.ds(start, rows), :] = turned[part * rows : (part + 1) * rows, :]


def turn(value, place):
    length, width = value.shape
    rows = width // place.shape[0]
    return pl.pallas_call(
        partial(turn_kernel, rows),
        grid_spec=pltpu.PrefetchScalarGridSpec(
            num_scalar_prefetch=1,
            grid=(width // 128,),
            in_specs=[pl.BlockSpec((length, 128), lambda b, p: (0, b))],
            out_specs=pl.BlockSpec((width, length), lambda b, p: (0, 0)),
        ),
        out_shape=jax.ShapeDtypeStruct((width, length), value.dtype),
        compiler_params=pltpu.CompilerParams(vmem_limit_bytes=VMEM),
        cost_estimate=pl.CostEstimate(flops=0, bytes_accessed=4 * length * width, transcendentals=0),
        name="turn",
    )(place, value)


def divisor(count):
    return next(size for size in (512, 384, 256, 128) if count % size == 0)


def mat_kernel(left_ref, right_ref, out_ref):
    out_ref[...] = mm(left_ref[...], right_ref[...]).astype(out_ref.dtype)


def mat_turned_kernel(left_ref, right_ref, out_ref, turned):
    @pl.when(pl.program_id(0) == 0)
    def _():
        turned[...] = left_ref[...].T

    out_ref[...] = mm(turned[...], right_ref[...]).astype(out_ref.dtype)


def mat(left, right, part=0, parts=1, turned=False):
    depth, columns = right.shape
    rows = left.shape[1] if turned else left.shape[0] // parts
    block = divisor(columns)
    return pl.pallas_call(
        mat_turned_kernel if turned else mat_kernel,
        grid=(columns // block,),
        in_specs=[
            pl.BlockSpec((depth, rows) if turned else (rows, depth), lambda j: (part, 0)),
            pl.BlockSpec((depth, block), lambda j: (0, j)),
        ],
        out_specs=pl.BlockSpec((rows, block), lambda j: (0, j)),
        out_shape=jax.ShapeDtypeStruct((rows, columns), jnp.bfloat16),
        scratch_shapes=[pltpu.VMEM((rows, depth), jnp.bfloat16)] if turned else [],
        compiler_params=pltpu.CompilerParams(vmem_limit_bytes=VMEM),
        cost_estimate=pl.CostEstimate(flops=rows * depth, bytes_accessed=0, transcendentals=0),
        name="mat",
    )(left, right)


def hidden_back_kernel(groups, *refs):
    values, (weight_ref, normed_ref, own_ref, peers_ref, sums_ref) = refs[:groups], refs[groups:]
    size = values[0].shape[1]
    tokens = own_ref.shape[0]
    total = mm(values[0][...], weight_ref[:, :size], NT)
    for group in range(1, groups):
        total += mm(values[group][...], weight_ref[:, group * size : (group + 1) * size], NT)
    own_ref[...] = total[:tokens]
    peers_ref[...] = total[tokens:].astype(peers_ref.dtype)
    sums_ref[0:1, :] = jnp.sum(total, 0, keepdims=True)
    sums_ref[1:2, :] = jnp.sum(total * normed_ref[...], 0, keepdims=True)


def hidden_back(values, weights, normed, tokens):
    length, width = normed.shape
    block = min(256, width)
    columns = lambda rows: pl.BlockSpec((rows, block), lambda j: (0, j))
    return pl.pallas_call(
        partial(hidden_back_kernel, len(values)),
        grid=(width // block,),
        in_specs=[pl.BlockSpec(value.shape, lambda j: (0, 0)) for value in values]
        + [pl.BlockSpec((block, weights.shape[1]), lambda j: (j, 0)), columns(length)],
        out_specs=[columns(tokens), columns(length - tokens), columns(2)],
        out_shape=[
            jax.ShapeDtypeStruct((tokens, width), jnp.float32),
            jax.ShapeDtypeStruct((length - tokens, width), jnp.bfloat16),
            jax.ShapeDtypeStruct((2, width), jnp.float32),
        ],
        compiler_params=pltpu.CompilerParams(vmem_limit_bytes=VMEM),
        cost_estimate=pl.CostEstimate(flops=length * width, bytes_accessed=0, transcendentals=0),
        name="hidden_back",
    )(*values, weights, normed)


def attend_back_kernel(pieces, all_ref, lse_ref, *rest):
    grad_refs, (out_ref, key_acc, value_acc) = rest[:pieces], rest[pieces:]
    tokens = grad_refs[0].shape[0]
    scaling = HD**-0.5
    chunk = min(CHUNK, tokens)
    for head in range(2):
        base = head * 3 * HD
        _, keys, values = head_parts(all_ref, head)
        for at in range(0, pieces * tokens, chunk):
            span = slice(at, at + chunk)
            inner = slice(at % tokens, at % tokens + chunk)
            queries = head_parts(all_ref, head, span)[0]
            grads = grad_refs[at // tokens][inner, head * HD : (head + 1) * HD]
            lse = lse_ref[0, head : head + 1, span]
            probs = jnp.exp2(mm(keys, queries, NT) * SCALE2 - lse)
            product = probs * mm(values, grads, NT)
            inner_sum = jnp.sum(product, 0, keepdims=True)
            score_grad = (product - probs * inner_sum).astype(jnp.bfloat16)
            value_part = mm(probs.astype(jnp.bfloat16), grads)
            key_part = mm(score_grad, queries)
            if at == 0:
                value_acc[...] = value_part
                key_acc[...] = key_part
            else:
                value_acc[...] += value_part
                key_acc[...] += key_part
            query_grad = mm(keys, score_grad, TN) * scaling
            out_ref[span, base : base + HD] = query_grad.T.astype(jnp.bfloat16)
        out_ref[:, base + HD : base + 2 * HD] = (key_acc[...] * scaling).astype(jnp.bfloat16)
        out_ref[:, base + 2 * HD : base + 3 * HD] = value_acc[...].astype(jnp.bfloat16)


def attend_back(qkv, grad_pieces, lse, first, pairs):
    length = qkv.shape[0]
    columns = pairs * 6 * HD
    tokens = grad_pieces[0].shape[0]
    return pl.pallas_call(
        partial(attend_back_kernel, len(grad_pieces)),
        grid=(pairs,),
        in_specs=[
            pl.BlockSpec((length, 6 * HD), lambda p: (0, first + p)),
            pl.BlockSpec((1, 2, length), lambda p: (first + p, 0, 0)),
        ]
        + [pl.BlockSpec((tokens, 2 * HD), lambda p: (0, first + p))] * len(grad_pieces),
        out_specs=pl.BlockSpec((length, 6 * HD), lambda p: (0, p)),
        out_shape=jax.ShapeDtypeStruct((length, columns), jnp.bfloat16),
        scratch_shapes=[
            pltpu.VMEM((length, HD), jnp.float32),
            pltpu.VMEM((length, HD), jnp.float32),
        ],
        compiler_params=pltpu.CompilerParams(vmem_limit_bytes=VMEM),
        cost_estimate=pl.CostEstimate(
            flops=10 * pairs * 2 * HD * length * length,
            bytes_accessed=0,
            transcendentals=0,
        ),
        name="attend_back",
    )(qkv, lse, *grad_pieces)


def per_device(sizes, latents, cond, cotangent, w_qkv, w_out, w_up, w_down, w_ada, b_ada):
    shards, splits = sizes["fsdp"], sizes["seq"]
    me = lax.axis_index("seq")
    tokens, width = latents.shape[1:]
    heads = H // splits
    low = jnp.bfloat16
    wide = jnp.float32

    def fetch(value, step):
        return lax.ppermute(value, "seq", [((i + step) % splits, i) for i in range(splits)])

    def send(value, step):
        return lax.ppermute(value, "seq", [(i, (i + step) % splits) for i in range(splits)])

    def everyone(value):
        return [value] + [fetch(value, step) for step in range(1, splits)]

    def in_order(pieces, axis):
        if splits == 1:
            return pieces[0]
        return jnp.concatenate(
            [
                lax.select_n(
                    (position - me) % splits == 1, *pieces
                ) if splits == 2 else
                lax.dynamic_index_in_dim(
                    jnp.stack(pieces), (position - me) % splits, 0, keepdims=False
                )
                for position in range(splits)
            ],
            axis,
        )

    def seq_sum(value):
        if splits != 2:
            return lax.psum(value, "seq").astype(wide)
        return value.astype(wide) + fetch(value, 1).astype(wide)

    spot = lax.axis_index("fsdp")
    depth = shards // 4
    core_at, x_at, z_at = spot % 2, (spot // 2) % 2, spot // 4

    def core_swap(value):
        return lax.ppermute(value, "fsdp", [(i, i ^ 1) for i in range(shards)])

    def x_swap(value):
        return lax.ppermute(value, "fsdp", [(i, i ^ 2) for i in range(shards)])

    def z_send(value, step):
        return lax.ppermute(value, "fsdp", [(i, (i + 4 * step) % shards) for i in range(shards)])

    def two(mine, other, at):
        return jnp.stack(
            [jnp.where(at == 0, mine, other), jnp.where(at == 0, other, mine)], 1
        )

    def gather_z(shard):
        return [shard] + [z_send(shard, step) for step in range(1, depth)]

    def gather_x(pieces):
        rows, cols = pieces[0].shape
        line = jnp.zeros((depth, rows, cols), pieces[0].dtype)
        for step, piece in enumerate(pieces):
            line = lax.dynamic_update_slice_in_dim(line, piece[None], (z_at - step) % depth, 0)
        return line, x_swap(line)

    def gather_core(pair):
        rows, cols = pair[0].shape[1:]
        plane = two(*pair, x_at).reshape(2 * depth, rows, cols)
        return plane, core_swap(plane)

    def gather_end(pair):
        rows, cols = pair[0].shape[1:]
        return two(*pair, core_at).reshape(shards * rows, cols)

    blocks_at = jnp.arange(shards)
    place = (
        ((blocks_at % 2) ^ core_at) * 2 + ((blocks_at // 2) % 2 ^ x_at)
    ) * depth + (blocks_at // 4 - z_at) % depth
    place = place.astype(jnp.int32)

    def scatter_core(turned, value):
        return mat(turned, value, 0, 2), core_swap(mat(turned, value, 1, 2))

    def x_part(pair):
        half = pair[0].shape[0] // 2
        return (pair[0][half:].astype(wide) + pair[1][half:].astype(wide)).astype(low)

    def scatter_x(pair, part):
        half = pair[0].shape[0] // 2
        return pair[0][:half], pair[1][:half], x_swap(part)

    def joined(*sums):
        return [jnp.concatenate([sum(part.astype(wide) for part in terms) for terms in sums], 1)]

    def scatter_z(terms):
        total = sum(term.astype(wide) for term in terms)
        rows = total.shape[0] // depth
        return [total[:rows]] + [
            z_send(total[step * rows : (step + 1) * rows].astype(low), step)
            for step in range(1, depth)
        ]

    def scatter_end(pieces):
        return sum(piece.astype(wide) for piece in pieces)

    after = lax.optimization_barrier
    own_latents, own_cotangent = latents[0], cotangent[0]
    cond_act, silu_back = jax.vjp(jax.nn.silu, cond.astype(wide))
    cond_all = lax.all_to_all(
        jnp.broadcast_to(cond_act.astype(low), (shards, width)),
        "fsdp",
        split_axis=0,
        concat_axis=0,
        tiled=True,
    )
    peer_latents = [fetch(own_latents, step) for step in range(1, splits)]
    cond_all, peer_latents = after((cond_all, peer_latents))
    mod_cols = (mm(cond_all, w_ada) + b_ada.astype(wide)).astype(low)
    modulation = lax.all_to_all(
        mod_cols, "fsdp", split_axis=0, concat_axis=1, tiled=True
    ).astype(wide)
    modulation, out_shard = after((modulation, w_out))
    out_pieces = gather_z(out_shard)
    shift_one, scale_one, gate_one, shift_two, scale_two, gate_two = [
        modulation[:, position * width : (position + 1) * width] for position in range(6)
    ]
    columns = heads * 3 * HD
    qkv_shard = lax.dynamic_slice_in_dim(w_qkv, me * columns, columns, 1)
    qkv_half = lax.all_gather(qkv_shard, "fsdp", axis=0, tiled=True)
    cond_all, up_shard, down_shard = after((cond_all, w_up, w_down))
    up_down = lax.all_gather(
        jnp.concatenate([up_shard, down_shard.T], 1), "fsdp", axis=0, tiled=True
    )
    units = w_up.shape[1]

    latents_all = jnp.concatenate([own_latents] + peer_latents, 0)
    cotangents = everyone(own_cotangent)

    normed_all, inverse_all = normalize(latents_all.astype(wide))
    hidden_one = (normed_all * (1.0 + scale_one) + shift_one).astype(low)
    turned_one = turn(hidden_one, place)
    hidden_one, turned_one, out_pieces = after((hidden_one, turned_one, out_pieces))
    out_pair = gather_x(out_pieces)
    qkv = mm(hidden_one, qkv_half).astype(low)
    attn_peers, lse_peers = attend(qkv, tokens, 1, splits - 1)
    attn_peers, qkv, out_pair, cotangents = after((attn_peers, qkv, out_pair, cotangents))
    out_pair = gather_core(out_pair)
    blocks = [None] + [attn_peers[r * tokens : (r + 1) * tokens] for r in range(splits - 1)]
    theirs = [{} for _ in range(splits)]
    for r in range(1, splits):
        for q in range(1, splits):
            theirs[(r + q) % splits][q] = fetch(blocks[r], q)
    attn_own, lse_own = attend(qkv, tokens, 0, 1)
    blocks[0] = attn_own
    attn_own, out_pair, theirs = after((attn_own, out_pair, theirs))
    for q in range(1, splits):
        theirs[q][q] = fetch(attn_own, q)
    out_full = gather_end(out_pair)

    def to_feed(rows, heads_of, piece):
        inputs = latents_all[piece * tokens : (piece + 1) * tokens].astype(wide)
        attn_rows = in_order([rows] + [heads_of[q] for q in range(1, splits)], 1)
        branch_one = mm(attn_rows, out_full)
        middle = inputs + gate_one * branch_one
        normed, inverse = normalize(middle)
        hidden = (normed * (1.0 + scale_two) + shift_two).astype(low)
        return hidden, attn_rows, branch_one, middle, normed, inverse

    own_theirs = theirs[0]
    hidden_two, attn_rows, branch_one, middle, normed_two, inverse_two = to_feed(
        attn_own, own_theirs, 0
    )
    hidden_two, theirs = after((hidden_two, theirs))
    grad_rows = (gate_two * jnp.concatenate(cotangents, 0).astype(wide)).astype(low)
    hidden_pieces = [hidden_two] + [
        to_feed(blocks[r], theirs[r], r)[0] for r in range(1, splits)
    ]

    hidden_all = jnp.concatenate(hidden_pieces, 0)
    turned_two, turned_attn = turn(hidden_all, place), turn(attn_rows, place)
    hidden_pieces, grad_rows, turned_two, turned_attn = after(
        (hidden_pieces, grad_rows, turned_two, turned_attn)
    )
    buffers, grad_parts, branch_parts = None, [], []
    for piece in range(splits):
        act, grad_up, branch_part, grad_part = feed(
            hidden_pieces[piece],
            grad_rows,
            up_down,
            piece,
            buffers,
            low if piece else wide,
        )
        buffers = (act, grad_up)
        grad_parts.append(grad_part)
        branch_parts.append(branch_part)

    def send_parts(parts):
        return [send(parts[step].astype(low), step) for step in range(1, splits)]

    def add_parts(own, received):
        for value in received:
            own = own + value.astype(wide)
        return own

    grad_sent = send_parts(grad_parts)
    term_down = mat(grad_rows, act, turned=True)
    term_down, grad_up = after((term_down, grad_up))
    grad_w_down = lax.psum_scatter(term_down, "fsdp", scatter_dimension=0, tiled=True).astype(wide)
    up_pair = scatter_core(turned_two, grad_up)
    up_part = x_part(up_pair)
    grad_sent, up_pair, up_part, branch_parts = after((grad_sent, up_pair, up_part, branch_parts))
    up_terms = scatter_x(up_pair, up_part)
    grad_hidden_two = add_parts(grad_parts[0], grad_sent)
    grad_mixed = own_cotangent.astype(wide)
    grad_shift_two = jnp.sum(grad_hidden_two, 0)
    grad_scale_two = jnp.sum(grad_hidden_two * normed_two, 0)
    grad_middle = grad_mixed + norm_grad(
        normed_two, inverse_two, grad_hidden_two * (1.0 + scale_two)
    )
    grad_gate_one = jnp.sum(grad_middle * branch_one, 0)
    grad_branch_one = (gate_one * grad_middle).astype(low)

    grad_attn = mm(grad_branch_one, out_full, NT).astype(low)
    own_width = heads * HD
    grad_pieces = [
        lax.dynamic_slice_in_dim(grad_attn, ((me + r) % splits) * own_width, own_width, 1)
        for r in range(splits)
    ]
    grad_arrived = [send(grad_pieces[r], r) for r in range(1, splits)]
    out_pair = scatter_core(turned_attn, grad_branch_one)
    out_part = x_part(out_pair)
    grad_arrived, branch_parts, out_pair, out_part = after(
        (grad_arrived, branch_parts, out_pair, out_part)
    )
    branch_sent = send_parts(branch_parts)
    out_terms = scatter_x(out_pair, out_part)
    grad_heads = [grad_pieces[0]] + grad_arrived[::-1]
    lse = jnp.concatenate([lse_own, lse_peers], 2)
    pairs = heads // 2
    groups = 2 if pairs % 2 == 0 else 1
    each = pairs // groups
    size = each * 6 * HD
    values, first_terms, first_pieces = [], [], []
    for group in range(groups):
        value = attend_back(qkv, grad_heads, lse, group * each, each)
        values.append(value)
        if group + 1 < groups:
            values, up_terms, out_terms = after((values, up_terms, out_terms))
            pair = scatter_core(turned_one, values[0])
            joint_pieces = scatter_z(joined(up_terms, out_terms))
            part = x_part(pair)
            pair, part, grad_heads, lse = after((pair, part, grad_heads, lse))
            first_terms = scatter_x(pair, part)
    values, first_terms, branch_sent, grad_w_down = after(
        (values, first_terms, branch_sent, grad_w_down)
    )
    pair = scatter_core(turned_one, values[-1])
    if groups == 1:
        joint_pieces = scatter_z(joined(up_terms, out_terms))
    else:
        first_pieces = scatter_z(first_terms)
    part = x_part(pair)
    pair, part, values = after((pair, part, values))
    last_terms = scatter_x(pair, part)
    own_grad, peers_grad, sums = hidden_back(values, qkv_half, normed_all, tokens)
    branch_two = add_parts(branch_parts[0], branch_sent)
    grad_gate_two = jnp.sum(grad_mixed * branch_two, 0)

    grad_mod_part = jnp.concatenate(
        [sums[0], sums[1], grad_gate_one, grad_shift_two, grad_scale_two, grad_gate_two]
    )[None]
    grad_mod = seq_sum(grad_mod_part).astype(low)
    hidden_parts = [own_grad] + [
        peers_grad[r * tokens : (r + 1) * tokens] for r in range(splits - 1)
    ]
    grad_mod, hidden_parts, last_terms = after((grad_mod, hidden_parts, last_terms))
    grad_mod_cols = lax.all_to_all(grad_mod, "fsdp", split_axis=1, concat_axis=0, tiled=True)
    hidden_sent = send_parts(hidden_parts)
    last_pieces = scatter_z(last_terms)
    mixed = (middle + gate_two * branch_two).astype(low)
    grad_w_ada = mm(cond_all, grad_mod_cols, TN)
    grad_b_ada = jnp.sum(grad_mod_cols.astype(wide), 0)
    cond_term = mm(grad_mod_cols, w_ada, NT).astype(low)
    cond_term, mixed, joint_pieces = after((cond_term, mixed, joint_pieces))
    cond_terms = lax.all_to_all(cond_term, "fsdp", split_axis=0, concat_axis=0, tiled=True)
    grad_joint = scatter_end(joint_pieces)
    grad_w_up = grad_joint[:, :units]
    grad_w_out = seq_sum(grad_joint[:, units:].astype(low))
    grad_hidden_one = add_parts(hidden_parts[0], hidden_sent)
    grad_latents = grad_middle + norm_grad(
        normed_all[:tokens], inverse_all[:tokens], grad_hidden_one * (1.0 + scale_one)
    )
    grad_cond = silu_back(jnp.sum(cond_terms.astype(wide), 0, keepdims=True))[0]
    shards_qkv = [scatter_end(pieces).astype(low) for pieces in (first_pieces, last_pieces) if pieces]
    grad_w_qkv = in_order(everyone(jnp.concatenate(shards_qkv, 1)), 1).astype(wide)
    return (
        mixed[None],
        grad_latents[None],
        grad_cond,
        grad_w_qkv,
        grad_w_out,
        grad_w_up,
        grad_w_down.T,
        grad_w_ada,
        grad_b_ada,
    )


def solution(mesh):
    return jax.shard_map(
        partial(per_device, dict(mesh.shape)),
        mesh=mesh,
        in_specs=(
            P("fsdp", "seq", None),
            P("fsdp", None),
            P("fsdp", "seq", None),
            P("fsdp", None),
            P("fsdp", None),
            P("fsdp", "seq"),
            P("seq", "fsdp"),
            P(None, "fsdp"),
            P("fsdp"),
        ),
        out_specs=(
            P("fsdp", "seq", None),
            P("fsdp", "seq", None),
            P("fsdp", None),
            P("fsdp", None),
            P("fsdp", None),
            P("fsdp", "seq"),
            P("seq", "fsdp"),
            P(None, "fsdp"),
            P("fsdp"),
        ),
        check_vma=False,
    )
```

```python
from functools import partial

import jax
import jax.numpy as jnp
from jax import lax
from jax.experimental import pallas as pl
from jax.experimental.pallas import tpu as pltpu
from jax.sharding import PartitionSpec as P

H = 16
HD = 64
EPSILON = 1e-06
LOG2E = 1.4426950408889634
SCALE2 = HD**-0.5 * LOG2E
MIB = 1024 * 1024
CHUNK = 512
ROOT = 0.7978845608028654
CUBE = 0.044715

NT = (((1,), (1,)), ((), ()))
TN = (((0,), (0,)), ((), ()))
NN = (((1,), (0,)), ((), ()))


def mm(a, b, dims=NN):
    return lax.dot_general(a, b, dims, preferred_element_type=jnp.float32)


def normalize(value_rows):
    center = value_rows - jnp.mean(value_rows, -1, keepdims=True)
    inverse = lax.rsqrt(jnp.mean(center * center, -1, keepdims=True) + EPSILON)
    return (center * inverse, inverse)


def norm_grad(normed, inverse, grad_normed):
    return inverse * (
        grad_normed
        - jnp.mean(grad_normed, -1, keepdims=True)
        - normed * jnp.mean(grad_normed * normed, -1, keepdims=True)
    )


def head_parts(ref, head, rows=slice(None)):
    base = head * 3 * HD
    return [ref[rows, base + j * HD : base + (j + 1) * HD] for j in range(3)]


def attend_kernel(query_ref, all_ref, out_ref, lse_ref):
    rows = query_ref.shape[0]
    for head in range(2):
        _, keys, values = head_parts(all_ref, head)
        chunk = min(CHUNK, rows)
        for at in range(0, rows, chunk):
            span = slice(at, at + chunk)
            queries = head_parts(query_ref, head, span)[0]
            scores = mm(keys, queries, NT)
            highest = jnp.max(scores, 0, keepdims=True)
            raised = jnp.exp2(scores * SCALE2 - highest * SCALE2)
            totals = jnp.sum(raised, 0, keepdims=True)
            result = mm(values, raised.astype(jnp.bfloat16), TN) / totals
            out_ref[span, head * HD : (head + 1) * HD] = result.T.astype(jnp.bfloat16)
            lse_ref[0, head : head + 1, span] = highest * SCALE2 + jnp.log2(totals)


def attend(qkv, tokens, first, count):
    length, columns = qkv.shape
    pairs = columns // (6 * HD)
    return pl.pallas_call(
        attend_kernel,
        grid=(pairs, count),
        in_specs=[
            pl.BlockSpec((tokens, 6 * HD), lambda p, b: (first + b, p)),
            pl.BlockSpec((length, 6 * HD), lambda p, b: (0, p)),
        ],
        out_specs=[
            pl.BlockSpec((tokens, 2 * HD), lambda p, b: (b, p)),
            pl.BlockSpec((1, 2, tokens), lambda p, b: (p, 0, b)),
        ],
        out_shape=[
            jax.ShapeDtypeStruct((count * tokens, pairs * 2 * HD), jnp.bfloat16),
            jax.ShapeDtypeStruct((pairs, 2, count * tokens), jnp.float32),
        ],
        compiler_params=pltpu.CompilerParams(vmem_limit_bytes=24 * MIB),
        cost_estimate=pl.CostEstimate(
            flops=4 * pairs * 2 * HD * length * count * tokens,
            bytes_accessed=0,
            transcendentals=0,
        ),
        name="attend",
    )(qkv, qkv)


def feed_kernel(aliased, hidden_ref, grad_ref, up_ref, down_ref, *rest):
    act_ref, grad_up_ref, branch_ref, part_ref, branch_acc, part_acc = rest[2 * aliased :]
    step = pl.program_id(0)
    up_weights, down_weights = up_ref[...], down_ref[...]
    value = mm(hidden_ref[...], up_weights)
    grad_act = mm(grad_ref[...], down_weights)
    square = value * value
    tanh = jnp.tanh(ROOT * value * (1.0 + CUBE * square))
    half = 0.5 * (1.0 + tanh)
    act = (value * half).astype(jnp.bfloat16)
    slope = half + (0.5 * ROOT) * value * (1.0 - tanh * tanh) * (1.0 + 3.0 * CUBE * square)
    grad_up = (grad_act * slope).astype(jnp.bfloat16)
    act_ref[...] = act
    grad_up_ref[...] = grad_up
    part = mm(grad_up, up_weights, NT)
    branch = mm(act, down_weights, NT)

    @pl.when(step == 0)
    def _():
        part_acc[...] = part
        branch_acc[...] = branch

    @pl.when(step > 0)
    def _():
        part_acc[...] += part
        branch_acc[...] += branch

    @pl.when(step == pl.num_programs(0) - 1)
    def _():
        part_ref[...] = part_acc[...].astype(part_ref.dtype)
        branch_ref[...] = branch_acc[...].astype(branch_ref.dtype)


def feed(hidden, grads_all, up_down, piece, buffers, out_type):
    tokens, width = hidden.shape
    units = up_down.shape[1] // 2
    block = min(512, units)
    count = units // block
    length = grads_all.shape[0]
    rows = pl.BlockSpec((tokens, block), lambda j: (piece, j))
    whole = pl.BlockSpec((tokens, width), lambda j: (0, 0))
    aliased = buffers is not None
    return pl.pallas_call(
        partial(feed_kernel, int(aliased)),
        grid=(count,),
        in_specs=[
            whole,
            pl.BlockSpec((tokens, width), lambda j: (piece, 0)),
            pl.BlockSpec((width, block), lambda j: (0, j)),
            pl.BlockSpec((width, block), lambda j: (0, count + j)),
        ]
        + [pl.BlockSpec(memory_space=pl.ANY)] * (2 * aliased),
        out_specs=[rows, rows, whole, whole],
        out_shape=[jax.ShapeDtypeStruct((length, units), jnp.bfloat16)] * 2
        + [jax.ShapeDtypeStruct((tokens, width), out_type)] * 2,
        scratch_shapes=[pltpu.VMEM((tokens, width), jnp.float32)] * 2,
        input_output_aliases={4: 0, 5: 1} if aliased else {},
        compiler_params=pltpu.CompilerParams(vmem_limit_bytes=40 * MIB),
        cost_estimate=pl.CostEstimate(
            flops=tokens * width * units, bytes_accessed=0, transcendentals=0
        ),
        name="feed",
    )(hidden, grads_all, up_down, up_down, *(buffers or ()))


def turn_kernel(rows, place_ref, value_ref, out_ref):
    at = pl.program_id(0)
    turned = value_ref[...].T
    each = 128 // rows
    for part in range(each):
        start = pl.multiple_of(place_ref[at * each + part] * rows, rows)
        out_ref[pl.ds(start, rows), :] = turned[part * rows : (part + 1) * rows, :]


def turn(value, place):
    length, width = value.shape
    rows = width // place.shape[0]
    return pl.pallas_call(
        partial(turn_kernel, rows),
        grid_spec=pltpu.PrefetchScalarGridSpec(
            num_scalar_prefetch=1,
            grid=(width // 128,),
            in_specs=[pl.BlockSpec((length, 128), lambda b, p: (0, b))],
            out_specs=pl.BlockSpec((width, length), lambda b, p: (0, 0)),
        ),
        out_shape=jax.ShapeDtypeStruct((width, length), value.dtype),
        compiler_params=pltpu.CompilerParams(vmem_limit_bytes=16 * MIB),
        cost_estimate=pl.CostEstimate(flops=0, bytes_accessed=4 * length * width, transcendentals=0),
        name="turn",
    )(place, value)


def hidden_back_kernel(groups, *refs):
    values, (weight_ref, normed_ref, own_ref, peers_ref, sums_ref) = refs[:groups], refs[groups:]
    size = values[0].shape[1]
    tokens = own_ref.shape[0]
    total = mm(values[0][...], weight_ref[:, :size], NT)
    for group in range(1, groups):
        total += mm(values[group][...], weight_ref[:, group * size : (group + 1) * size], NT)
    own_ref[...] = total[:tokens]
    peers_ref[...] = total[tokens:].astype(peers_ref.dtype)
    sums_ref[0:1, :] = jnp.sum(total, 0, keepdims=True)
    sums_ref[1:2, :] = jnp.sum(total * normed_ref[...], 0, keepdims=True)


def hidden_back(values, weights, normed, tokens):
    length, width = normed.shape
    block = min(256, width)
    columns = lambda rows: pl.BlockSpec((rows, block), lambda j: (0, j))
    return pl.pallas_call(
        partial(hidden_back_kernel, len(values)),
        grid=(width // block,),
        in_specs=[pl.BlockSpec(value.shape, lambda j: (0, 0)) for value in values]
        + [pl.BlockSpec((block, weights.shape[1]), lambda j: (j, 0)), columns(length)],
        out_specs=[columns(tokens), columns(length - tokens), columns(2)],
        out_shape=[
            jax.ShapeDtypeStruct((tokens, width), jnp.float32),
            jax.ShapeDtypeStruct((length - tokens, width), jnp.bfloat16),
            jax.ShapeDtypeStruct((2, width), jnp.float32),
        ],
        compiler_params=pltpu.CompilerParams(vmem_limit_bytes=24 * MIB),
        cost_estimate=pl.CostEstimate(flops=length * width, bytes_accessed=0, transcendentals=0),
        name="hidden_back",
    )(*values, weights, normed)


def attend_back_kernel(pieces, all_ref, lse_ref, *rest):
    grad_refs, (out_ref, key_acc, value_acc) = rest[:pieces], rest[pieces:]
    tokens = grad_refs[0].shape[0]
    scaling = HD**-0.5
    chunk = min(CHUNK, tokens)
    for head in range(2):
        base = head * 3 * HD
        _, keys, values = head_parts(all_ref, head)
        for at in range(0, pieces * tokens, chunk):
            span = slice(at, at + chunk)
            inner = slice(at % tokens, at % tokens + chunk)
            queries = head_parts(all_ref, head, span)[0]
            grads = grad_refs[at // tokens][inner, head * HD : (head + 1) * HD]
            lse = lse_ref[0, head : head + 1, span]
            probs = jnp.exp2(mm(keys, queries, NT) * SCALE2 - lse)
            product = probs * mm(values, grads, NT)
            inner_sum = jnp.sum(product, 0, keepdims=True)
            score_grad = (product - probs * inner_sum).astype(jnp.bfloat16)
            value_part = mm(probs.astype(jnp.bfloat16), grads)
            key_part = mm(score_grad, queries)
            if at == 0:
                value_acc[...] = value_part
                key_acc[...] = key_part
            else:
                value_acc[...] += value_part
                key_acc[...] += key_part
            query_grad = mm(keys, score_grad, TN) * scaling
            out_ref[span, base : base + HD] = query_grad.T.astype(jnp.bfloat16)
        out_ref[:, base + HD : base + 2 * HD] = (key_acc[...] * scaling).astype(jnp.bfloat16)
        out_ref[:, base + 2 * HD : base + 3 * HD] = value_acc[...].astype(jnp.bfloat16)


def attend_back(qkv, grad_pieces, lse, first, pairs):
    length = qkv.shape[0]
    columns = pairs * 6 * HD
    tokens = grad_pieces[0].shape[0]
    return pl.pallas_call(
        partial(attend_back_kernel, len(grad_pieces)),
        grid=(pairs,),
        in_specs=[
            pl.BlockSpec((length, 6 * HD), lambda p: (0, first + p)),
            pl.BlockSpec((1, 2, length), lambda p: (first + p, 0, 0)),
        ]
        + [pl.BlockSpec((tokens, 2 * HD), lambda p: (0, first + p))] * len(grad_pieces),
        out_specs=pl.BlockSpec((length, 6 * HD), lambda p: (0, p)),
        out_shape=jax.ShapeDtypeStruct((length, columns), jnp.bfloat16),
        scratch_shapes=[
            pltpu.VMEM((length, HD), jnp.float32),
            pltpu.VMEM((length, HD), jnp.float32),
        ],
        compiler_params=pltpu.CompilerParams(vmem_limit_bytes=32 * MIB),
        cost_estimate=pl.CostEstimate(
            flops=10 * pairs * 2 * HD * length * length,
            bytes_accessed=0,
            transcendentals=0,
        ),
        name="attend_back",
    )(qkv, lse, *grad_pieces)


def per_device(sizes, latents, cond, cotangent, w_qkv, w_out, w_up, w_down, w_ada, b_ada):
    shards, splits = sizes["fsdp"], sizes["seq"]
    me = lax.axis_index("seq")
    tokens, width = latents.shape[1:]
    heads = H // splits
    low = jnp.bfloat16
    wide = jnp.float32

    def fetch(value, step):
        return lax.ppermute(value, "seq", [((i + step) % splits, i) for i in range(splits)])

    def send(value, step):
        return lax.ppermute(value, "seq", [(i, (i + step) % splits) for i in range(splits)])

    def everyone(value):
        return [value] + [fetch(value, step) for step in range(1, splits)]

    def in_order(pieces, axis):
        if splits == 1:
            return pieces[0]
        return jnp.concatenate(
            [
                lax.select_n(
                    (position - me) % splits == 1, *pieces
                ) if splits == 2 else
                lax.dynamic_index_in_dim(
                    jnp.stack(pieces), (position - me) % splits, 0, keepdims=False
                )
                for position in range(splits)
            ],
            axis,
        )

    def seq_sum(value):
        if splits != 2:
            return lax.psum(value, "seq").astype(wide)
        return value.astype(wide) + fetch(value, 1).astype(wide)

    spot = lax.axis_index("fsdp")
    depth = shards // 4
    core_at, x_at, z_at = spot % 2, (spot // 2) % 2, spot // 4

    def core_swap(value):
        return lax.ppermute(value, "fsdp", [(i, i ^ 1) for i in range(shards)])

    def x_swap(value):
        return lax.ppermute(value, "fsdp", [(i, i ^ 2) for i in range(shards)])

    def z_send(value, step):
        return lax.ppermute(value, "fsdp", [(i, (i + 4 * step) % shards) for i in range(shards)])

    def two(mine, other, at):
        return jnp.stack(
            [jnp.where(at == 0, mine, other), jnp.where(at == 0, other, mine)], 1
        )

    def gather_z(shard):
        return [shard] + [z_send(shard, step) for step in range(1, depth)]

    def gather_x(pieces):
        rows, cols = pieces[0].shape
        line = jnp.zeros((depth, rows, cols), pieces[0].dtype)
        for step, piece in enumerate(pieces):
            line = lax.dynamic_update_slice_in_dim(line, piece[None], (z_at - step) % depth, 0)
        return line, x_swap(line)

    def gather_core(pair):
        rows, cols = pair[0].shape[1:]
        plane = two(*pair, x_at).reshape(2 * depth, rows, cols)
        return plane, core_swap(plane)

    def gather_end(pair):
        rows, cols = pair[0].shape[1:]
        return two(*pair, core_at).reshape(shards * rows, cols)

    blocks_at = jnp.arange(shards)
    place = (
        ((blocks_at % 2) ^ core_at) * 2 + ((blocks_at // 2) % 2 ^ x_at)
    ) * depth + (blocks_at // 4 - z_at) % depth
    place = place.astype(jnp.int32)

    def scatter_core(turned, value):
        half = turned.shape[0] // 2
        other = mm(turned[half:], value).astype(low)
        return mm(turned[:half], value).astype(low), core_swap(other)

    def x_part(pair):
        half = pair[0].shape[0] // 2
        return (pair[0][half:].astype(wide) + pair[1][half:].astype(wide)).astype(low)

    def scatter_x(pair, part):
        return *pair, x_swap(part)

    def scatter_z(*many):
        total = jnp.concatenate(
            [sum(part[: terms[2].shape[0]].astype(wide) for part in terms) for terms in many], 1
        )
        rows = total.shape[0] // depth
        return [total[:rows]] + [
            z_send(total[step * rows : (step + 1) * rows].astype(low), step)
            for step in range(1, depth)
        ]

    def tick(value):
        return core_swap(lax.slice(value, (0, 0), (16, 128)))

    def scatter_end(pieces):
        return sum(piece.astype(wide) for piece in pieces)

    after = lax.optimization_barrier
    own_latents, own_cotangent = latents[0], cotangent[0]
    cond_act, silu_back = jax.vjp(jax.nn.silu, cond.astype(wide))
    cond_all = lax.all_to_all(
        jnp.broadcast_to(cond_act.astype(low), (shards, width)),
        "fsdp",
        split_axis=0,
        concat_axis=0,
        tiled=True,
    )
    peer_latents = [fetch(own_latents, step) for step in range(1, splits)]
    cond_all, peer_latents = after((cond_all, peer_latents))
    mod_cols = (mm(cond_all, w_ada) + b_ada.astype(wide)).astype(low)
    modulation = lax.all_to_all(
        mod_cols, "fsdp", split_axis=0, concat_axis=1, tiled=True
    ).astype(wide)
    modulation, out_shard = after((modulation, w_out))
    out_pieces = gather_z(out_shard)
    shift_one, scale_one, gate_one, shift_two, scale_two, gate_two = [
        modulation[:, position * width : (position + 1) * width] for position in range(6)
    ]
    columns = heads * 3 * HD
    qkv_shard = lax.dynamic_slice_in_dim(w_qkv, me * columns, columns, 1)
    qkv_half = lax.all_gather(qkv_shard, "fsdp", axis=0, tiled=True)
    cond_all, up_shard, down_shard = after((cond_all, w_up, w_down))
    up_down = lax.all_gather(
        jnp.concatenate([up_shard, down_shard.T], 1), "fsdp", axis=0, tiled=True
    )
    units = w_up.shape[1]

    latents_all = jnp.concatenate([own_latents] + peer_latents, 0)
    cotangents = everyone(own_cotangent)

    normed_all, inverse_all = normalize(latents_all.astype(wide))
    hidden_one = (normed_all * (1.0 + scale_one) + shift_one).astype(low)
    qkv = mm(hidden_one, qkv_half).astype(low)
    qkv, out_pieces = after((qkv, out_pieces))
    out_pair = gather_x(out_pieces)
    attn_peers, lse_peers = attend(qkv, tokens, 1, splits - 1)
    attn_peers, qkv, cotangents = after((attn_peers, qkv, cotangents))
    blocks = [None] + [attn_peers[r * tokens : (r + 1) * tokens] for r in range(splits - 1)]
    theirs = [{} for _ in range(splits)]
    for r in range(1, splits):
        for q in range(1, splits):
            theirs[(r + q) % splits][q] = fetch(blocks[r], q)
    attn_own, lse_own = attend(qkv, tokens, 0, 1)
    blocks[0] = attn_own
    attn_own, out_pair, theirs = after((attn_own, out_pair, theirs))
    for q in range(1, splits):
        theirs[q][q] = fetch(attn_own, q)
    out_full = gather_end(gather_core(out_pair))

    def to_feed(rows, heads_of, piece):
        inputs = latents_all[piece * tokens : (piece + 1) * tokens].astype(wide)
        attn_rows = in_order([rows] + [heads_of[q] for q in range(1, splits)], 1)
        branch_one = mm(attn_rows, out_full)
        middle = inputs + gate_one * branch_one
        normed, inverse = normalize(middle)
        hidden = (normed * (1.0 + scale_two) + shift_two).astype(low)
        return hidden, attn_rows, branch_one, middle, normed, inverse

    own_theirs = theirs[0]
    hidden_two, attn_rows, branch_one, middle, normed_two, inverse_two = to_feed(
        attn_own, own_theirs, 0
    )
    hidden_two, theirs = after((hidden_two, theirs))
    grad_rows = (gate_two * jnp.concatenate(cotangents, 0).astype(wide)).astype(low)
    hidden_pieces = [hidden_two] + [
        to_feed(blocks[r], theirs[r], r)[0] for r in range(1, splits)
    ]

    hidden_all = jnp.concatenate(hidden_pieces, 0)
    turned_one, turned_two = turn(hidden_one, place), turn(hidden_all, place)
    turned_attn = turn(attn_rows, place)
    hidden_pieces, grad_rows, turned_one, turned_two, turned_attn = after(
        (hidden_pieces, grad_rows, turned_one, turned_two, turned_attn)
    )
    buffers, grad_parts, branch_parts = None, [None] * splits, [None] * splits
    grad_sent = []
    for piece in list(range(1, splits)) + [0]:
        act, grad_up, branch_parts[piece], grad_parts[piece] = feed(
            hidden_pieces[piece],
            grad_rows,
            up_down,
            piece,
            buffers,
            low if piece else wide,
        )
        buffers = (act, grad_up)
        if piece:
            grad_sent.append(send(grad_parts[piece], piece))
            beat, buffers = after((tick(grad_parts[piece]), buffers))

    def send_parts(parts):
        return [send(parts[step].astype(low), step) for step in range(1, splits)]

    def add_parts(own, received):
        for value in received:
            own = own + value.astype(wide)
        return own

    term_down = mm(grad_rows, act, TN).astype(low)
    term_down, grad_up = after((term_down, grad_up))
    grad_w_down = lax.psum_scatter(term_down, "fsdp", scatter_dimension=0, tiled=True)
    up_pair = scatter_core(turned_two, grad_up)
    up_part = x_part(up_pair)
    grad_sent, up_pair, up_part, branch_parts = after((grad_sent, up_pair, up_part, branch_parts))
    up_terms = scatter_x(up_pair, up_part)
    grad_hidden_two = add_parts(grad_parts[0], grad_sent)
    grad_mixed = own_cotangent.astype(wide)
    grad_shift_two = jnp.sum(grad_hidden_two, 0)
    grad_scale_two = jnp.sum(grad_hidden_two * normed_two, 0)
    grad_middle = grad_mixed + norm_grad(
        normed_two, inverse_two, grad_hidden_two * (1.0 + scale_two)
    )
    grad_gate_one = jnp.sum(grad_middle * branch_one, 0)
    grad_branch_one = (gate_one * grad_middle).astype(low)

    grad_attn = mm(grad_branch_one, out_full, NT).astype(low)
    own_width = heads * HD
    grad_pieces = [
        lax.dynamic_slice_in_dim(grad_attn, ((me + r) % splits) * own_width, own_width, 1)
        for r in range(splits)
    ]
    grad_arrived = [send(grad_pieces[r], r) for r in range(1, splits)]
    beat, turned_attn = after((tick(grad_pieces[-1]), turned_attn))
    out_pair = scatter_core(turned_attn, grad_branch_one)
    out_part = x_part(out_pair)
    grad_arrived, branch_parts, out_pair, out_part = after(
        (grad_arrived, branch_parts, out_pair, out_part)
    )
    branch_sent = send_parts(branch_parts)
    out_terms = scatter_x(out_pair, out_part)
    grad_heads = [grad_pieces[0]] + grad_arrived[::-1]
    lse = jnp.concatenate([lse_own, lse_peers], 2)
    pairs = heads // 2
    groups = 2 if pairs % 2 == 0 else 1
    each = pairs // groups
    size = each * 6 * HD
    values, first_terms = [], []
    for group in range(groups):
        value = attend_back(qkv, grad_heads, lse, group * each, each)
        values.append(value)
        if group + 1 < groups:
            values, up_terms = after((values, up_terms))
            pair = scatter_core(turned_one, values[0])
            up_pieces = scatter_z(up_terms)
            part = x_part(pair)
            pair, part, grad_heads, lse = after((pair, part, grad_heads, lse))
            first_terms = scatter_x(pair, part)
            beat, grad_heads = after((tick(part), grad_heads))
    values, first_terms, out_terms, branch_sent, grad_w_down = after(
        (values, first_terms, out_terms, branch_sent, grad_w_down)
    )
    pair = scatter_core(turned_one, values[-1])
    if groups == 1:
        up_pieces = scatter_z(up_terms)
    part = x_part(pair)
    pair, part, values, first_terms, out_terms = after(
        (pair, part, values, first_terms, out_terms)
    )
    last_terms = scatter_x(pair, part)
    beat, values = after((tick(part), values))
    joint_pieces = scatter_z(*([out_terms, first_terms] if groups > 1 else [out_terms]))
    own_grad, peers_grad, sums = hidden_back(values, qkv_half, normed_all, tokens)
    branch_two = add_parts(branch_parts[0], branch_sent)
    grad_gate_two = jnp.sum(grad_mixed * branch_two, 0)

    grad_mod_part = jnp.concatenate(
        [sums[0], sums[1], grad_gate_one, grad_shift_two, grad_scale_two, grad_gate_two]
    )[None]
    grad_mod = seq_sum(grad_mod_part).astype(low)
    hidden_parts = [own_grad] + [
        peers_grad[r * tokens : (r + 1) * tokens] for r in range(splits - 1)
    ]
    grad_mod, hidden_parts, last_terms = after((grad_mod, hidden_parts, last_terms))
    grad_mod_cols = lax.all_to_all(grad_mod, "fsdp", split_axis=1, concat_axis=0, tiled=True)
    hidden_sent = send_parts(hidden_parts)
    last_pieces = scatter_z(last_terms)
    mixed = (middle + gate_two * branch_two).astype(low)
    grad_w_ada = mm(cond_all, grad_mod_cols, TN)
    grad_b_ada = jnp.sum(grad_mod_cols.astype(wide), 0)
    cond_term = mm(grad_mod_cols, w_ada, NT).astype(low)
    cond_term, mixed, joint_pieces = after((cond_term, mixed, joint_pieces))
    cond_terms = lax.all_to_all(cond_term, "fsdp", split_axis=0, concat_axis=0, tiled=True)
    grad_w_up = scatter_end(up_pieces)
    grad_joint = scatter_end(joint_pieces).astype(low)
    grad_w_out = seq_sum(grad_joint[:, :width])
    grad_hidden_one = add_parts(hidden_parts[0], hidden_sent)
    grad_latents = grad_middle + norm_grad(
        normed_all[:tokens], inverse_all[:tokens], grad_hidden_one * (1.0 + scale_one)
    )
    grad_cond = silu_back(jnp.sum(cond_terms.astype(wide), 0, keepdims=True))[0]
    last_pieces, grad_latents, grad_cond, grad_w_out = after(
        (last_pieces, grad_latents, grad_cond, grad_w_out)
    )
    shards_qkv = [grad_joint[:, width:], scatter_end(last_pieces).astype(low)]
    grad_w_qkv = in_order(everyone(jnp.concatenate(shards_qkv, 1)), 1).astype(wide)
    return (
        mixed[None],
        grad_latents[None],
        grad_cond,
        grad_w_qkv,
        grad_w_out,
        grad_w_up,
        grad_w_down.T.astype(wide),
        grad_w_ada,
        grad_b_ada,
    )


def solution(mesh):
    return jax.shard_map(
        partial(per_device, dict(mesh.shape)),
        mesh=mesh,
        in_specs=(
            P("fsdp", "seq", None),
            P("fsdp", None),
            P("fsdp", "seq", None),
            P("fsdp", None),
            P("fsdp", None),
            P("fsdp", "seq"),
            P("seq", "fsdp"),
            P(None, "fsdp"),
            P("fsdp"),
        ),
        out_specs=(
            P("fsdp", "seq", None),
            P("fsdp", "seq", None),
            P("fsdp", None),
            P("fsdp", None),
            P("fsdp", None),
            P("fsdp", "seq"),
            P("seq", "fsdp"),
            P(None, "fsdp"),
            P("fsdp"),
        ),
        check_vma=False,
    )
```

```python
from functools import partial

import jax
import jax.numpy as jnp
from jax import lax
from jax.experimental import pallas as pl
from jax.experimental.pallas import tpu as pltpu
from jax.sharding import PartitionSpec as P

H = 16
HD = 64
EPSILON = 1e-06
LOG2E = 1.4426950408889634
SCALE2 = HD**-0.5 * LOG2E
MIB = 1024 * 1024
CHUNK = 512
ROOT = 0.7978845608028654
CUBE = 0.044715

NT = (((1,), (1,)), ((), ()))
TN = (((0,), (0,)), ((), ()))
NN = (((1,), (0,)), ((), ()))


def mm(a, b, dims=NN):
    return lax.dot_general(a, b, dims, preferred_element_type=jnp.float32)


def normalize(value_rows):
    center = value_rows - jnp.mean(value_rows, -1, keepdims=True)
    inverse = lax.rsqrt(jnp.mean(center * center, -1, keepdims=True) + EPSILON)
    return (center * inverse, inverse)


def norm_grad(normed, inverse, grad_normed):
    return inverse * (
        grad_normed
        - jnp.mean(grad_normed, -1, keepdims=True)
        - normed * jnp.mean(grad_normed * normed, -1, keepdims=True)
    )


def head_parts(ref, head, rows=slice(None)):
    base = head * 3 * HD
    return [ref[rows, base + j * HD : base + (j + 1) * HD] for j in range(3)]


def attend_kernel(query_ref, all_ref, out_ref, lse_ref):
    rows = query_ref.shape[0]
    for head in range(2):
        _, keys, values = head_parts(all_ref, head)
        chunk = min(CHUNK, rows)
        for at in range(0, rows, chunk):
            span = slice(at, at + chunk)
            queries = head_parts(query_ref, head, span)[0]
            scores = mm(keys, queries, NT)
            highest = jnp.max(scores, 0, keepdims=True)
            raised = jnp.exp2(scores * SCALE2 - highest * SCALE2)
            totals = jnp.sum(raised, 0, keepdims=True)
            result = mm(values, raised.astype(jnp.bfloat16), TN) / totals
            out_ref[span, head * HD : (head + 1) * HD] = result.T.astype(jnp.bfloat16)
            lse_ref[0, head : head + 1, span] = highest * SCALE2 + jnp.log2(totals)


def attend(qkv, tokens, first, count):
    length, columns = qkv.shape
    pairs = columns // (6 * HD)
    return pl.pallas_call(
        attend_kernel,
        grid=(pairs, count),
        in_specs=[
            pl.BlockSpec((tokens, 6 * HD), lambda p, b: (first + b, p)),
            pl.BlockSpec((length, 6 * HD), lambda p, b: (0, p)),
        ],
        out_specs=[
            pl.BlockSpec((tokens, 2 * HD), lambda p, b: (b, p)),
            pl.BlockSpec((1, 2, tokens), lambda p, b: (p, 0, b)),
        ],
        out_shape=[
            jax.ShapeDtypeStruct((count * tokens, pairs * 2 * HD), jnp.bfloat16),
            jax.ShapeDtypeStruct((pairs, 2, count * tokens), jnp.float32),
        ],
        compiler_params=pltpu.CompilerParams(vmem_limit_bytes=24 * MIB),
        cost_estimate=pl.CostEstimate(
            flops=pairs * length * count * tokens,
            bytes_accessed=0,
            transcendentals=0,
        ),
        name="attend",
    )(qkv, qkv)


def feed_kernel(aliased, hidden_ref, grad_ref, up_ref, down_ref, *rest):
    act_ref, grad_up_ref, branch_ref, part_ref, branch_acc, part_acc = rest[2 * aliased :]
    step = pl.program_id(0)
    up_weights, down_weights = up_ref[...], down_ref[...]
    value = mm(hidden_ref[...], up_weights)
    grad_act = mm(grad_ref[...], down_weights)
    square = value * value
    tanh = jnp.tanh(ROOT * value * (1.0 + CUBE * square))
    half = 0.5 * (1.0 + tanh)
    act = (value * half).astype(jnp.bfloat16)
    slope = half + (0.5 * ROOT) * value * (1.0 - tanh * tanh) * (1.0 + 3.0 * CUBE * square)
    grad_up = (grad_act * slope).astype(jnp.bfloat16)
    act_ref[...] = act
    grad_up_ref[...] = grad_up
    part = mm(grad_up, up_weights, NT)
    branch = mm(act, down_weights, NT)

    @pl.when(step == 0)
    def _():
        part_acc[...] = part
        branch_acc[...] = branch

    @pl.when(step > 0)
    def _():
        part_acc[...] += part
        branch_acc[...] += branch

    @pl.when(step == pl.num_programs(0) - 1)
    def _():
        part_ref[...] = part_acc[...].astype(part_ref.dtype)
        branch_ref[...] = branch_acc[...].astype(branch_ref.dtype)


def feed(hidden, grads_all, up_down, piece, buffers, out_type):
    tokens, width = hidden.shape
    units = up_down.shape[1] // 2
    block = min(512, units)
    count = units // block
    length = grads_all.shape[0]
    rows = pl.BlockSpec((tokens, block), lambda j: (piece, j))
    whole = pl.BlockSpec((tokens, width), lambda j: (0, 0))
    aliased = buffers is not None
    return pl.pallas_call(
        partial(feed_kernel, int(aliased)),
        grid=(count,),
        in_specs=[
            whole,
            pl.BlockSpec((tokens, width), lambda j: (piece, 0)),
            pl.BlockSpec((width, block), lambda j: (0, j)),
            pl.BlockSpec((width, block), lambda j: (0, count + j)),
        ]
        + [pl.BlockSpec(memory_space=pl.ANY)] * (2 * aliased),
        out_specs=[rows, rows, whole, whole],
        out_shape=[jax.ShapeDtypeStruct((length, units), jnp.bfloat16)] * 2
        + [jax.ShapeDtypeStruct((tokens, width), out_type)] * 2,
        scratch_shapes=[pltpu.VMEM((tokens, width), jnp.float32)] * 2,
        input_output_aliases={4: 0, 5: 1} if aliased else {},
        compiler_params=pltpu.CompilerParams(vmem_limit_bytes=40 * MIB),
        cost_estimate=pl.CostEstimate(
            flops=tokens * units, bytes_accessed=0, transcendentals=0
        ),
        name="feed",
    )(hidden, grads_all, up_down, up_down, *(buffers or ()))


def turn_kernel(rows, place_ref, value_ref, out_ref):
    at = pl.program_id(0)
    turned = value_ref[...].T
    each = 128 // rows
    for part in range(each):
        start = pl.multiple_of(place_ref[at * each + part] * rows, rows)
        out_ref[pl.ds(start, rows), :] = turned[part * rows : (part + 1) * rows, :]


def turn(value, place):
    length, width = value.shape
    rows = width // place.shape[0]
    return pl.pallas_call(
        partial(turn_kernel, rows),
        grid_spec=pltpu.PrefetchScalarGridSpec(
            num_scalar_prefetch=1,
            grid=(width // 128,),
            in_specs=[pl.BlockSpec((length, 128), lambda b, p: (0, b))],
            out_specs=pl.BlockSpec((width, length), lambda b, p: (0, 0)),
        ),
        out_shape=jax.ShapeDtypeStruct((width, length), value.dtype),
        compiler_params=pltpu.CompilerParams(vmem_limit_bytes=16 * MIB),
        cost_estimate=pl.CostEstimate(flops=0, bytes_accessed=4 * length * width, transcendentals=0),
        name="turn",
    )(place, value)


def hidden_back_kernel(groups, *refs):
    values, (weight_ref, normed_ref, own_ref, peers_ref, sums_ref) = refs[:groups], refs[groups:]
    size = values[0].shape[1]
    tokens = own_ref.shape[0]
    total = mm(values[0][...], weight_ref[:, :size], NT)
    for group in range(1, groups):
        total += mm(values[group][...], weight_ref[:, group * size : (group + 1) * size], NT)
    own_ref[...] = total[:tokens]
    peers_ref[...] = total[tokens:].astype(peers_ref.dtype)
    sums_ref[0:1, :] = jnp.sum(total, 0, keepdims=True)
    sums_ref[1:2, :] = jnp.sum(total * normed_ref[...], 0, keepdims=True)


def hidden_back(values, weights, normed, tokens):
    length, width = normed.shape
    block = min(256, width)
    columns = lambda rows: pl.BlockSpec((rows, block), lambda j: (0, j))
    return pl.pallas_call(
        partial(hidden_back_kernel, len(values)),
        grid=(width // block,),
        in_specs=[pl.BlockSpec(value.shape, lambda j: (0, 0)) for value in values]
        + [pl.BlockSpec((block, weights.shape[1]), lambda j: (j, 0)), columns(length)],
        out_specs=[columns(tokens), columns(length - tokens), columns(2)],
        out_shape=[
            jax.ShapeDtypeStruct((tokens, width), jnp.float32),
            jax.ShapeDtypeStruct((length - tokens, width), jnp.bfloat16),
            jax.ShapeDtypeStruct((2, width), jnp.float32),
        ],
        compiler_params=pltpu.CompilerParams(vmem_limit_bytes=24 * MIB),
        cost_estimate=pl.CostEstimate(
            flops=length * width, bytes_accessed=0, transcendentals=0
        ),
        name="hidden_back",
    )(*values, weights, normed)


def attend_back_kernel(pieces, all_ref, lse_ref, *rest):
    grad_refs, (out_ref, key_acc, value_acc) = rest[:pieces], rest[pieces:]
    tokens = grad_refs[0].shape[0]
    scaling = HD**-0.5
    chunk = min(CHUNK, tokens)
    for head in range(2):
        base = head * 3 * HD
        _, keys, values = head_parts(all_ref, head)
        for at in range(0, pieces * tokens, chunk):
            span = slice(at, at + chunk)
            inner = slice(at % tokens, at % tokens + chunk)
            queries = head_parts(all_ref, head, span)[0]
            grads = grad_refs[at // tokens][inner, head * HD : (head + 1) * HD]
            lse = lse_ref[0, head : head + 1, span]
            probs = jnp.exp2(mm(keys, queries, NT) * SCALE2 - lse)
            product = probs * mm(values, grads, NT)
            inner_sum = jnp.sum(product, 0, keepdims=True)
            score_grad = (product - probs * inner_sum).astype(jnp.bfloat16)
            value_part = mm(probs.astype(jnp.bfloat16), grads)
            key_part = mm(score_grad, queries)
            if at == 0:
                value_acc[...] = value_part
                key_acc[...] = key_part
            else:
                value_acc[...] += value_part
                key_acc[...] += key_part
            query_grad = mm(keys, score_grad, TN) * scaling
            out_ref[span, base : base + HD] = query_grad.T.astype(jnp.bfloat16)
        out_ref[:, base + HD : base + 2 * HD] = (key_acc[...] * scaling).astype(jnp.bfloat16)
        out_ref[:, base + 2 * HD : base + 3 * HD] = value_acc[...].astype(jnp.bfloat16)


def attend_back(qkv, grad_pieces, lse, first, pairs):
    length = qkv.shape[0]
    columns = pairs * 6 * HD
    tokens = grad_pieces[0].shape[0]
    return pl.pallas_call(
        partial(attend_back_kernel, len(grad_pieces)),
        grid=(pairs,),
        in_specs=[
            pl.BlockSpec((length, 6 * HD), lambda p: (0, first + p)),
            pl.BlockSpec((1, 2, length), lambda p: (first + p, 0, 0)),
        ]
        + [pl.BlockSpec((tokens, 2 * HD), lambda p: (0, first + p))] * len(grad_pieces),
        out_specs=pl.BlockSpec((length, 6 * HD), lambda p: (0, p)),
        out_shape=jax.ShapeDtypeStruct((length, columns), jnp.bfloat16),
        scratch_shapes=[
            pltpu.VMEM((length, HD), jnp.float32),
            pltpu.VMEM((length, HD), jnp.float32),
        ],
        compiler_params=pltpu.CompilerParams(vmem_limit_bytes=32 * MIB),
        cost_estimate=pl.CostEstimate(
            flops=pairs * length * length,
            bytes_accessed=0,
            transcendentals=0,
        ),
        name="attend_back",
    )(qkv, lse, *grad_pieces)


def per_device(sizes, latents, cond, cotangent, w_qkv, w_out, w_up, w_down, w_ada, b_ada):
    shards, splits = sizes["fsdp"], sizes["seq"]
    me = lax.axis_index("seq")
    tokens, width = latents.shape[1:]
    heads = H // splits
    low = jnp.bfloat16
    wide = jnp.float32

    def fetch(value, step):
        return lax.ppermute(value, "seq", [((i + step) % splits, i) for i in range(splits)])

    def send(value, step):
        return lax.ppermute(value, "seq", [(i, (i + step) % splits) for i in range(splits)])

    def everyone(value):
        return [value] + [fetch(value, step) for step in range(1, splits)]

    def in_order(pieces, axis):
        if splits == 1:
            return pieces[0]
        return jnp.concatenate(
            [
                lax.select_n(
                    (position - me) % splits == 1, *pieces
                ) if splits == 2 else
                lax.dynamic_index_in_dim(
                    jnp.stack(pieces), (position - me) % splits, 0, keepdims=False
                )
                for position in range(splits)
            ],
            axis,
        )

    def seq_sum(value):
        if splits != 2:
            return lax.psum(value, "seq").astype(wide)
        return value.astype(wide) + fetch(value, 1).astype(wide)

    spot = lax.axis_index("fsdp")
    depth = shards // 4
    core_at, x_at, z_at = spot % 2, (spot // 2) % 2, spot // 4

    def core_swap(value):
        return lax.ppermute(value, "fsdp", [(i, i ^ 1) for i in range(shards)])

    def x_swap(value):
        return lax.ppermute(value, "fsdp", [(i, i ^ 2) for i in range(shards)])

    def z_send(value, step):
        return lax.ppermute(value, "fsdp", [(i, (i + 4 * step) % shards) for i in range(shards)])

    def two(mine, other, at):
        return jnp.stack(
            [jnp.where(at == 0, mine, other), jnp.where(at == 0, other, mine)], 1
        )

    def gather_z(shard):
        return [shard] + [z_send(shard, step) for step in range(1, depth)]

    def gather_x(pieces):
        rows, cols = pieces[0].shape
        line = jnp.zeros((depth, rows, cols), pieces[0].dtype)
        for step, piece in enumerate(pieces):
            line = lax.dynamic_update_slice_in_dim(line, piece[None], (z_at - step) % depth, 0)
        return line, x_swap(line)

    def gather_core(pair):
        rows, cols = pair[0].shape[1:]
        plane = two(*pair, x_at).reshape(2 * depth, rows, cols)
        return plane, core_swap(plane)

    def gather_end(pair):
        rows, cols = pair[0].shape[1:]
        return two(*pair, core_at).reshape(shards * rows, cols)

    blocks_at = jnp.arange(shards)
    place = (
        ((blocks_at % 2) ^ core_at) * 2 + ((blocks_at // 2) % 2 ^ x_at)
    ) * depth + (blocks_at // 4 - z_at) % depth
    place = place.astype(jnp.int32)

    def scatter_core(turned, value):
        half = turned.shape[0] // 2
        other = mm(turned[half:], value).astype(low)
        return mm(turned[:half], value).astype(low), core_swap(other)

    def x_part(pair):
        half = pair[0].shape[0] // 2
        return (pair[0][half:].astype(wide) + pair[1][half:].astype(wide)).astype(low)

    def scatter_x(pair, part):
        return *pair, x_swap(part)

    def scatter_z(*many):
        total = jnp.concatenate(
            [sum(part[: terms[2].shape[0]].astype(wide) for part in terms) for terms in many], 1
        )
        rows = total.shape[0] // depth
        return [total[:rows]] + [
            z_send(total[step * rows : (step + 1) * rows].astype(low), step)
            for step in range(1, depth)
        ]

    def scatter_end(pieces):
        return sum(piece.astype(wide) for piece in pieces)

    after = lax.optimization_barrier
    own_latents, own_cotangent = latents[0], cotangent[0]
    cond_act, silu_back = jax.vjp(jax.nn.silu, cond.astype(wide))
    cond_all = lax.all_to_all(
        jnp.broadcast_to(cond_act.astype(low), (shards, width)),
        "fsdp",
        split_axis=0,
        concat_axis=0,
        tiled=True,
    )
    peer_latents = [fetch(own_latents, step) for step in range(1, splits)]
    cond_all, peer_latents = after((cond_all, peer_latents))
    mod_cols = (mm(cond_all, w_ada) + b_ada.astype(wide)).astype(low)
    modulation = lax.all_to_all(
        mod_cols, "fsdp", split_axis=0, concat_axis=1, tiled=True
    ).astype(wide)
    modulation, out_shard = after((modulation, w_out))
    out_pieces = gather_z(out_shard)
    shift_one, scale_one, gate_one, shift_two, scale_two, gate_two = [
        modulation[:, position * width : (position + 1) * width] for position in range(6)
    ]
    columns = heads * 3 * HD
    qkv_shard = lax.dynamic_slice_in_dim(w_qkv, me * columns, columns, 1)
    qkv_half = lax.all_gather(qkv_shard, "fsdp", axis=0, tiled=True)
    cond_all, up_shard, down_shard = after((cond_all, w_up, w_down))
    up_down = lax.all_gather(
        jnp.concatenate([up_shard, down_shard.T], 1), "fsdp", axis=0, tiled=True
    )
    units = w_up.shape[1]

    latents_all = jnp.concatenate([own_latents] + peer_latents, 0)
    cotangents = everyone(own_cotangent)

    normed_all, inverse_all = normalize(latents_all.astype(wide))
    hidden_one = (normed_all * (1.0 + scale_one) + shift_one).astype(low)
    qkv = mm(hidden_one, qkv_half).astype(low)
    qkv, out_pieces = after((qkv, out_pieces))
    out_pair = gather_x(out_pieces)
    attn_peers, lse_peers = attend(qkv, tokens, 1, splits - 1)
    attn_peers, qkv, cotangents = after((attn_peers, qkv, cotangents))
    blocks = [None] + [attn_peers[r * tokens : (r + 1) * tokens] for r in range(splits - 1)]
    theirs = [{} for _ in range(splits)]
    for r in range(1, splits):
        for q in range(1, splits):
            theirs[(r + q) % splits][q] = fetch(blocks[r], q)
    attn_own, lse_own = attend(qkv, tokens, 0, 1)
    blocks[0] = attn_own
    attn_own, out_pair, theirs = after((attn_own, out_pair, theirs))
    for q in range(1, splits):
        theirs[q][q] = fetch(attn_own, q)
    out_full = gather_end(gather_core(out_pair))

    def to_feed(rows, heads_of, piece):
        inputs = latents_all[piece * tokens : (piece + 1) * tokens].astype(wide)
        attn_rows = in_order([rows] + [heads_of[q] for q in range(1, splits)], 1)
        branch_one = mm(attn_rows, out_full)
        middle = inputs + gate_one * branch_one
        normed, inverse = normalize(middle)
        hidden = (normed * (1.0 + scale_two) + shift_two).astype(low)
        return hidden, attn_rows, branch_one, middle, normed, inverse

    own_theirs = theirs[0]
    hidden_two, attn_rows, branch_one, middle, normed_two, inverse_two = to_feed(
        attn_own, own_theirs, 0
    )
    hidden_two, theirs = after((hidden_two, theirs))
    grad_rows = (gate_two * jnp.concatenate(cotangents, 0).astype(wide)).astype(low)
    hidden_pieces = [hidden_two] + [
        to_feed(blocks[r], theirs[r], r)[0] for r in range(1, splits)
    ]

    hidden_all = jnp.concatenate(hidden_pieces, 0)
    turned_one, turned_two = turn(hidden_one, place), turn(hidden_all, place)
    turned_attn = turn(attn_rows, place)
    hidden_pieces, grad_rows, turned_one, turned_two, turned_attn = after(
        (hidden_pieces, grad_rows, turned_one, turned_two, turned_attn)
    )
    buffers, grad_parts, branch_parts = None, [None] * splits, [None] * splits
    grad_sent = []
    for piece in list(range(1, splits)) + [0]:
        act, grad_up, branch_parts[piece], grad_parts[piece] = feed(
            hidden_pieces[piece],
            grad_rows,
            up_down,
            piece,
            buffers,
            low if piece else wide,
        )
        buffers = (act, grad_up)
        if piece:
            grad_sent.append(send(grad_parts[piece], piece))

    def send_parts(parts):
        return [send(parts[step].astype(low), step) for step in range(1, splits)]

    def add_parts(own, received):
        for value in received:
            own = own + value.astype(wide)
        return own

    grad_sent, act, grad_up, branch_parts = after((grad_sent, act, grad_up, branch_parts))
    grad_hidden_two = add_parts(grad_parts[0], grad_sent)
    grad_mixed = own_cotangent.astype(wide)
    grad_shift_two = jnp.sum(grad_hidden_two, 0)
    grad_scale_two = jnp.sum(grad_hidden_two * normed_two, 0)
    grad_middle = grad_mixed + norm_grad(
        normed_two, inverse_two, grad_hidden_two * (1.0 + scale_two)
    )
    grad_gate_one = jnp.sum(grad_middle * branch_one, 0)
    grad_branch_one = (gate_one * grad_middle).astype(low)

    grad_attn = mm(grad_branch_one, out_full, NT).astype(low)
    own_width = heads * HD
    grad_pieces = [
        lax.dynamic_slice_in_dim(grad_attn, ((me + r) % splits) * own_width, own_width, 1)
        for r in range(splits)
    ]
    grad_arrived = [send(grad_pieces[r], r) for r in range(1, splits)]
    term_down = mm(grad_rows, act, TN).astype(low)
    grad_arrived, branch_parts, term_down, act, grad_up = after(
        (grad_arrived, branch_parts, term_down, act, grad_up)
    )
    grad_w_down = lax.psum_scatter(term_down, "fsdp", scatter_dimension=0, tiled=True)
    up_pair = scatter_core(turned_two, grad_up)
    out_pair = scatter_core(turned_attn, grad_branch_one)
    up_part, out_part = x_part(up_pair), x_part(out_pair)
    up_pair, out_pair, up_part, out_part, grad_arrived = after(
        (up_pair, out_pair, up_part, out_part, grad_arrived)
    )
    up_terms = scatter_x(up_pair, up_part)
    branch_sent = send_parts(branch_parts)
    out_terms = scatter_x(out_pair, out_part)
    grad_heads = [grad_pieces[0]] + grad_arrived[::-1]
    lse = jnp.concatenate([lse_own, lse_peers], 2)
    pairs = heads // 2
    groups = 2 if pairs % 2 == 0 else 1
    each = pairs // groups
    size = each * 6 * HD
    values, first_terms = [], []
    for group in range(groups):
        value = attend_back(qkv, grad_heads, lse, group * each, each)
        values.append(value)
        if group + 1 < groups:
            values, up_terms = after((values, up_terms))
            pair = scatter_core(turned_one, values[0])
            up_pieces = scatter_z(up_terms)
            part = x_part(pair)
            pair, part, grad_heads, lse = after((pair, part, grad_heads, lse))
            first_terms = scatter_x(pair, part)
    if groups == 1:
        up_pieces = scatter_z(up_terms)
    values, first_terms, out_terms, up_pieces, branch_sent, grad_w_down = after(
        (values, first_terms, out_terms, up_pieces, branch_sent, grad_w_down)
    )
    pair = scatter_core(turned_one, values[-1])
    part = x_part(pair)
    pair, part, values = after((pair, part, values))
    last_terms = scatter_x(pair, part)
    own_grad, peers_grad, sums = hidden_back(values, qkv_half, normed_all, tokens)
    own_grad, peers_grad, sums, first_terms, out_terms = after(
        (own_grad, peers_grad, sums, first_terms, out_terms)
    )
    joint_pieces = scatter_z(*([out_terms, first_terms] if groups > 1 else [out_terms]))
    branch_two = add_parts(branch_parts[0], branch_sent)
    grad_gate_two = jnp.sum(grad_mixed * branch_two, 0)

    grad_mod_part = jnp.concatenate(
        [sums[0], sums[1], grad_gate_one, grad_shift_two, grad_scale_two, grad_gate_two]
    )[None]
    grad_mod = seq_sum(grad_mod_part).astype(low)
    hidden_parts = [own_grad] + [
        peers_grad[r * tokens : (r + 1) * tokens] for r in range(splits - 1)
    ]
    grad_mod, hidden_parts = after((grad_mod, hidden_parts))
    grad_mod_cols = lax.all_to_all(grad_mod, "fsdp", split_axis=1, concat_axis=0, tiled=True)
    hidden_sent = send_parts(hidden_parts)
    grad_mod_cols, last_terms, up_pieces, grad_w_down = after(
        (grad_mod_cols, last_terms, up_pieces, grad_w_down)
    )
    last_pieces = scatter_z(last_terms)
    grad_w_ada = mm(cond_all, grad_mod_cols, TN)
    grad_b_ada = jnp.sum(grad_mod_cols.astype(wide), 0)
    cond_term = mm(grad_mod_cols, w_ada, NT).astype(low)
    cond_term, middle, joint_pieces = after((cond_term, middle, joint_pieces))
    mixed = (middle + gate_two * branch_two).astype(low)
    cond_terms = lax.all_to_all(cond_term, "fsdp", split_axis=0, concat_axis=0, tiled=True)
    grad_w_up = scatter_end(up_pieces)
    grad_joint = scatter_end(joint_pieces).astype(low)
    grad_w_out = seq_sum(grad_joint[:, :width])
    grad_hidden_one = add_parts(hidden_parts[0], hidden_sent)
    grad_latents = grad_middle + norm_grad(
        normed_all[:tokens], inverse_all[:tokens], grad_hidden_one * (1.0 + scale_one)
    )
    grad_cond = silu_back(jnp.sum(cond_terms.astype(wide), 0, keepdims=True))[0]
    last_pieces, grad_latents, grad_cond, grad_w_out = after(
        (last_pieces, grad_latents, grad_cond, grad_w_out)
    )
    shards_qkv = [grad_joint[:, width:], scatter_end(last_pieces).astype(low)]
    grad_w_qkv = in_order(everyone(jnp.concatenate(shards_qkv, 1)), 1).astype(wide)
    return (
        mixed[None],
        grad_latents[None],
        grad_cond,
        grad_w_qkv,
        grad_w_out,
        grad_w_up,
        grad_w_down.T.astype(wide),
        grad_w_ada,
        grad_b_ada,
    )


def solution(mesh):
    return jax.shard_map(
        partial(per_device, dict(mesh.shape)),
        mesh=mesh,
        in_specs=(
            P("fsdp", "seq", None),
            P("fsdp", None),
            P("fsdp", "seq", None),
            P("fsdp", None),
            P("fsdp", None),
            P("fsdp", "seq"),
            P("seq", "fsdp"),
            P(None, "fsdp"),
            P("fsdp"),
        ),
        out_specs=(
            P("fsdp", "seq", None),
            P("fsdp", "seq", None),
            P("fsdp", None),
            P("fsdp", None),
            P("fsdp", None),
            P("fsdp", "seq"),
            P("seq", "fsdp"),
            P(None, "fsdp"),
            P("fsdp"),
        ),
        check_vma=False,
    )
```

```python
from functools import partial

import jax
import jax.numpy as jnp
from jax import lax
from jax.experimental import pallas as pl
from jax.experimental.pallas import tpu as pltpu
from jax.sharding import PartitionSpec as P

H = 16
HD = 64
EPSILON = 1e-06
LOG2E = 1.4426950408889634
SCALE2 = HD**-0.5 * LOG2E
MIB = 1024 * 1024
CHUNK = 512
ROOT = 0.7978845608028654
CUBE = 0.044715

NT = (((1,), (1,)), ((), ()))
TN = (((0,), (0,)), ((), ()))
NN = (((1,), (0,)), ((), ()))


def mm(a, b, dims=NN):
    return lax.dot_general(a, b, dims, preferred_element_type=jnp.float32)


def normalize(value_rows):
    center = value_rows - jnp.mean(value_rows, -1, keepdims=True)
    inverse = lax.rsqrt(jnp.mean(center * center, -1, keepdims=True) + EPSILON)
    return (center * inverse, inverse)


def norm_grad(normed, inverse, grad_normed):
    return inverse * (
        grad_normed
        - jnp.mean(grad_normed, -1, keepdims=True)
        - normed * jnp.mean(grad_normed * normed, -1, keepdims=True)
    )


def head_parts(ref, head, rows=slice(None)):
    base = head * 3 * HD
    return [ref[rows, base + j * HD : base + (j + 1) * HD] for j in range(3)]


def attend_kernel(query_ref, all_ref, out_ref, lse_ref):
    rows = query_ref.shape[0]
    for head in range(2):
        _, keys, values = head_parts(all_ref, head)
        chunk = min(CHUNK, rows)
        for at in range(0, rows, chunk):
            span = slice(at, at + chunk)
            queries = head_parts(query_ref, head, span)[0]
            scores = mm(keys, queries, NT)
            highest = jnp.max(scores, 0, keepdims=True)
            raised = jnp.exp2(scores * SCALE2 - highest * SCALE2)
            totals = jnp.sum(raised, 0, keepdims=True)
            result = mm(values, raised.astype(jnp.bfloat16), TN) / totals
            out_ref[span, head * HD : (head + 1) * HD] = result.T.astype(jnp.bfloat16)
            lse_ref[0, head : head + 1, span] = highest * SCALE2 + jnp.log2(totals)


def attend(qkv, tokens, first, count):
    length, columns = qkv.shape
    pairs = columns // (6 * HD)
    return pl.pallas_call(
        attend_kernel,
        grid=(pairs, count),
        in_specs=[
            pl.BlockSpec((tokens, 6 * HD), lambda p, b: (first + b, p)),
            pl.BlockSpec((length, 6 * HD), lambda p, b: (0, p)),
        ],
        out_specs=[
            pl.BlockSpec((tokens, 2 * HD), lambda p, b: (b, p)),
            pl.BlockSpec((1, 2, tokens), lambda p, b: (p, 0, b)),
        ],
        out_shape=[
            jax.ShapeDtypeStruct((count * tokens, pairs * 2 * HD), jnp.bfloat16),
            jax.ShapeDtypeStruct((pairs, 2, count * tokens), jnp.float32),
        ],
        compiler_params=pltpu.CompilerParams(vmem_limit_bytes=24 * MIB),
        cost_estimate=pl.CostEstimate(
            flops=pairs * length * count * tokens,
            bytes_accessed=0,
            transcendentals=0,
        ),
        name="attend",
    )(qkv, qkv)


def feed_kernel(aliased, hidden_ref, grad_ref, up_ref, down_ref, *rest):
    act_ref, grad_up_ref, branch_ref, part_ref, branch_acc, part_acc = rest[2 * aliased :]
    step = pl.program_id(0)
    up_weights, down_weights = up_ref[...], down_ref[...]
    value = mm(hidden_ref[...], up_weights)
    grad_act = mm(grad_ref[...], down_weights)
    square = value * value
    tanh = jnp.tanh(ROOT * value * (1.0 + CUBE * square))
    half = 0.5 * (1.0 + tanh)
    act = (value * half).astype(jnp.bfloat16)
    slope = half + (0.5 * ROOT) * value * (1.0 - tanh * tanh) * (1.0 + 3.0 * CUBE * square)
    grad_up = (grad_act * slope).astype(jnp.bfloat16)
    act_ref[...] = act
    grad_up_ref[...] = grad_up
    part = mm(grad_up, up_weights, NT)
    branch = mm(act, down_weights, NT)

    @pl.when(step == 0)
    def _():
        part_acc[...] = part
        branch_acc[...] = branch

    @pl.when(step > 0)
    def _():
        part_acc[...] += part
        branch_acc[...] += branch

    @pl.when(step == pl.num_programs(0) - 1)
    def _():
        part_ref[...] = part_acc[...].astype(part_ref.dtype)
        branch_ref[...] = branch_acc[...].astype(branch_ref.dtype)


def feed(hidden, grads_all, up_down, piece, buffers, out_type):
    tokens, width = hidden.shape
    units = up_down.shape[1] // 2
    block = min(512, units)
    count = units // block
    length = grads_all.shape[0]
    rows = pl.BlockSpec((tokens, block), lambda j: (piece, j))
    whole = pl.BlockSpec((tokens, width), lambda j: (0, 0))
    aliased = buffers is not None
    return pl.pallas_call(
        partial(feed_kernel, int(aliased)),
        grid=(count,),
        in_specs=[
            whole,
            pl.BlockSpec((tokens, width), lambda j: (piece, 0)),
            pl.BlockSpec((width, block), lambda j: (0, j)),
            pl.BlockSpec((width, block), lambda j: (0, count + j)),
        ]
        + [pl.BlockSpec(memory_space=pl.ANY)] * (2 * aliased),
        out_specs=[rows, rows, whole, whole],
        out_shape=[jax.ShapeDtypeStruct((length, units), jnp.bfloat16)] * 2
        + [jax.ShapeDtypeStruct((tokens, width), out_type)] * 2,
        scratch_shapes=[pltpu.VMEM((tokens, width), jnp.float32)] * 2,
        input_output_aliases={4: 0, 5: 1} if aliased else {},
        compiler_params=pltpu.CompilerParams(vmem_limit_bytes=40 * MIB),
        cost_estimate=pl.CostEstimate(
            flops=tokens * units, bytes_accessed=0, transcendentals=0
        ),
        name="feed",
    )(hidden, grads_all, up_down, up_down, *(buffers or ()))


def turn_kernel(rows, place_ref, value_ref, out_ref):
    at = pl.program_id(0)
    turned = value_ref[...].T
    each = 128 // rows
    for part in range(each):
        start = pl.multiple_of(place_ref[at * each + part] * rows, rows)
        out_ref[pl.ds(start, rows), :] = turned[part * rows : (part + 1) * rows, :]


def turn(value, place):
    length, width = value.shape
    rows = width // place.shape[0]
    return pl.pallas_call(
        partial(turn_kernel, rows),
        grid_spec=pltpu.PrefetchScalarGridSpec(
            num_scalar_prefetch=1,
            grid=(width // 128,),
            in_specs=[pl.BlockSpec((length, 128), lambda b, p: (0, b))],
            out_specs=pl.BlockSpec((width, length), lambda b, p: (0, 0)),
        ),
        out_shape=jax.ShapeDtypeStruct((width, length), value.dtype),
        compiler_params=pltpu.CompilerParams(vmem_limit_bytes=16 * MIB),
        cost_estimate=pl.CostEstimate(flops=0, bytes_accessed=4 * length * width, transcendentals=0),
        name="turn",
    )(place, value)


def divisor(count):
    return next(size for size in (512, 384, 256, 128) if count % size == 0)


def mat_kernel(left_ref, right_ref, out_ref):
    out_ref[...] = mm(left_ref[...], right_ref[...]).astype(out_ref.dtype)


def mat_turned_kernel(left_ref, right_ref, out_ref, turned):
    @pl.when(pl.program_id(0) == 0)
    def _():
        turned[...] = left_ref[...].T

    out_ref[...] = mm(turned[...], right_ref[...]).astype(out_ref.dtype)


def mat(left, right, part=0, parts=1, turned=False):
    depth, columns = right.shape
    rows = left.shape[1] if turned else left.shape[0] // parts
    block = divisor(columns)
    return pl.pallas_call(
        mat_turned_kernel if turned else mat_kernel,
        grid=(columns // block,),
        in_specs=[
            pl.BlockSpec((depth, rows) if turned else (rows, depth), lambda j: (part, 0)),
            pl.BlockSpec((depth, block), lambda j: (0, j)),
        ],
        out_specs=pl.BlockSpec((rows, block), lambda j: (0, j)),
        out_shape=jax.ShapeDtypeStruct((rows, columns), jnp.bfloat16),
        scratch_shapes=[pltpu.VMEM((rows, depth), jnp.bfloat16)] if turned else [],
        compiler_params=pltpu.CompilerParams(vmem_limit_bytes=18 * MIB),
        cost_estimate=pl.CostEstimate(flops=rows * depth, bytes_accessed=0, transcendentals=0),
        name="mat",
    )(left, right)


def hidden_back_kernel(groups, *refs):
    values, (weight_ref, normed_ref, own_ref, peers_ref, sums_ref) = refs[:groups], refs[groups:]
    size = values[0].shape[1]
    tokens = own_ref.shape[0]
    total = mm(values[0][...], weight_ref[:, :size], NT)
    for group in range(1, groups):
        total += mm(values[group][...], weight_ref[:, group * size : (group + 1) * size], NT)
    own_ref[...] = total[:tokens]
    peers_ref[...] = total[tokens:].astype(peers_ref.dtype)
    sums_ref[0:1, :] = jnp.sum(total, 0, keepdims=True)
    sums_ref[1:2, :] = jnp.sum(total * normed_ref[...], 0, keepdims=True)


def hidden_back(values, weights, normed, tokens):
    length, width = normed.shape
    block = min(256, width)
    columns = lambda rows: pl.BlockSpec((rows, block), lambda j: (0, j))
    return pl.pallas_call(
        partial(hidden_back_kernel, len(values)),
        grid=(width // block,),
        in_specs=[pl.BlockSpec(value.shape, lambda j: (0, 0)) for value in values]
        + [pl.BlockSpec((block, weights.shape[1]), lambda j: (j, 0)), columns(length)],
        out_specs=[columns(tokens), columns(length - tokens), columns(2)],
        out_shape=[
            jax.ShapeDtypeStruct((tokens, width), jnp.float32),
            jax.ShapeDtypeStruct((length - tokens, width), jnp.bfloat16),
            jax.ShapeDtypeStruct((2, width), jnp.float32),
        ],
        compiler_params=pltpu.CompilerParams(vmem_limit_bytes=24 * MIB),
        cost_estimate=pl.CostEstimate(
            flops=length * width, bytes_accessed=0, transcendentals=0
        ),
        name="hidden_back",
    )(*values, weights, normed)


def attend_back_kernel(pieces, all_ref, lse_ref, *rest):
    grad_refs, (out_ref, key_acc, value_acc) = rest[:pieces], rest[pieces:]
    tokens = grad_refs[0].shape[0]
    scaling = HD**-0.5
    chunk = min(CHUNK, tokens)
    for head in range(2):
        base = head * 3 * HD
        _, keys, values = head_parts(all_ref, head)
        for at in range(0, pieces * tokens, chunk):
            span = slice(at, at + chunk)
            inner = slice(at % tokens, at % tokens + chunk)
            queries = head_parts(all_ref, head, span)[0]
            grads = grad_refs[at // tokens][inner, head * HD : (head + 1) * HD]
            lse = lse_ref[0, head : head + 1, span]
            probs = jnp.exp2(mm(keys, queries, NT) * SCALE2 - lse)
            product = probs * mm(values, grads, NT)
            inner_sum = jnp.sum(product, 0, keepdims=True)
            score_grad = (product - probs * inner_sum).astype(jnp.bfloat16)
            value_part = mm(probs.astype(jnp.bfloat16), grads)
            key_part = mm(score_grad, queries)
            if at == 0:
                value_acc[...] = value_part
                key_acc[...] = key_part
            else:
                value_acc[...] += value_part
                key_acc[...] += key_part
            query_grad = mm(keys, score_grad, TN) * scaling
            out_ref[span, base : base + HD] = query_grad.T.astype(jnp.bfloat16)
        out_ref[:, base + HD : base + 2 * HD] = (key_acc[...] * scaling).astype(jnp.bfloat16)
        out_ref[:, base + 2 * HD : base + 3 * HD] = value_acc[...].astype(jnp.bfloat16)


def attend_back(qkv, grad_pieces, lse, first, pairs):
    length = qkv.shape[0]
    columns = pairs * 6 * HD
    tokens = grad_pieces[0].shape[0]
    return pl.pallas_call(
        partial(attend_back_kernel, len(grad_pieces)),
        grid=(pairs,),
        in_specs=[
            pl.BlockSpec((length, 6 * HD), lambda p: (0, first + p)),
            pl.BlockSpec((1, 2, length), lambda p: (first + p, 0, 0)),
        ]
        + [pl.BlockSpec((tokens, 2 * HD), lambda p: (0, first + p))] * len(grad_pieces),
        out_specs=pl.BlockSpec((length, 6 * HD), lambda p: (0, p)),
        out_shape=jax.ShapeDtypeStruct((length, columns), jnp.bfloat16),
        scratch_shapes=[
            pltpu.VMEM((length, HD), jnp.float32),
            pltpu.VMEM((length, HD), jnp.float32),
        ],
        compiler_params=pltpu.CompilerParams(vmem_limit_bytes=32 * MIB),
        cost_estimate=pl.CostEstimate(
            flops=pairs * length * length,
            bytes_accessed=0,
            transcendentals=0,
        ),
        name="attend_back",
    )(qkv, lse, *grad_pieces)


def per_device(sizes, latents, cond, cotangent, w_qkv, w_out, w_up, w_down, w_ada, b_ada):
    shards, splits = sizes["fsdp"], sizes["seq"]
    me = lax.axis_index("seq")
    tokens, width = latents.shape[1:]
    heads = H // splits
    low = jnp.bfloat16
    wide = jnp.float32

    def fetch(value, step):
        return lax.ppermute(value, "seq", [((i + step) % splits, i) for i in range(splits)])

    def send(value, step):
        return lax.ppermute(value, "seq", [(i, (i + step) % splits) for i in range(splits)])

    def everyone(value):
        return [value] + [fetch(value, step) for step in range(1, splits)]

    def in_order(pieces, axis):
        if splits == 1:
            return pieces[0]
        return jnp.concatenate(
            [
                lax.select_n(
                    (position - me) % splits == 1, *pieces
                ) if splits == 2 else
                lax.dynamic_index_in_dim(
                    jnp.stack(pieces), (position - me) % splits, 0, keepdims=False
                )
                for position in range(splits)
            ],
            axis,
        )

    def seq_sum(value):
        if splits != 2:
            return lax.psum(value, "seq").astype(wide)
        return value.astype(wide) + fetch(value, 1).astype(wide)

    spot = lax.axis_index("fsdp")
    depth = shards // 4
    core_at, x_at, z_at = spot % 2, (spot // 2) % 2, spot // 4

    def core_swap(value):
        return lax.ppermute(value, "fsdp", [(i, i ^ 1) for i in range(shards)])

    def x_swap(value):
        return lax.ppermute(value, "fsdp", [(i, i ^ 2) for i in range(shards)])

    def z_send(value, step):
        return lax.ppermute(value, "fsdp", [(i, (i + 4 * step) % shards) for i in range(shards)])

    def two(mine, other, at):
        return jnp.stack(
            [jnp.where(at == 0, mine, other), jnp.where(at == 0, other, mine)], 1
        )

    def gather_z(shard):
        return [shard] + [z_send(shard, step) for step in range(1, depth)]

    def gather_x(pieces):
        rows, cols = pieces[0].shape
        line = jnp.zeros((depth, rows, cols), pieces[0].dtype)
        for step, piece in enumerate(pieces):
            line = lax.dynamic_update_slice_in_dim(line, piece[None], (z_at - step) % depth, 0)
        return line, x_swap(line)

    def gather_core(pair):
        rows, cols = pair[0].shape[1:]
        plane = two(*pair, x_at).reshape(2 * depth, rows, cols)
        return plane, core_swap(plane)

    def gather_end(pair):
        rows, cols = pair[0].shape[1:]
        return two(*pair, core_at).reshape(shards * rows, cols)

    blocks_at = jnp.arange(shards)
    place = (
        ((blocks_at % 2) ^ core_at) * 2 + ((blocks_at // 2) % 2 ^ x_at)
    ) * depth + (blocks_at // 4 - z_at) % depth
    place = place.astype(jnp.int32)

    def scatter_core(turned, value):
        return mat(turned, value, 0, 2), core_swap(mat(turned, value, 1, 2))

    def x_part(pair):
        half = pair[0].shape[0] // 2
        return (pair[0][half:].astype(wide) + pair[1][half:].astype(wide)).astype(low)

    def scatter_x(pair, part):
        return *pair, x_swap(part)

    def scatter_z(*many):
        total = jnp.concatenate(
            [sum(part[: terms[2].shape[0]].astype(wide) for part in terms) for terms in many], 1
        )
        rows = total.shape[0] // depth
        return [total[:rows]] + [
            z_send(total[step * rows : (step + 1) * rows].astype(low), step)
            for step in range(1, depth)
        ]

    def scatter_end(pieces):
        return sum(piece.astype(wide) for piece in pieces)

    after = lax.optimization_barrier
    own_latents, own_cotangent = latents[0], cotangent[0]
    cond_act, silu_back = jax.vjp(jax.nn.silu, cond.astype(wide))
    cond_all = lax.all_to_all(
        jnp.broadcast_to(cond_act.astype(low), (shards, width)),
        "fsdp",
        split_axis=0,
        concat_axis=0,
        tiled=True,
    )
    peer_latents = [fetch(own_latents, step) for step in range(1, splits)]
    cond_all, peer_latents = after((cond_all, peer_latents))
    mod_cols = (mm(cond_all, w_ada) + b_ada.astype(wide)).astype(low)
    modulation = lax.all_to_all(
        mod_cols, "fsdp", split_axis=0, concat_axis=1, tiled=True
    ).astype(wide)
    modulation, out_shard = after((modulation, w_out))
    out_pieces = gather_z(out_shard)
    shift_one, scale_one, gate_one, shift_two, scale_two, gate_two = [
        modulation[:, position * width : (position + 1) * width] for position in range(6)
    ]
    columns = heads * 3 * HD
    qkv_shard = lax.dynamic_slice_in_dim(w_qkv, me * columns, columns, 1)
    qkv_half = lax.all_gather(qkv_shard, "fsdp", axis=0, tiled=True)
    cond_all, up_shard, down_shard = after((cond_all, w_up, w_down))
    up_down = lax.all_gather(
        jnp.concatenate([up_shard, down_shard.T], 1), "fsdp", axis=0, tiled=True
    )
    units = w_up.shape[1]

    latents_all = jnp.concatenate([own_latents] + peer_latents, 0)
    cotangents = everyone(own_cotangent)

    normed_all, inverse_all = normalize(latents_all.astype(wide))
    hidden_one = (normed_all * (1.0 + scale_one) + shift_one).astype(low)
    qkv = mm(hidden_one, qkv_half).astype(low)
    qkv, out_pieces = after((qkv, out_pieces))
    out_pair = gather_x(out_pieces)
    attn_peers, lse_peers = attend(qkv, tokens, 1, splits - 1)
    attn_peers, qkv, cotangents = after((attn_peers, qkv, cotangents))
    blocks = [None] + [attn_peers[r * tokens : (r + 1) * tokens] for r in range(splits - 1)]
    theirs = [{} for _ in range(splits)]
    for r in range(1, splits):
        for q in range(1, splits):
            theirs[(r + q) % splits][q] = fetch(blocks[r], q)
    attn_own, lse_own = attend(qkv, tokens, 0, 1)
    blocks[0] = attn_own
    attn_own, out_pair, theirs = after((attn_own, out_pair, theirs))
    for q in range(1, splits):
        theirs[q][q] = fetch(attn_own, q)
    out_full = gather_end(gather_core(out_pair))

    def to_feed(rows, heads_of, piece):
        inputs = latents_all[piece * tokens : (piece + 1) * tokens].astype(wide)
        attn_rows = in_order([rows] + [heads_of[q] for q in range(1, splits)], 1)
        branch_one = mm(attn_rows, out_full)
        middle = inputs + gate_one * branch_one
        normed, inverse = normalize(middle)
        hidden = (normed * (1.0 + scale_two) + shift_two).astype(low)
        return hidden, attn_rows, branch_one, middle, normed, inverse

    own_theirs = theirs[0]
    hidden_two, attn_rows, branch_one, middle, normed_two, inverse_two = to_feed(
        attn_own, own_theirs, 0
    )
    hidden_two, theirs = after((hidden_two, theirs))
    grad_rows = (gate_two * jnp.concatenate(cotangents, 0).astype(wide)).astype(low)
    hidden_pieces = [hidden_two] + [
        to_feed(blocks[r], theirs[r], r)[0] for r in range(1, splits)
    ]

    hidden_all = jnp.concatenate(hidden_pieces, 0)
    turned_one, turned_two = turn(hidden_one, place), turn(hidden_all, place)
    turned_attn = turn(attn_rows, place)
    hidden_pieces, grad_rows, turned_one, turned_two, turned_attn = after(
        (hidden_pieces, grad_rows, turned_one, turned_two, turned_attn)
    )
    buffers, grad_parts, branch_parts = None, [None] * splits, [None] * splits
    grad_sent = []
    for piece in list(range(1, splits)) + [0]:
        act, grad_up, branch_parts[piece], grad_parts[piece] = feed(
            hidden_pieces[piece],
            grad_rows,
            up_down,
            piece,
            buffers,
            low if piece else wide,
        )
        buffers = (act, grad_up)
        if piece:
            grad_sent.append(send(grad_parts[piece], piece))

    def send_parts(parts):
        return [send(parts[step].astype(low), step) for step in range(1, splits)]

    def add_parts(own, received):
        for value in received:
            own = own + value.astype(wide)
        return own

    term_down = mat(grad_rows, act, turned=True)
    grad_sent, term_down, act, grad_up, branch_parts = after(
        (grad_sent, term_down, act, grad_up, branch_parts)
    )
    grad_w_down = lax.psum_scatter(term_down, "fsdp", scatter_dimension=0, tiled=True)
    grad_hidden_two = add_parts(grad_parts[0], grad_sent)
    grad_mixed = own_cotangent.astype(wide)
    grad_shift_two = jnp.sum(grad_hidden_two, 0)
    grad_scale_two = jnp.sum(grad_hidden_two * normed_two, 0)
    grad_middle = grad_mixed + norm_grad(
        normed_two, inverse_two, grad_hidden_two * (1.0 + scale_two)
    )
    grad_gate_one = jnp.sum(grad_middle * branch_one, 0)
    grad_branch_one = (gate_one * grad_middle).astype(low)

    grad_attn = mm(grad_branch_one, out_full, NT).astype(low)
    own_width = heads * HD
    grad_pieces = [
        lax.dynamic_slice_in_dim(grad_attn, ((me + r) % splits) * own_width, own_width, 1)
        for r in range(splits)
    ]
    grad_arrived = [send(grad_pieces[r], r) for r in range(1, splits)]
    up_pair = scatter_core(turned_two, grad_up)
    out_pair = scatter_core(turned_attn, grad_branch_one)
    up_part, out_part = x_part(up_pair), x_part(out_pair)
    up_pair, out_pair, up_part, out_part, grad_arrived, branch_parts = after(
        (up_pair, out_pair, up_part, out_part, grad_arrived, branch_parts)
    )
    up_terms = scatter_x(up_pair, up_part)
    branch_sent = send_parts(branch_parts)
    out_terms = scatter_x(out_pair, out_part)
    grad_heads = [grad_pieces[0]] + grad_arrived[::-1]
    lse = jnp.concatenate([lse_own, lse_peers], 2)
    pairs = heads // 2
    groups = 2 if pairs % 2 == 0 else 1
    each = pairs // groups
    size = each * 6 * HD
    values, first_terms = [], []
    for group in range(groups):
        value = attend_back(qkv, grad_heads, lse, group * each, each)
        values.append(value)
        if group + 1 < groups:
            pair = scatter_core(turned_one, values[0])
            part = x_part(pair)
            pair, part, grad_heads, lse, up_terms = after(
                (pair, part, grad_heads, lse, up_terms)
            )
            first_terms = scatter_x(pair, part)
    up_pieces = scatter_z(up_terms)
    values, first_terms, out_terms, branch_sent = after(
        (values, first_terms, out_terms, branch_sent)
    )
    pair = scatter_core(turned_one, values[-1])
    part = x_part(pair)
    pair, part, values = after((pair, part, values))
    last_terms = scatter_x(pair, part)
    own_grad, peers_grad, sums = hidden_back(values, qkv_half, normed_all, tokens)
    own_grad, peers_grad, sums, last_terms = after((own_grad, peers_grad, sums, last_terms))
    branch_two = add_parts(branch_parts[0], branch_sent)
    grad_gate_two = jnp.sum(grad_mixed * branch_two, 0)

    grad_mod_part = jnp.concatenate(
        [sums[0], sums[1], grad_gate_one, grad_shift_two, grad_scale_two, grad_gate_two]
    )[None]
    grad_mod = seq_sum(grad_mod_part).astype(low)
    hidden_parts = [own_grad] + [
        peers_grad[r * tokens : (r + 1) * tokens] for r in range(splits - 1)
    ]
    grad_mod, hidden_parts = after((grad_mod, hidden_parts))
    grad_mod_cols = lax.all_to_all(grad_mod, "fsdp", split_axis=1, concat_axis=0, tiled=True)
    hidden_sent = send_parts(hidden_parts)
    last_pieces = scatter_z(last_terms)
    grad_mod_cols, first_terms, out_terms = after((grad_mod_cols, first_terms, out_terms))
    joint_pieces = scatter_z(*([out_terms, first_terms] if groups > 1 else [out_terms]))
    grad_w_ada = mm(cond_all, grad_mod_cols, TN)
    grad_b_ada = jnp.sum(grad_mod_cols.astype(wide), 0)
    cond_term = mm(grad_mod_cols, w_ada, NT).astype(low)
    cond_term, middle, grad_w_down, last_pieces, hidden_sent, up_pieces = after(
        (cond_term, middle, grad_w_down, last_pieces, hidden_sent, up_pieces)
    )
    mixed = (middle + gate_two * branch_two).astype(low)
    cond_terms = lax.all_to_all(cond_term, "fsdp", split_axis=0, concat_axis=0, tiled=True)
    cond_terms, joint_pieces = after((cond_terms, joint_pieces))
    grad_w_up = scatter_end(up_pieces)
    grad_joint = scatter_end(joint_pieces).astype(low)
    grad_w_out = seq_sum(grad_joint[:, :width])
    grad_hidden_one = add_parts(hidden_parts[0], hidden_sent)
    grad_latents = grad_middle + norm_grad(
        normed_all[:tokens], inverse_all[:tokens], grad_hidden_one * (1.0 + scale_one)
    )
    grad_cond = silu_back(jnp.sum(cond_terms.astype(wide), 0, keepdims=True))[0]
    last_pieces, grad_latents, grad_cond, grad_w_out = after(
        (last_pieces, grad_latents, grad_cond, grad_w_out)
    )
    shards_qkv = [grad_joint[:, width:], scatter_end(last_pieces).astype(low)]
    grad_w_qkv = in_order(everyone(jnp.concatenate(shards_qkv, 1)), 1).astype(wide)
    return (
        mixed[None],
        grad_latents[None],
        grad_cond,
        grad_w_qkv,
        grad_w_out,
        grad_w_up,
        grad_w_down.T.astype(wide),
        grad_w_ada,
        grad_b_ada,
    )


def solution(mesh):
    return jax.shard_map(
        partial(per_device, dict(mesh.shape)),
        mesh=mesh,
        in_specs=(
            P("fsdp", "seq", None),
            P("fsdp", None),
            P("fsdp", "seq", None),
            P("fsdp", None),
            P("fsdp", None),
            P("fsdp", "seq"),
            P("seq", "fsdp"),
            P(None, "fsdp"),
            P("fsdp"),
        ),
        out_specs=(
            P("fsdp", "seq", None),
            P("fsdp", "seq", None),
            P("fsdp", None),
            P("fsdp", None),
            P("fsdp", None),
            P("fsdp", "seq"),
            P("seq", "fsdp"),
            P(None, "fsdp"),
            P("fsdp"),
        ),
        check_vma=False,
    )
```

```python
from functools import partial

import jax
import jax.numpy as jnp
from jax import lax
from jax.experimental import pallas as pl
from jax.experimental.pallas import tpu as pltpu
from jax.sharding import PartitionSpec as P

H = 16
HD = 64
EPSILON = 1e-06
LOG2E = 1.4426950408889634
SCALE2 = HD**-0.5 * LOG2E
MIB = 1024 * 1024
CHUNK = 512
ROOT = 0.7978845608028654
CUBE = 0.044715

NT = (((1,), (1,)), ((), ()))
TN = (((0,), (0,)), ((), ()))
NN = (((1,), (0,)), ((), ()))


def mm(a, b, dims=NN):
    return lax.dot_general(a, b, dims, preferred_element_type=jnp.float32)


def normalize(value_rows):
    center = value_rows - jnp.mean(value_rows, -1, keepdims=True)
    inverse = lax.rsqrt(jnp.mean(center * center, -1, keepdims=True) + EPSILON)
    return (center * inverse, inverse)


def norm_grad(normed, inverse, grad_normed):
    return inverse * (
        grad_normed
        - jnp.mean(grad_normed, -1, keepdims=True)
        - normed * jnp.mean(grad_normed * normed, -1, keepdims=True)
    )


def head_parts(ref, head, rows=slice(None)):
    base = head * 3 * HD
    return [ref[rows, base + j * HD : base + (j + 1) * HD] for j in range(3)]


def attend_kernel(query_ref, all_ref, out_ref, lse_ref):
    rows = query_ref.shape[0]
    for head in range(2):
        _, keys, values = head_parts(all_ref, head)
        chunk = min(CHUNK, rows)
        for at in range(0, rows, chunk):
            span = slice(at, at + chunk)
            queries = head_parts(query_ref, head, span)[0]
            scores = mm(keys, queries, NT)
            highest = jnp.max(scores, 0, keepdims=True)
            raised = jnp.exp2(scores * SCALE2 - highest * SCALE2)
            totals = jnp.sum(raised, 0, keepdims=True)
            result = mm(values, raised.astype(jnp.bfloat16), TN) / totals
            out_ref[span, head * HD : (head + 1) * HD] = result.T.astype(jnp.bfloat16)
            lse_ref[0, head : head + 1, span] = highest * SCALE2 + jnp.log2(totals)


def attend(qkv, tokens, first, count):
    length, columns = qkv.shape
    pairs = columns // (6 * HD)
    return pl.pallas_call(
        attend_kernel,
        grid=(pairs, count),
        in_specs=[
            pl.BlockSpec((tokens, 6 * HD), lambda p, b: (first + b, p)),
            pl.BlockSpec((length, 6 * HD), lambda p, b: (0, p)),
        ],
        out_specs=[
            pl.BlockSpec((tokens, 2 * HD), lambda p, b: (b, p)),
            pl.BlockSpec((1, 2, tokens), lambda p, b: (p, 0, b)),
        ],
        out_shape=[
            jax.ShapeDtypeStruct((count * tokens, pairs * 2 * HD), jnp.bfloat16),
            jax.ShapeDtypeStruct((pairs, 2, count * tokens), jnp.float32),
        ],
        compiler_params=pltpu.CompilerParams(vmem_limit_bytes=24 * MIB),
        cost_estimate=pl.CostEstimate(
            flops=pairs * length * count * tokens,
            bytes_accessed=0,
            transcendentals=0,
        ),
        name="attend",
    )(qkv, qkv)


def feed_kernel(aliased, hidden_ref, grad_ref, up_ref, down_ref, *rest):
    act_ref, grad_up_ref, branch_ref, part_ref, branch_acc, part_acc = rest[2 * aliased :]
    step = pl.program_id(0)
    up_weights, down_weights = up_ref[...], down_ref[...]
    value = mm(hidden_ref[...], up_weights)
    grad_act = mm(grad_ref[...], down_weights)
    square = value * value
    tanh = jnp.tanh(ROOT * value * (1.0 + CUBE * square))
    half = 0.5 * (1.0 + tanh)
    act = (value * half).astype(jnp.bfloat16)
    slope = half + (0.5 * ROOT) * value * (1.0 - tanh * tanh) * (1.0 + 3.0 * CUBE * square)
    grad_up = (grad_act * slope).astype(jnp.bfloat16)
    act_ref[...] = act
    grad_up_ref[...] = grad_up
    part = mm(grad_up, up_weights, NT)
    branch = mm(act, down_weights, NT)

    @pl.when(step == 0)
    def _():
        part_acc[...] = part
        branch_acc[...] = branch

    @pl.when(step > 0)
    def _():
        part_acc[...] += part
        branch_acc[...] += branch

    @pl.when(step == pl.num_programs(0) - 1)
    def _():
        part_ref[...] = part_acc[...].astype(part_ref.dtype)
        branch_ref[...] = branch_acc[...].astype(branch_ref.dtype)


def feed(hidden, grads_all, up_down, piece, buffers, out_type):
    tokens, width = hidden.shape
    units = up_down.shape[1] // 2
    block = min(512, units)
    count = units // block
    length = grads_all.shape[0]
    rows = pl.BlockSpec((tokens, block), lambda j: (piece, j))
    whole = pl.BlockSpec((tokens, width), lambda j: (0, 0))
    aliased = buffers is not None
    return pl.pallas_call(
        partial(feed_kernel, int(aliased)),
        grid=(count,),
        in_specs=[
            whole,
            pl.BlockSpec((tokens, width), lambda j: (piece, 0)),
            pl.BlockSpec((width, block), lambda j: (0, j)),
            pl.BlockSpec((width, block), lambda j: (0, count + j)),
        ]
        + [pl.BlockSpec(memory_space=pl.ANY)] * (2 * aliased),
        out_specs=[rows, rows, whole, whole],
        out_shape=[jax.ShapeDtypeStruct((length, units), jnp.bfloat16)] * 2
        + [jax.ShapeDtypeStruct((tokens, width), out_type)] * 2,
        scratch_shapes=[pltpu.VMEM((tokens, width), jnp.float32)] * 2,
        input_output_aliases={4: 0, 5: 1} if aliased else {},
        compiler_params=pltpu.CompilerParams(vmem_limit_bytes=40 * MIB),
        cost_estimate=pl.CostEstimate(
            flops=tokens * units, bytes_accessed=0, transcendentals=0
        ),
        name="feed",
    )(hidden, grads_all, up_down, up_down, *(buffers or ()))


def turn_kernel(rows, place_ref, value_ref, out_ref):
    at = pl.program_id(0)
    turned = value_ref[...].T
    each = 128 // rows
    for part in range(each):
        start = pl.multiple_of(place_ref[at * each + part] * rows, rows)
        out_ref[pl.ds(start, rows), :] = turned[part * rows : (part + 1) * rows, :]


def turn(value, place):
    length, width = value.shape
    rows = width // place.shape[0]
    return pl.pallas_call(
        partial(turn_kernel, rows),
        grid_spec=pltpu.PrefetchScalarGridSpec(
            num_scalar_prefetch=1,
            grid=(width // 128,),
            in_specs=[pl.BlockSpec((length, 128), lambda b, p: (0, b))],
            out_specs=pl.BlockSpec((width, length), lambda b, p: (0, 0)),
        ),
        out_shape=jax.ShapeDtypeStruct((width, length), value.dtype),
        compiler_params=pltpu.CompilerParams(vmem_limit_bytes=16 * MIB),
        cost_estimate=pl.CostEstimate(flops=0, bytes_accessed=4 * length * width, transcendentals=0),
        name="turn",
    )(place, value)


def divisor(count):
    return next(size for size in (512, 384, 256, 128) if count % size == 0)


def mat_kernel(left_ref, right_ref, out_ref):
    out_ref[...] = mm(left_ref[...], right_ref[...]).astype(out_ref.dtype)


def mat_turned_kernel(left_ref, right_ref, out_ref, turned):
    @pl.when(pl.program_id(0) == 0)
    def _():
        turned[...] = left_ref[...].T

    out_ref[...] = mm(turned[...], right_ref[...]).astype(out_ref.dtype)


def mat(left, right, part=0, parts=1, turned=False):
    depth, columns = right.shape
    rows = left.shape[1] if turned else left.shape[0] // parts
    block = divisor(columns)
    return pl.pallas_call(
        mat_turned_kernel if turned else mat_kernel,
        grid=(columns // block,),
        in_specs=[
            pl.BlockSpec((depth, rows) if turned else (rows, depth), lambda j: (part, 0)),
            pl.BlockSpec((depth, block), lambda j: (0, j)),
        ],
        out_specs=pl.BlockSpec((rows, block), lambda j: (0, j)),
        out_shape=jax.ShapeDtypeStruct((rows, columns), jnp.bfloat16),
        scratch_shapes=[pltpu.VMEM((rows, depth), jnp.bfloat16)] if turned else [],
        compiler_params=pltpu.CompilerParams(vmem_limit_bytes=18 * MIB),
        cost_estimate=pl.CostEstimate(flops=rows * depth, bytes_accessed=0, transcendentals=0),
        name="mat",
    )(left, right)


def hidden_back_kernel(groups, *refs):
    values, (weight_ref, normed_ref, own_ref, peers_ref, sums_ref) = refs[:groups], refs[groups:]
    size = values[0].shape[1]
    tokens = own_ref.shape[0]
    total = mm(values[0][...], weight_ref[:, :size], NT)
    for group in range(1, groups):
        total += mm(values[group][...], weight_ref[:, group * size : (group + 1) * size], NT)
    own_ref[...] = total[:tokens]
    peers_ref[...] = total[tokens:].astype(peers_ref.dtype)
    sums_ref[0:1, :] = jnp.sum(total, 0, keepdims=True)
    sums_ref[1:2, :] = jnp.sum(total * normed_ref[...], 0, keepdims=True)


def hidden_back(values, weights, normed, tokens):
    length, width = normed.shape
    block = min(256, width)
    columns = lambda rows: pl.BlockSpec((rows, block), lambda j: (0, j))
    return pl.pallas_call(
        partial(hidden_back_kernel, len(values)),
        grid=(width // block,),
        in_specs=[pl.BlockSpec(value.shape, lambda j: (0, 0)) for value in values]
        + [pl.BlockSpec((block, weights.shape[1]), lambda j: (j, 0)), columns(length)],
        out_specs=[columns(tokens), columns(length - tokens), columns(2)],
        out_shape=[
            jax.ShapeDtypeStruct((tokens, width), jnp.float32),
            jax.ShapeDtypeStruct((length - tokens, width), jnp.bfloat16),
            jax.ShapeDtypeStruct((2, width), jnp.float32),
        ],
        compiler_params=pltpu.CompilerParams(vmem_limit_bytes=24 * MIB),
        cost_estimate=pl.CostEstimate(
            flops=length * width, bytes_accessed=0, transcendentals=0
        ),
        name="hidden_back",
    )(*values, weights, normed)


def attend_back_kernel(pieces, all_ref, lse_ref, *rest):
    grad_refs, (out_ref, key_acc, value_acc) = rest[:pieces], rest[pieces:]
    tokens = grad_refs[0].shape[0]
    scaling = HD**-0.5
    chunk = min(CHUNK, tokens)
    for head in range(2):
        base = head * 3 * HD
        _, keys, values = head_parts(all_ref, head)
        for at in range(0, pieces * tokens, chunk):
            span = slice(at, at + chunk)
            inner = slice(at % tokens, at % tokens + chunk)
            queries = head_parts(all_ref, head, span)[0]
            grads = grad_refs[at // tokens][inner, head * HD : (head + 1) * HD]
            lse = lse_ref[0, head : head + 1, span]
            probs = jnp.exp2(mm(keys, queries, NT) * SCALE2 - lse)
            product = probs * mm(values, grads, NT)
            inner_sum = jnp.sum(product, 0, keepdims=True)
            score_grad = (product - probs * inner_sum).astype(jnp.bfloat16)
            value_part = mm(probs.astype(jnp.bfloat16), grads)
            key_part = mm(score_grad, queries)
            if at == 0:
                value_acc[...] = value_part
                key_acc[...] = key_part
            else:
                value_acc[...] += value_part
                key_acc[...] += key_part
            query_grad = mm(keys, score_grad, TN) * scaling
            out_ref[span, base : base + HD] = query_grad.T.astype(jnp.bfloat16)
        out_ref[:, base + HD : base + 2 * HD] = (key_acc[...] * scaling).astype(jnp.bfloat16)
        out_ref[:, base + 2 * HD : base + 3 * HD] = value_acc[...].astype(jnp.bfloat16)


def attend_back(qkv, grad_pieces, lse, first, pairs):
    length = qkv.shape[0]
    columns = pairs * 6 * HD
    tokens = grad_pieces[0].shape[0]
    return pl.pallas_call(
        partial(attend_back_kernel, len(grad_pieces)),
        grid=(pairs,),
        in_specs=[
            pl.BlockSpec((length, 6 * HD), lambda p: (0, first + p)),
            pl.BlockSpec((1, 2, length), lambda p: (first + p, 0, 0)),
        ]
        + [pl.BlockSpec((tokens, 2 * HD), lambda p: (0, first + p))] * len(grad_pieces),
        out_specs=pl.BlockSpec((length, 6 * HD), lambda p: (0, p)),
        out_shape=jax.ShapeDtypeStruct((length, columns), jnp.bfloat16),
        scratch_shapes=[
            pltpu.VMEM((length, HD), jnp.float32),
            pltpu.VMEM((length, HD), jnp.float32),
        ],
        compiler_params=pltpu.CompilerParams(vmem_limit_bytes=32 * MIB),
        cost_estimate=pl.CostEstimate(
            flops=pairs * length * length,
            bytes_accessed=0,
            transcendentals=0,
        ),
        name="attend_back",
    )(qkv, lse, *grad_pieces)


def per_device(sizes, latents, cond, cotangent, w_qkv, w_out, w_up, w_down, w_ada, b_ada):
    shards, splits = sizes["fsdp"], sizes["seq"]
    me = lax.axis_index("seq")
    tokens, width = latents.shape[1:]
    heads = H // splits
    low = jnp.bfloat16
    wide = jnp.float32

    def fetch(value, step):
        return lax.ppermute(value, "seq", [((i + step) % splits, i) for i in range(splits)])

    def send(value, step):
        return lax.ppermute(value, "seq", [(i, (i + step) % splits) for i in range(splits)])

    def everyone(value):
        return [value] + [fetch(value, step) for step in range(1, splits)]

    def in_order(pieces, axis):
        if splits == 1:
            return pieces[0]
        return jnp.concatenate(
            [
                lax.select_n(
                    (position - me) % splits == 1, *pieces
                ) if splits == 2 else
                lax.dynamic_index_in_dim(
                    jnp.stack(pieces), (position - me) % splits, 0, keepdims=False
                )
                for position in range(splits)
            ],
            axis,
        )

    def seq_sum(value):
        if splits != 2:
            return lax.psum(value, "seq").astype(wide)
        return value.astype(wide) + fetch(value, 1).astype(wide)

    spot = lax.axis_index("fsdp")
    depth = shards // 4
    core_at, x_at, z_at = spot % 2, (spot // 2) % 2, spot // 4

    def core_swap(value):
        return lax.ppermute(value, "fsdp", [(i, i ^ 1) for i in range(shards)])

    def x_swap(value):
        return lax.ppermute(value, "fsdp", [(i, i ^ 2) for i in range(shards)])

    def z_send(value, step):
        return lax.ppermute(value, "fsdp", [(i, (i + 4 * step) % shards) for i in range(shards)])

    def two(mine, other, at):
        return jnp.stack(
            [jnp.where(at == 0, mine, other), jnp.where(at == 0, other, mine)], 1
        )

    def gather_z(shard):
        return [shard] + [z_send(shard, step) for step in range(1, depth)]

    def gather_x(pieces):
        rows, cols = pieces[0].shape
        line = jnp.zeros((depth, rows, cols), pieces[0].dtype)
        for step, piece in enumerate(pieces):
            line = lax.dynamic_update_slice_in_dim(line, piece[None], (z_at - step) % depth, 0)
        return line, x_swap(line)

    def gather_core(pair):
        rows, cols = pair[0].shape[1:]
        plane = two(*pair, x_at).reshape(2 * depth, rows, cols)
        return plane, core_swap(plane)

    def gather_end(pair):
        rows, cols = pair[0].shape[1:]
        return two(*pair, core_at).reshape(shards * rows, cols)

    blocks_at = jnp.arange(shards)
    place = (
        ((blocks_at % 2) ^ core_at) * 2 + ((blocks_at // 2) % 2 ^ x_at)
    ) * depth + (blocks_at // 4 - z_at) % depth
    place = place.astype(jnp.int32)

    def scatter_core(turned, value):
        return mat(turned, value, 0, 2), core_swap(mat(turned, value, 1, 2))

    def x_part(pair):
        half = pair[0].shape[0] // 2
        return (pair[0][half:].astype(wide) + pair[1][half:].astype(wide)).astype(low)

    def scatter_x(pair, part):
        return *pair, x_swap(part)

    def scatter_z(*many):
        total = jnp.concatenate(
            [sum(part[: terms[2].shape[0]].astype(wide) for part in terms) for terms in many], 1
        )
        rows = total.shape[0] // depth
        return [total[:rows]] + [
            z_send(total[step * rows : (step + 1) * rows].astype(low), step)
            for step in range(1, depth)
        ]

    def scatter_end(pieces):
        return sum(piece.astype(wide) for piece in pieces)

    after = lax.optimization_barrier
    own_latents, own_cotangent = latents[0], cotangent[0]
    cond_act, silu_back = jax.vjp(jax.nn.silu, cond.astype(wide))
    cond_all = lax.all_to_all(
        jnp.broadcast_to(cond_act.astype(low), (shards, width)),
        "fsdp",
        split_axis=0,
        concat_axis=0,
        tiled=True,
    )
    peer_latents = [fetch(own_latents, step) for step in range(1, splits)]
    cond_all, peer_latents = after((cond_all, peer_latents))
    mod_cols = (mm(cond_all, w_ada) + b_ada.astype(wide)).astype(low)
    modulation = lax.all_to_all(
        mod_cols, "fsdp", split_axis=0, concat_axis=1, tiled=True
    ).astype(wide)
    modulation, out_shard = after((modulation, w_out))
    out_pieces = gather_z(out_shard)
    shift_one, scale_one, gate_one, shift_two, scale_two, gate_two = [
        modulation[:, position * width : (position + 1) * width] for position in range(6)
    ]
    columns = heads * 3 * HD
    qkv_shard = lax.dynamic_slice_in_dim(w_qkv, me * columns, columns, 1)
    qkv_half = lax.all_gather(qkv_shard, "fsdp", axis=0, tiled=True)
    cond_all, up_shard, down_shard = after((cond_all, w_up, w_down))
    up_down = lax.all_gather(
        jnp.concatenate([up_shard, down_shard.T], 1), "fsdp", axis=0, tiled=True
    )
    units = w_up.shape[1]

    latents_all = jnp.concatenate([own_latents] + peer_latents, 0)
    cotangents = everyone(own_cotangent)

    normed_all, inverse_all = normalize(latents_all.astype(wide))
    hidden_one = (normed_all * (1.0 + scale_one) + shift_one).astype(low)
    qkv = mm(hidden_one, qkv_half).astype(low)
    qkv, out_pieces = after((qkv, out_pieces))
    out_pair = gather_x(out_pieces)
    attn_peers, lse_peers = attend(qkv, tokens, 1, splits - 1)
    attn_peers, qkv, cotangents = after((attn_peers, qkv, cotangents))
    blocks = [None] + [attn_peers[r * tokens : (r + 1) * tokens] for r in range(splits - 1)]
    theirs = [{} for _ in range(splits)]
    for r in range(1, splits):
        for q in range(1, splits):
            theirs[(r + q) % splits][q] = fetch(blocks[r], q)
    attn_own, lse_own = attend(qkv, tokens, 0, 1)
    blocks[0] = attn_own
    attn_own, out_pair, theirs = after((attn_own, out_pair, theirs))
    for q in range(1, splits):
        theirs[q][q] = fetch(attn_own, q)
    out_full = gather_end(gather_core(out_pair))

    def to_feed(rows, heads_of, piece):
        inputs = latents_all[piece * tokens : (piece + 1) * tokens].astype(wide)
        attn_rows = in_order([rows] + [heads_of[q] for q in range(1, splits)], 1)
        branch_one = mm(attn_rows, out_full)
        middle = inputs + gate_one * branch_one
        normed, inverse = normalize(middle)
        hidden = (normed * (1.0 + scale_two) + shift_two).astype(low)
        return hidden, attn_rows, branch_one, middle, normed, inverse

    own_theirs = theirs[0]
    hidden_two, attn_rows, branch_one, middle, normed_two, inverse_two = to_feed(
        attn_own, own_theirs, 0
    )
    hidden_two, theirs = after((hidden_two, theirs))
    grad_rows = (gate_two * jnp.concatenate(cotangents, 0).astype(wide)).astype(low)
    hidden_pieces = [hidden_two] + [
        to_feed(blocks[r], theirs[r], r)[0] for r in range(1, splits)
    ]

    hidden_all = jnp.concatenate(hidden_pieces, 0)
    turned_one, turned_two = turn(hidden_one, place), turn(hidden_all, place)
    turned_attn = turn(attn_rows, place)
    hidden_pieces, grad_rows, turned_one, turned_two, turned_attn = after(
        (hidden_pieces, grad_rows, turned_one, turned_two, turned_attn)
    )
    buffers, grad_parts, branch_parts = None, [None] * splits, [None] * splits
    grad_sent = []
    for piece in list(range(1, splits)) + [0]:
        act, grad_up, branch_parts[piece], grad_parts[piece] = feed(
            hidden_pieces[piece],
            grad_rows,
            up_down,
            piece,
            buffers,
            low if piece else wide,
        )
        buffers = (act, grad_up)
        if piece:
            grad_sent.append(send(grad_parts[piece], piece))

    def send_parts(parts):
        return [send(parts[step].astype(low), step) for step in range(1, splits)]

    def add_parts(own, received):
        for value in received:
            own = own + value.astype(wide)
        return own

    term_down = mat(grad_rows, act, turned=True)
    grad_sent, term_down, act, grad_up, branch_parts = after(
        (grad_sent, term_down, act, grad_up, branch_parts)
    )
    grad_w_down = lax.psum_scatter(term_down, "fsdp", scatter_dimension=0, tiled=True)
    grad_hidden_two = add_parts(grad_parts[0], grad_sent)
    grad_mixed = own_cotangent.astype(wide)
    grad_shift_two = jnp.sum(grad_hidden_two, 0)
    grad_scale_two = jnp.sum(grad_hidden_two * normed_two, 0)
    grad_middle = grad_mixed + norm_grad(
        normed_two, inverse_two, grad_hidden_two * (1.0 + scale_two)
    )
    grad_gate_one = jnp.sum(grad_middle * branch_one, 0)
    grad_branch_one = (gate_one * grad_middle).astype(low)

    grad_attn = mm(grad_branch_one, out_full, NT).astype(low)
    own_width = heads * HD
    grad_pieces = [
        lax.dynamic_slice_in_dim(grad_attn, ((me + r) % splits) * own_width, own_width, 1)
        for r in range(splits)
    ]
    grad_arrived = [send(grad_pieces[r], r) for r in range(1, splits)]
    up_pair = scatter_core(turned_two, grad_up)
    out_pair = scatter_core(turned_attn, grad_branch_one)
    up_part, out_part = x_part(up_pair), x_part(out_pair)
    up_pair, out_pair, up_part, out_part, grad_arrived, branch_parts = after(
        (up_pair, out_pair, up_part, out_part, grad_arrived, branch_parts)
    )
    up_terms = scatter_x(up_pair, up_part)
    branch_sent = send_parts(branch_parts)
    out_terms = scatter_x(out_pair, out_part)
    grad_heads = [grad_pieces[0]] + grad_arrived[::-1]
    lse = jnp.concatenate([lse_own, lse_peers], 2)
    pairs = heads // 2
    groups = 2 if pairs % 2 == 0 else 1
    each = pairs // groups
    size = each * 6 * HD
    values, first_terms = [], []
    for group in range(groups):
        value = attend_back(qkv, grad_heads, lse, group * each, each)
        values.append(value)
        if group + 1 < groups:
            pair = scatter_core(turned_one, values[0])
            part = x_part(pair)
            pair, part, grad_heads, lse, up_terms = after(
                (pair, part, grad_heads, lse, up_terms)
            )
            first_terms = scatter_x(pair, part)
    up_pieces = scatter_z(up_terms)
    values, first_terms, out_terms, branch_sent = after(
        (values, first_terms, out_terms, branch_sent)
    )
    pair = scatter_core(turned_one, values[-1])
    part = x_part(pair)
    pair, part, values = after((pair, part, values))
    last_terms = scatter_x(pair, part)
    own_grad, peers_grad, sums = hidden_back(values, qkv_half, normed_all, tokens)
    own_grad, peers_grad, sums, grad_w_down, up_pieces = after(
        (own_grad, peers_grad, sums, grad_w_down, up_pieces)
    )
    branch_two = add_parts(branch_parts[0], branch_sent)
    grad_gate_two = jnp.sum(grad_mixed * branch_two, 0)

    grad_mod_part = jnp.concatenate(
        [sums[0], sums[1], grad_gate_one, grad_shift_two, grad_scale_two, grad_gate_two]
    )[None]
    grad_mod = seq_sum(grad_mod_part).astype(low)
    hidden_parts = [own_grad] + [
        peers_grad[r * tokens : (r + 1) * tokens] for r in range(splits - 1)
    ]
    grad_mod, hidden_parts, first_terms, out_terms, up_pieces, grad_w_down = after(
        (grad_mod, hidden_parts, first_terms, out_terms, up_pieces, grad_w_down)
    )
    grad_mod_cols = lax.all_to_all(grad_mod, "fsdp", split_axis=1, concat_axis=0, tiled=True)
    hidden_sent = send_parts(hidden_parts)
    grad_mod_cols, last_terms = after((grad_mod_cols, last_terms))
    last_pieces = scatter_z(last_terms)
    joint_pieces = scatter_z(*([out_terms, first_terms] if groups > 1 else [out_terms]))
    grad_w_ada = mm(cond_all, grad_mod_cols, TN)
    grad_b_ada = jnp.sum(grad_mod_cols.astype(wide), 0)
    cond_term = mm(grad_mod_cols, w_ada, NT).astype(low)
    cond_term, middle, grad_w_down, up_pieces, last_pieces, joint_pieces, hidden_sent = after(
        (cond_term, middle, grad_w_down, up_pieces, last_pieces, joint_pieces, hidden_sent)
    )
    mixed = (middle + gate_two * branch_two).astype(low)
    cond_terms = lax.all_to_all(cond_term, "fsdp", split_axis=0, concat_axis=0, tiled=True)
    grad_w_up = scatter_end(up_pieces)
    grad_joint = scatter_end(joint_pieces).astype(low)
    grad_w_out = seq_sum(grad_joint[:, :width])
    grad_hidden_one = add_parts(hidden_parts[0], hidden_sent)
    grad_latents = grad_middle + norm_grad(
        normed_all[:tokens], inverse_all[:tokens], grad_hidden_one * (1.0 + scale_one)
    )
    grad_cond = silu_back(jnp.sum(cond_terms.astype(wide), 0, keepdims=True))[0]
    last_pieces, grad_latents, grad_cond, grad_w_out = after(
        (last_pieces, grad_latents, grad_cond, grad_w_out)
    )
    shards_qkv = [grad_joint[:, width:], scatter_end(last_pieces).astype(low)]
    grad_w_qkv = in_order(everyone(jnp.concatenate(shards_qkv, 1)), 1).astype(wide)
    return (
        mixed[None],
        grad_latents[None],
        grad_cond,
        grad_w_qkv,
        grad_w_out,
        grad_w_up,
        grad_w_down.T.astype(wide),
        grad_w_ada,
        grad_b_ada,
    )


def solution(mesh):
    return jax.shard_map(
        partial(per_device, dict(mesh.shape)),
        mesh=mesh,
        in_specs=(
            P("fsdp", "seq", None),
            P("fsdp", None),
            P("fsdp", "seq", None),
            P("fsdp", None),
            P("fsdp", None),
            P("fsdp", "seq"),
            P("seq", "fsdp"),
            P(None, "fsdp"),
            P("fsdp"),
        ),
        out_specs=(
            P("fsdp", "seq", None),
            P("fsdp", "seq", None),
            P("fsdp", None),
            P("fsdp", None),
            P("fsdp", None),
            P("fsdp", "seq"),
            P("seq", "fsdp"),
            P(None, "fsdp"),
            P("fsdp"),
        ),
        check_vma=False,
    )
```
